128 devices in a mesh: front: 4 (over x), row: 8 (over y, core), col: 4 (over z).
Axes of the slice: x: 4, y: 4, z: 4, core: 2. Of those that a mesh axis runs over, the one named last changes fastest.
Arguments:
- front: float32 [4, 9, 8, 128, 18, 4, 128], P('front', None, 'row', None, None, 'col')
- child_updates: float32 [4, 1024, 128, 128], P('front', ('row', 'col')), may hold values from -3 to 3
- child_owner: int32 [4, 1024, 1], P('front', ('row', 'col')), may hold values from 0 to 31; in each aligned block of 32 rows (0 to 31, 32 to 63, ..., all dimensions but the last counted through in order) at most 2 rows name the same one
- child_rows: int32 [4, 1024, 128], P('front', ('row', 'col')), may hold values from 0 to 128, as said below
- child_cols: int32 [4, 1024, 128], P('front', ('row', 'col')), may hold values from 0 to 128, as said below
- child_slot: int32 [4, 1024], P('front', ('row', 'col')), may hold values from 0 to 161, as said below
Outputs:
- factored: float32 [4, 9, 8, 128, 18, 4, 128], P('front', None, 'row', None, None, 'col')
The draws below stay inside these ranges and needn't reach their ends.
Inputs may be any that keep to these rules, and one draw needn't show every extreme that they name: `child_owner`: among the child blocks of one device (aligned blocks of 32), no owner is named more than 2 times. `child_rows`: in each block the entries below 128 come first and rise strictly; the rest equal 128. `child_cols`: in each block the entries below 128 come first and rise strictly; the rest equal 128. `child_slot`: A slot never names local tile column 0 together with one of the first 1 local tile rows.
All inputs are finite; a program needn't handle non-finite values.
Results may differ from the reference program's by a relative error of at most 0.0003.
Values sent between devices are 32-bit elements; how exact they have to be, the bound alone decides.
No kernel may reach another device: no remote copies, remote signals or barrier semaphores. Data moves between devices by JAX's collectives and lax.ppermute only.
A program may use at most 192 MiB of HBM per device.

```python
import math
import jax
import jax.numpy as jnp
import numpy as np
from jax import lax

NF = 9216
TILE = 128
PANEL = 512
CB = 32
FRONTS = 4
GRID_ROWS = 8
GRID_COLS = 4
OWNERS = 32
CAP = 2
TPR = 9
TPC = 18
LEADING = 1


lead_scale = 0.1


def draw_front(key, part):
    full_shape = (FRONTS, TPR, GRID_ROWS, TILE, TPC, GRID_COLS, TILE)
    first_key, second_key = jax.random.split(key, 2)
    values = jnp.clip(jax.random.normal(first_key, full_shape, jnp.float32), -2.5, 2.5) / 2.5
    tile_a = jnp.arange(TPR).reshape(1, TPR, 1, 1, 1, 1, 1)
    grid_r = jnp.arange(GRID_ROWS).reshape(1, 1, GRID_ROWS, 1, 1, 1, 1)
    inner_i = jnp.arange(TILE).reshape(1, 1, 1, TILE, 1, 1, 1)
    tile_b = jnp.arange(TPC).reshape(1, 1, 1, 1, TPC, 1, 1)
    grid_c = jnp.arange(GRID_COLS).reshape(1, 1, 1, 1, 1, GRID_COLS, 1)
    inner_j = jnp.arange(TILE).reshape(1, 1, 1, 1, 1, 1, TILE)
    global_row = (tile_a * GRID_ROWS + grid_r) * TILE + inner_i
    global_col = (tile_b * GRID_COLS + grid_c) * TILE + inner_j
    diagonal = PANEL * lead_scale * (1.25 + jax.random.uniform(second_key, (FRONTS, TPR, GRID_ROWS, TILE, 1, 1, 1), jnp.float32))
    in_lead = (global_row < PANEL) & (global_col < PANEL)
    lead_values = jnp.where(global_row == global_col, diagonal, lead_scale * values)
    return jnp.where(in_lead, lead_values, values).astype(jnp.float32)


def index_blocks(key):
    full_shape = (FRONTS, OWNERS * CB, TILE)
    keep = jax.random.randint(key, full_shape, 0, 4) > 0
    positions = jnp.broadcast_to(jnp.arange(TILE, dtype=jnp.int32), full_shape)
    scores = jnp.where(keep, positions, TILE + positions)
    ordered = jnp.argsort(scores, axis=-1, stable=True).astype(jnp.int32)
    kept_total = jnp.sum(keep.astype(jnp.int32), axis=-1, keepdims=True)
    return jnp.where(positions < kept_total, ordered, TILE).astype(jnp.int32)


def draw_child_rows(key, part):
    return index_blocks(jax.random.fold_in(key, 11))


def draw_child_cols(key, part):
    return index_blocks(jax.random.fold_in(key, 23))


def draw_child_slot(key, part):
    row_key, col_key, other_key = jax.random.split(jax.random.fold_in(key, 37), 3)
    full_shape = (FRONTS, OWNERS * CB)
    tile_a = jax.random.randint(row_key, full_shape, 0, TPR)
    tile_b = jax.random.randint(col_key, full_shape, 0, TPC)
    moved_b = jax.random.randint(other_key, full_shape, 1, TPC)
    tile_b = jnp.where((tile_a < LEADING) & (tile_b == 0), moved_b, tile_b)
    return (tile_a * TPC + tile_b).astype(jnp.int32)


def block_scale(key, extent, cuts, low, largest):
    def one(axis_at, shards_of):
        heights = jax.random.uniform(jax.random.fold_in(jax.random.fold_in(key, 6), axis_at), (shards_of,), jnp.float32, low / len(cuts), largest / len(cuts))
        return jnp.repeat(jnp.exp(heights), extent[axis_at] // shards_of).reshape((-1,) + (1,) * (len(extent) - axis_at - 1))

    loudness = one(*cuts[0])
    for cut in cuts[1:]:
        loudness = loudness * one(*cut)
    return loudness


def routed_block(own_key, own, number, rows, amount, top, reach, slope):
    order = jax.random.permutation(own_key, amount)
    crowded, usual = load_shares(amount, rows * top, reach, slope, True), load_shares(amount, rows * top, reach, slope, False)
    places = jnp.arange(amount)

    def named(tallies, turn):
        used = int((tallies > 0).sum())
        fixed = max(1, used // 4)
        moved = fixed + (places - fixed + turn * (used - fixed)) % max(1, amount - fixed)
        return jnp.zeros((amount,), jnp.int32).at[order[jnp.where(places < fixed, places, moved)]].set(jnp.asarray(tallies, jnp.int32))

    tallies = jnp.where(number % 4 == 0, named(crowded, number // 4), named(usual, number - number // 4 - 1))
    mixed = jax.random.permutation(jax.random.fold_in(own, 3), amount)
    giver, taker = mixed[0:amount // 2 * 2:2], mixed[1:amount // 2 * 2:2]
    margin = jnp.minimum(tallies[giver] - 1, reach - tallies[taker]) // 2
    margin = jnp.where((giver == order[0]) | (taker == order[0]) | (tallies[taker] == 0), 0, jnp.maximum(margin, 0))
    moved = jax.random.randint(jax.random.fold_in(own, 4), (amount // 2,), 0, 1 << 20) % (margin + 1)
    tallies = tallies.at[giver].add(-moved).at[taker].add(moved)
    items = jnp.searchsorted(jnp.cumsum(tallies), jnp.arange(rows * top), side="right").astype(jnp.int32)
    listing = items.reshape(top, rows).T
    listing = listing[jax.random.permutation(jax.random.fold_in(own, 1), rows)]
    turn = jax.random.randint(jax.random.fold_in(own, 2), (rows, 1), 0, top)
    return jnp.take_along_axis(listing, (jnp.arange(top)[None, :] + turn) % top, axis=1)


def load_shares(number_of, total, most, slope, full):
    weights = [(1 << 20) // math.isqrt(rank ** slope) + 1 for rank in range(1, number_of + 1)]
    largest = most if full else min(most, max(-(-total // number_of), total * weights[0] // sum(weights)))
    least = 1 if total - largest >= number_of - 1 else 0
    counts, rest = [largest] + [least] * (number_of - 1), total - largest - least * (number_of - 1)
    while rest > 0:
        movable = [i for i in range(1, number_of) if counts[i] < largest] or [i for i in range(1, number_of) if counts[i] < most]
        pool, remaining = sum([weights[i] for i in movable]), rest
        for i in movable:
            extra = min(most - counts[i], max(1, remaining * weights[i] // pool), rest)
            counts[i] = counts[i] + extra
            rest = rest - extra
    return np.array(counts)


def centred(key, extent, scale, bound, shards=(), kind=jnp.bfloat16):
    values = scale * jax.random.normal(key, extent, jnp.float32)
    if shards:
        values = values * block_scale(key, extent, shards, -0.22, 0.18)
    return jnp.clip(values, -bound, bound).astype(kind)


def setup_inputs(seed: int = 0) -> dict:
    streams_of = jax.random.split(jax.random.key(seed), 7)
    front = draw_front(jax.random.fold_in(streams_of[6], 71), 0)
    child_updates = centred(streams_of[1], (FRONTS, OWNERS * CB, TILE, TILE), 0.5, 3.0, ((0, 4), (1, 32)), jnp.float32)
    child_owner_keys = jax.random.split(jax.random.fold_in(streams_of[2], 1), FRONTS * (OWNERS * CB) // CB)
    child_owner_turns = jax.random.permutation(jax.random.fold_in(streams_of[2], 3), FRONTS * (OWNERS * CB) // CB)
    child_owner = jax.vmap(lambda own, number: routed_block(jax.random.fold_in(streams_of[2], 2), own, number, CB, OWNERS, 1, CAP, 2))(child_owner_keys, child_owner_turns).reshape((FRONTS, OWNERS * CB, 1))
    child_rows = draw_child_rows(jax.random.fold_in(streams_of[6], 71), 0)
    child_cols = draw_child_cols(jax.random.fold_in(streams_of[6], 71), 0)
    child_slot = draw_child_slot(jax.random.fold_in(streams_of[6], 71), 0)
    return {"front": front, "child_updates": child_updates, "child_owner": child_owner, "child_rows": child_rows, "child_cols": child_cols, "child_slot": child_slot}


def one_front(operands):
    matrix, updates, owners_of, rows_map, cols_map, slot_index = operands
    matrix = matrix.reshape(NF, NF)
    owner_row = owners_of[:, 0] // GRID_COLS
    owner_col = owners_of[:, 0] % GRID_COLS
    tile_row = slot_index // TPC * GRID_ROWS + owner_row
    tile_col = slot_index % TPC * GRID_COLS + owner_col
    place_rows = jnp.where(rows_map < TILE, tile_row[:, None] * TILE + rows_map, NF).astype(jnp.int32)
    place_cols = jnp.where(cols_map < TILE, tile_col[:, None] * TILE + cols_map, NF).astype(jnp.int32)
    assembled = matrix.at[place_rows[:, :, None], place_cols[:, None, :]].add(updates, mode='drop')
    panel = assembled[:, :PANEL]
    leading = panel[:PANEL]
    factor = jnp.linalg.cholesky(0.5 * (leading + leading.T))
    panel_factor = jax.scipy.linalg.solve_triangular(factor, panel.T, lower=True).T
    lower_rows = panel_factor[PANEL:]
    update = jnp.dot(lower_rows, lower_rows.T, precision=lax.Precision.HIGHEST)
    result = assembled.at[PANEL:, PANEL:].set(assembled[PANEL:, PANEL:] - update)
    result = result.at[:, :PANEL].set(panel_factor)
    return result.reshape(TPR, GRID_ROWS, TILE, TPC, GRID_COLS, TILE)

def reference(front, child_updates, child_owner, child_rows, child_cols, child_slot):
    return lax.map(one_front, (front, child_updates, child_owner, child_rows, child_cols, child_slot))
```

```python
import functools

import jax
import jax.numpy as jnp
from jax import lax
from jax.experimental import pallas as pl
from jax.experimental.pallas import tpu as pltpu
from jax.sharding import PartitionSpec as P

T = 128
F32 = jnp.float32
BF16 = jnp.bfloat16
HIGHEST = lax.Precision.HIGHEST
NT = (((1,), (1,)), ((), ()))
NN = (((1,), (0,)), ((), ()))
VM = functools.partial(pl.BlockSpec, memory_space=pltpu.VMEM)
ANY = functools.partial(pl.BlockSpec, memory_space=pl.ANY)
LIMIT = 60 * 1024 * 1024


def params():
    return pltpu.CompilerParams(vmem_limit_bytes=LIMIT)


def split(x):
    high = x.astype(BF16)
    low = (x - high.astype(F32)).astype(BF16)
    return high, low


def dot3(x, y, dims):
    xh, xl = split(x)
    yh, yl = split(y)
    dot = functools.partial(lax.dot_general, dimension_numbers=dims, preferred_element_type=F32)
    return dot(xh, yh) + (dot(xh, yl) + dot(xl, yh))


def route_kernel(blocks, slot_total, owner_ref, slot_ref, blocks_ref, rows_ref, cols_ref, send_ref, meta, count, sem):
    owners = meta.shape[0]
    meta[...] = jnp.full(meta.shape, float(slot_total), F32)

    def clear(o, _):
        count[o] = 0
        return 0

    lax.fori_loop(0, owners, clear, 0)

    def place(g, _):
        o = owner_ref[g]
        k = count[o]
        count[o] = k + 1
        pltpu.make_async_copy(blocks_ref.at[g], send_ref.at[o, pl.ds(pl.multiple_of(k * T, T), T), :], sem.at[g]).start()
        meta[o, pl.ds(2 * k, 1), :] = rows_ref[pl.ds(g, 1), :].astype(F32)
        meta[o, pl.ds(2 * k + 1, 1), :] = cols_ref[pl.ds(g, 1), :].astype(F32)
        meta[o, pl.ds(4 + k, 1), :] = jnp.full((1, T), slot_ref[g], jnp.int32).astype(F32)
        return 0

    lax.fori_loop(0, blocks, place, 0)
    tail = pltpu.make_async_copy(meta, send_ref.at[:, pl.ds(2 * T, 8), :], sem.at[blocks])
    tail.start()

    def finish(g, _):
        pltpu.make_async_copy(blocks_ref.at[g], send_ref.at[0, pl.ds(0, T), :], sem.at[g]).wait()
        return 0

    lax.fori_loop(0, blocks, finish, 0)
    tail.wait()


def route(owner, slot, blocks, rows, cols, owners, slot_total):
    count = blocks.shape[0]
    return pl.pallas_call(
        functools.partial(route_kernel, count, slot_total),
        out_shape=jax.ShapeDtypeStruct((owners, 2 * T + 8, T), F32),
        grid_spec=pltpu.PrefetchScalarGridSpec(
            num_scalar_prefetch=2,
            grid=(),
            in_specs=[ANY(), VM(), VM()],
            out_specs=ANY(),
            scratch_shapes=[
                pltpu.VMEM((owners, 8, T), F32),
                pltpu.SMEM((owners,), jnp.int32),
                pltpu.SemaphoreType.DMA((count + 1,)),
            ],
        ),
        compiler_params=params(),
        name="route",
    )(owner, slot, blocks, rows, cols)


def inverse_factor(s, out_ref):
    groups = T // 8
    lane = lax.broadcasted_iota(jnp.int32, (8, T), 1)
    sub = lax.broadcasted_iota(jnp.int32, (8, T), 0)
    m = [s[8 * g : 8 * g + 8, :] for g in range(groups)]
    e = [jnp.where(lane == sub + 8 * g, 1.0, 0.0).astype(F32) for g in range(groups)]
    for k in range(T):
        g0, s0 = divmod(k, 8)
        row = jnp.broadcast_to(m[g0][s0 : s0 + 1, :], (8, T))
        erow = jnp.broadcast_to(e[g0][s0 : s0 + 1, :], (8, T))
        pivot = jnp.broadcast_to(row[:, k : k + 1], (8, T))
        out_ref[k : k + 1, :] = (erow * lax.rsqrt(pivot))[0:1, :]
        if k == T - 1:
            break
        inv = 1.0 / pivot
        row = row * inv
        erow = erow * inv
        for g in range(g0, groups):
            col = jnp.broadcast_to(m[g][:, k : k + 1], (8, T))
            if g == g0:
                if s0 == 7:
                    continue
                col = jnp.where(sub > s0, col, 0.0)
            m[g] = m[g] - col * row
            e[g] = e[g] - col * erow


def leading_kernel(lead_ref, wt_ref, s_ref, e_ref, w_ref):
    n = 4
    dot = functools.partial(lax.dot_general, precision=HIGHEST, preferred_element_type=F32)
    for i in range(n):
        for j in range(i + 1):
            s_ref[i, j] = 0.5 * (lead_ref[j, i] + lead_ref[i, j].T)
    e_ref[...] = jnp.zeros_like(e_ref)

    def step(k, _):
        inverse_factor(s_ref[k, k], w_ref)
        wk = w_ref[...]
        own = dot(wk, e_ref[k], NN)
        column = lax.broadcasted_iota(jnp.int32, (T, n * T), 1)
        spread = jnp.concatenate([wk] * n, axis=1)
        own = jnp.where(column // T == k, spread, own)
        for j in range(n):
            wt_ref[j, :, pl.ds(pl.multiple_of(k * T, T), T)] = own[:, j * T : (j + 1) * T].T

        for i in range(1, n):
            @pl.when(i > k)
            def _():
                lik = dot(s_ref[i, k], wk, NT)
                s_ref[i, k] = lik
                e_ref[i] = e_ref[i] - dot(lik, own, NN)
                for j in range(1, i + 1):
                    @pl.when(j > k)
                    def _():
                        s_ref[i, j] = s_ref[i, j] - dot(lik, s_ref[j, k], NT)
        return 0

    lax.fori_loop(0, n, step, 0)


def leading_inverse(lead):
    return pl.pallas_call(
        leading_kernel,
        out_shape=jax.ShapeDtypeStruct((4, T, 4 * T), F32),
        in_specs=[VM()],
        out_specs=VM(),
        scratch_shapes=[
            pltpu.VMEM((4, 4, T, T), F32),
            pltpu.VMEM((4, T, 4 * T), F32),
            pltpu.VMEM((T, T), F32),
        ],
        compiler_params=params(),
        cost_estimate=pl.CostEstimate(flops=60_000_000_000, bytes_accessed=2_000_000, transcendentals=0),
        name="leading_inverse",
    )(lead)


def placed_block(block, rows, cols):
    inner = lax.broadcasted_iota(jnp.int32, (T, T), 0).astype(F32)
    row_hot = jnp.where(inner == rows, 1.0, 0.0).astype(BF16)
    col_hot = jnp.where(inner == cols, 1.0, 0.0).astype(BF16)
    high, low = split(block)
    x = lax.dot_general(
        jnp.concatenate([row_hot, row_hot], axis=1), jnp.concatenate([high, low], axis=0), NN, preferred_element_type=F32
    )
    high, low = split(x)
    return lax.dot_general(
        jnp.concatenate([high, low], axis=1), jnp.concatenate([col_hot, col_hot], axis=1), NT, preferred_element_type=F32
    )


def got_block(got_ref, n):
    g, k = n // 2, n % 2
    block = got_ref[g, pl.ds(pl.multiple_of(k * T, T), T), :]
    rows = got_ref[g, pl.ds(2 * T + 2 * k, 1), :]
    cols = got_ref[g, pl.ds(2 * T + 2 * k + 1, 1), :]
    return placed_block(block, rows, cols)


def panel_kernel(tile_cols, slot_total, slot_ref, got_ref, base_ref, out_ref):
    out_ref[...] = base_ref[...]

    def step(n, _):
        slot = slot_ref[n]

        @pl.when((slot < slot_total) & (slot % tile_cols == 0))
        def _():
            a = pl.ds(pl.multiple_of(slot // tile_cols * T, T), T)
            out_ref[a, :] = out_ref[a, :] + got_block(got_ref, n)

        return 0

    lax.fori_loop(0, slot_ref.shape[0], step, 0)


def panel(slots, got, base, tile_cols, slot_total):
    return pl.pallas_call(
        functools.partial(panel_kernel, tile_cols, slot_total),
        out_shape=jax.ShapeDtypeStruct(base.shape, F32),
        grid_spec=pltpu.PrefetchScalarGridSpec(
            num_scalar_prefetch=1, grid=(), in_specs=[VM(), VM()], out_specs=VM()
        ),
        compiler_params=params(),
        name="panel",
    )(slots, got, base)


def rest_kernel(tile_cols, slot_total, slot_ref, got_ref, base_ref, out_ref):
    a = pl.program_id(0)
    out_ref[...] = base_ref[...]

    def step(n, _):
        slot = slot_ref[n]
        b = slot % tile_cols

        @pl.when((slot < slot_total) & (slot // tile_cols == a) & (b > 0))
        def _():
            at = pl.ds(b, T, stride=tile_cols)
            out_ref[at, :] = out_ref[at, :] + got_block(got_ref, n)

        return 0

    lax.fori_loop(0, slot_ref.shape[0], step, 0)


def rest(slots, got, base, tile_rows, tile_cols):
    size = T * tile_cols
    block = pl.BlockSpec((size, T), lambda a, s: (a, 0))
    return pl.pallas_call(
        functools.partial(rest_kernel, tile_cols, tile_rows * tile_cols),
        out_shape=jax.ShapeDtypeStruct(base.shape, F32),
        grid_spec=pltpu.PrefetchScalarGridSpec(
            num_scalar_prefetch=1,
            grid=(tile_rows,),
            in_specs=[pl.BlockSpec(got.shape, lambda a, s: (0, 0, 0)), block],
            out_specs=block,
        ),
        compiler_params=params(),
        cost_estimate=pl.CostEstimate(flops=10_000_000_000, bytes_accessed=26_000_000, transcendentals=0),
        name="rest",
    )(slots, got, base)


def share_kernel(order_ref, x0, x1, x2, x3, wt_ref, out_ref):
    total = None
    for m, x in enumerate((x0, x1, x2, x3)):
        term = dot3(x[...], wt_ref[order_ref[m]], NN)
        total = term if total is None else total + term
    out_ref[...] = total


def share_solve(order, parts, wt):
    return pl.pallas_call(
        share_kernel,
        out_shape=jax.ShapeDtypeStruct((parts[0].shape[0], 4 * T), F32),
        grid_spec=pltpu.PrefetchScalarGridSpec(
            num_scalar_prefetch=1, grid=(), in_specs=[VM()] * 5, out_specs=VM()
        ),
        compiler_params=params(),
        name="share_solve",
    )(order, *parts, wt)


def rows_kernel(info_ref, x0, x1, x2, x3, wt_ref, lhs_ref, own_ref):
    my_col, zero_first = info_ref[4], info_ref[5]
    total = None
    for m, x in enumerate((x0, x1, x2, x3)):
        term = dot3(x[...], wt_ref[info_ref[m]], NN)
        total = term if total is None else total + term
    for j in range(4):
        @pl.when(my_col == j)
        def _():
            own_ref[...] = total[:, j * T : (j + 1) * T]

    row = lax.broadcasted_iota(jnp.int32, total.shape, 0)
    total = jnp.where((row < T) & (zero_first == 1), 0.0, total)
    high, low = split(total)
    lhs_ref[:, 0:512] = high
    lhs_ref[:, 512:1024] = high
    lhs_ref[:, 1024:1536] = low


def rows_solve(info, parts, wt):
    rows = parts[0].shape[0]
    return pl.pallas_call(
        rows_kernel,
        out_shape=(jax.ShapeDtypeStruct((rows, 12 * T), BF16), jax.ShapeDtypeStruct((rows, T), F32)),
        grid_spec=pltpu.PrefetchScalarGridSpec(
            num_scalar_prefetch=1, grid=(), in_specs=[VM()] * 5, out_specs=(VM(), VM())
        ),
        compiler_params=params(),
        cost_estimate=pl.CostEstimate(flops=4_000_000_000, bytes_accessed=8_000_000, transcendentals=0),
        name="rows_solve",
    )(info, *parts, wt)


def update_kernel(tile_cols, group, g_ref, lhs_ref, own_ref, base_ref, out_ref, rhs_ref):
    pairs = tile_cols // 2

    @pl.when(pl.program_id(0) == 0)
    def _():
        for q in range(pairs):
            x = g_ref[:, 32 * q : 32 * q + 32, :].reshape(2 * T, 4 * T)
            high, low = split(x)
            rhs_ref[q, :, 0:512] = high
            rhs_ref[q, :, 512:1024] = low
            rhs_ref[q, :, 1024:1536] = high

    for q in range(pairs):
        u = lax.dot_general(lhs_ref[...], rhs_ref[q], NT, preferred_element_type=F32)
        for a in range(group):
            for b in (2 * q, 2 * q + 1):
                at = pl.ds(a * T * tile_cols + b, T, stride=tile_cols)
                if b == 0:
                    out_ref[at, :] = own_ref[a * T : (a + 1) * T, :]
                else:
                    h = b - 2 * q
                    out_ref[at, :] = base_ref[at, :] - u[a * T : (a + 1) * T, h * T : (h + 1) * T]


def update(gathered, lhs, own, base, tile_rows, tile_cols):
    group = 3
    size = group * T * tile_cols
    return pl.pallas_call(
        functools.partial(update_kernel, tile_cols, group),
        out_shape=jax.ShapeDtypeStruct(base.shape, F32),
        grid=(tile_rows // group,),
        in_specs=[
            pl.BlockSpec(gathered.shape, lambda a: (0, 0, 0)),
            pl.BlockSpec((group * T, 12 * T), lambda a: (a, 0)),
            pl.BlockSpec((group * T, T), lambda a: (a, 0)),
            pl.BlockSpec((size, T), lambda a: (a, 0)),
        ],
        out_specs=pl.BlockSpec((size, T), lambda a: (a, 0)),
        scratch_shapes=[pltpu.VMEM((tile_cols // 2, 2 * T, 12 * T), BF16)],
        compiler_params=params(),
        name="update",
    )(gathered, lhs, own, base)


def local(front, child_updates, child_owner, child_rows, child_cols, child_slot):
    my_row = lax.axis_index("row")
    my_col = lax.axis_index("col")
    tile_rows, tile_cols = front.shape[1], front.shape[4]
    slot_total = tile_rows * tile_cols
    flat = front.reshape(tile_rows * T * tile_cols, T)
    base_panel = front[0, :, 0, :, 0, 0, :].reshape(tile_rows * T, T)

    send = route(child_owner[0, :, 0], child_slot[0], child_updates[0], child_rows[0], child_cols[0], 32, slot_total)
    got = lax.all_to_all(send, ("row", "col"), split_axis=0, concat_axis=0, tiled=True)

    lead = lax.all_gather(base_panel[:T], "row", axis=0)
    lead = lax.all_gather(lead[:4], "col", axis=0)
    wt = leading_inverse(lead)

    slots = got[:, 2 * T + 4 : 2 * T + 6, 0].astype(jnp.int32).reshape(64)
    columns = panel(slots, got, base_panel, tile_cols, slot_total)

    pieces = columns.reshape(tile_rows, 4, T // 4, T)
    parts = []
    for m in range(4):
        piece = lax.dynamic_index_in_dim(pieces, (my_col + m) % 4, axis=1, keepdims=False)
        piece = piece.reshape(tile_rows * T // 4, T)
        moves = [
            ((4 * h + c) * 4 + j, (4 * h + (j + m) % 4) * 4 + c) for h in range(2) for c in range(4) for j in range(4)
        ]
        parts.append(lax.ppermute(piece, ("row", "col"), moves))
    order = (my_row - jnp.arange(4, dtype=jnp.int32)) % 4
    share = share_solve(order, parts, wt)
    gathered = lax.all_gather(share, "row", axis=0)

    right = [(i, (i + 1) % 4) for i in range(4)]
    left = [(i, (i - 1) % 4) for i in range(4)]
    half = tile_rows * T // 2
    from_left = lax.ppermute(columns, "col", right)
    from_right = lax.ppermute(columns, "col", left)
    far_top = lax.ppermute(from_left[:half], "col", right)
    far_bottom = lax.ppermute(from_right[half:], "col", left)
    far = jnp.concatenate([far_top, far_bottom], axis=0)
    info = jnp.concatenate(
        [
            (my_col + jnp.array([0, -1, 1, 2], jnp.int32)) % 4,
            jnp.stack([my_col, (my_row < 4).astype(jnp.int32)]).astype(jnp.int32),
        ]
    )
    lhs, own = rows_solve(info, (columns, from_left, from_right, far), wt)
    base = rest(slots, got, flat, tile_rows, tile_cols)
    result = update(gathered, lhs, own, base, tile_rows, tile_cols)
    return result.reshape(front.shape)


def solution(mesh):
    in_specs = (
        P("front", None, "row", None, None, "col", None),
        P("front", ("row", "col"), None, None),
        P("front", ("row", "col"), None),
        P("front", ("row", "col"), None),
        P("front", ("row", "col"), None),
        P("front", ("row", "col")),
    )
    out_specs = P("front", None, "row", None, None, "col", None)
    return jax.shard_map(local, mesh=mesh, in_specs=in_specs, out_specs=out_specs, check_vma=False)
```

```python
import functools

import jax
import jax.numpy as jnp
from jax import lax
from jax.experimental import pallas as pl
from jax.experimental.pallas import tpu as pltpu
from jax.sharding import PartitionSpec as P

T = 128
F32 = jnp.float32
BF16 = jnp.bfloat16
HIGHEST = lax.Precision.HIGHEST
NT = (((1,), (1,)), ((), ()))
NN = (((1,), (0,)), ((), ()))
VM = functools.partial(pl.BlockSpec, memory_space=pltpu.VMEM)
ANY = functools.partial(pl.BlockSpec, memory_space=pl.ANY)
LIMIT = 60 * 1024 * 1024


def params():
    return pltpu.CompilerParams(vmem_limit_bytes=LIMIT)


def split(x):
    high = x.astype(BF16)
    low = (x - high.astype(F32)).astype(BF16)
    return high, low


def placed_block(block, rows, cols):
    inner = lax.broadcasted_iota(jnp.int32, (T, T), 0)
    row_hot = jnp.where(inner == rows, 1.0, 0.0).astype(BF16)
    col_hot = jnp.where(inner == cols, 1.0, 0.0).astype(BF16)
    high, low = split(block)
    x = lax.dot_general(
        jnp.concatenate([row_hot, row_hot], axis=1), jnp.concatenate([high, low], axis=0), NN, preferred_element_type=F32
    )
    high, low = split(x)
    return lax.dot_general(
        jnp.concatenate([high, low], axis=1), jnp.concatenate([col_hot, col_hot], axis=1), NT, preferred_element_type=F32
    )


def route_kernel(group, slot_total, owner_ref, slot_ref, blocks_ref, rows_ref, cols_ref, send_ref, meta, held, count, sem):
    owners = meta.shape[0]
    blocks = held.shape[0]
    step = pl.program_id(0)

    def at(g, o, k):
        return pltpu.make_async_copy(
            held.at[g], send_ref.at[o, pl.ds(pl.multiple_of(k * T, T), T), :], sem.at[g]
        )

    @pl.when(step == 0)
    def _():
        meta[...] = jnp.full(meta.shape, float(slot_total), F32)

        def clear(o, _):
            count[o] = 0
            return 0

        lax.fori_loop(0, owners, clear, 0)

    for q in range(group):
        g = step * group + q
        held[g] = placed_block(blocks_ref[q], rows_ref[pl.ds(g, 1), :], cols_ref[pl.ds(g, 1), :])
    for q in range(group):
        g = step * group + q
        o = owner_ref[g]
        k = jnp.minimum(count[o], 1)
        count[o] = k + 1
        meta[o, pl.ds(k, 1), :] = jnp.full((1, T), slot_ref[g], jnp.int32).astype(F32)
        at(g, o, k).start()

    @pl.when(step == pl.num_programs(0) - 1)
    def _():
        tail = pltpu.make_async_copy(meta, send_ref.at[:, pl.ds(2 * T, 8), :], sem.at[blocks])
        tail.start()

        def finish(g, _):
            at(g, 0, 0).wait()
            return 0

        lax.fori_loop(0, blocks, finish, 0)
        tail.wait()


def route(owner, slot, blocks, rows, cols, owners, slot_total):
    count = blocks.shape[0]
    group = 4
    whole = pl.BlockSpec((count, T), lambda i, *_: (0, 0))
    return pl.pallas_call(
        functools.partial(route_kernel, group, slot_total),
        out_shape=jax.ShapeDtypeStruct((owners, 2 * T + 8, T), F32),
        grid_spec=pltpu.PrefetchScalarGridSpec(
            num_scalar_prefetch=2,
            grid=(count // group,),
            in_specs=[pl.BlockSpec((group, T, T), lambda i, *_: (i, 0, 0)), whole, whole],
            out_specs=ANY(),
            scratch_shapes=[
                pltpu.VMEM((owners, 8, T), F32),
                pltpu.VMEM((count, T, T), F32),
                pltpu.SMEM((owners,), jnp.int32),
                pltpu.SemaphoreType.DMA((count + 1,)),
            ],
        ),
        compiler_params=params(),
        name="route",
    )(owner, slot, blocks, rows, cols)


def sub_row(x, k):
    return jnp.broadcast_to(x[k : k + 1, :], (8, T))


def lane_col(x, k):
    return jnp.broadcast_to(x[:, k : k + 1], (8, T))


def tree_sum(x):
    while len(x) > 1:
        x = [x[i] + x[i + 1] for i in range(0, len(x), 2)]
    return x[0]


def inverse_factor(s, out_ref):
    groups = T // 8
    lane = lax.broadcasted_iota(jnp.int32, (8, T), 1)
    sub = lax.broadcasted_iota(jnp.int32, (8, T), 0)
    m = [s[8 * g : 8 * g + 8, :] for g in range(groups)]
    e = [jnp.where(lane == sub + 8 * g, 1.0, 0.0).astype(F32) for g in range(groups)]
    for p in range(groups):
        v = [sub_row(m[p], k) for k in range(8)]
        x = [sub_row(e[p], k) for k in range(8)]
        column = [lane_col(m[p], 8 * p + c) for c in range(8)]
        d = [[sub_row(column[c], r) if c <= r else None for c in range(8)] for r in range(8)]
        below = {g: [lane_col(m[g], 8 * p + c) for c in range(8)] for g in range(p + 1, groups)}
        inv = [None] * 8
        low = [[None] * 8 for _ in range(8)]
        for k in range(8):
            inv[k] = 1.0 / d[k][k]
            for r in range(k + 1, 8):
                low[r][k] = d[r][k] * inv[k]
            for r in range(k + 1, 8):
                for c in range(k + 1, r + 1):
                    d[r][c] = d[r][c] - low[r][k] * d[c][k]
                v[r] = v[r] - low[r][k] * v[k]
                x[r] = x[r] - low[r][k] * x[k]
        for k in range(8):
            out_ref[8 * p + k : 8 * p + k + 1, :] = (x[k] * lax.sqrt(inv[k]))[0:1, :]
        if p == groups - 1:
            break
        v = [v[k] * inv[k] for k in range(8)]
        x = [x[k] * inv[k] for k in range(8)]
        for k in range(7, 0, -1):
            for j in range(k):
                v[j] = v[j] - low[k][j] * v[k]
                x[j] = x[j] - low[k][j] * x[k]
        for g in range(p + 1, groups):
            m[g] = m[g] - tree_sum([below[g][k] * v[k] for k in range(8)])
            e[g] = e[g] - tree_sum([below[g][k] * x[k] for k in range(8)])


def leading_kernel(lead_ref, high_ref, low_ref, s_ref, e_ref, w_ref):
    n = 4
    dot = functools.partial(lax.dot_general, precision=HIGHEST, preferred_element_type=F32)
    for i in range(n):
        for j in range(i + 1):
            s_ref[i, j] = 0.5 * (lead_ref[i, j] + lead_ref[j, i].T)
    e_ref[...] = jnp.zeros_like(e_ref)

    def step(k, _):
        inverse_factor(s_ref[k, k], w_ref)
        wk = w_ref[...]
        own = dot(wk, e_ref[k], NN)
        column = lax.broadcasted_iota(jnp.int32, (T, n * T), 1)
        spread = jnp.concatenate([wk] * n, axis=1)
        own = jnp.where(column // T == k, spread, own)
        for j in range(n):
            at = pl.ds(pl.multiple_of(k * T, T), T)
            high, low = split(own[:, j * T : (j + 1) * T].T)
            high_ref[j, :, at] = high
            low_ref[j, :, at] = low

        for i in range(1, n):
            @pl.when(i > k)
            def _():
                lik = dot(s_ref[i, k], wk, NT)
                s_ref[i, k] = lik
                e_ref[i] = e_ref[i] - dot(lik, own, NN)
                for j in range(1, i + 1):
                    @pl.when(j > k)
                    def _():
                        s_ref[i, j] = s_ref[i, j] - dot(lik, s_ref[j, k], NT)
        return 0

    lax.fori_loop(0, n, step, 0)


def leading_inverse(lead):
    return pl.pallas_call(
        leading_kernel,
        out_shape=(jax.ShapeDtypeStruct((4, T, 4 * T), BF16),) * 2,
        in_specs=[VM()],
        out_specs=(VM(), VM()),
        scratch_shapes=[
            pltpu.VMEM((4, 4, T, T), F32),
            pltpu.VMEM((4, T, 4 * T), F32),
            pltpu.VMEM((T, T), F32),
        ],
        compiler_params=params(),
        cost_estimate=pl.CostEstimate(flops=60_000_000_000, bytes_accessed=2_000_000, transcendentals=0),
        name="leading_inverse",
    )(lead)


def panel_kernel(tile_cols, slot_total, slot_ref, col_ref, got_ref, base_ref, out_ref, p0, p1, p2, p3, held, sem):
    total = slot_ref.shape[0]

    def wanted(n):
        slot = slot_ref[n]
        return (slot < slot_total) & (slot % tile_cols == 0)

    def copy(n):
        block = got_ref.at[n // 2, pl.ds(pl.multiple_of(n % 2 * T, T), T), :]
        return pltpu.make_async_copy(block, held.at[n], sem.at[n])

    def fetch(n, _):
        @pl.when(wanted(n))
        def _():
            copy(n).start()

        return 0

    lax.fori_loop(0, total, fetch, 0)
    out_ref[...] = base_ref[...]

    def add(n, _):
        @pl.when(wanted(n))
        def _():
            copy(n).wait()
            a = pl.ds(pl.multiple_of(slot_ref[n] // tile_cols * T, T), T)
            out_ref[a, :] = out_ref[a, :] + held[n]

        return 0

    lax.fori_loop(0, total, add, 0)
    quarter = T // 4
    for m, piece in enumerate((p0, p1, p2, p3)):
        first = lax.rem(col_ref[0] + m, 4) * quarter
        for a in range(out_ref.shape[0] // T):
            piece[a * quarter : (a + 1) * quarter, :] = out_ref[pl.ds(pl.multiple_of(a * T + first, quarter), quarter), :]


def panel(slots, col, got, base, tile_cols, slot_total):
    rows = base.shape[0]
    total = slots.shape[0]
    return pl.pallas_call(
        functools.partial(panel_kernel, tile_cols, slot_total),
        out_shape=(jax.ShapeDtypeStruct((rows, T), F32),) + (jax.ShapeDtypeStruct((rows // 4, T), F32),) * 4,
        grid_spec=pltpu.PrefetchScalarGridSpec(
            num_scalar_prefetch=2,
            grid=(),
            in_specs=[ANY(), VM()],
            out_specs=(VM(),) * 5,
            scratch_shapes=[pltpu.VMEM((total, T, T), F32), pltpu.SemaphoreType.DMA((total,))],
        ),
        compiler_params=params(),
        name="panel",
    )(slots, col, got, base)


def rest_kernel(tile_cols, slot_total, slot_ref, got_ref, base_ref, out_ref):
    a = pl.program_id(0)
    out_ref[...] = base_ref[...]

    def step(n, _):
        slot = slot_ref[n]
        b = slot - a * tile_cols

        @pl.when((b > 0) & (b < tile_cols))
        def _():
            at = pl.ds(b, T, stride=tile_cols)
            out_ref[at, :] = out_ref[at, :] + got_ref[n // 2, pl.ds(pl.multiple_of(n % 2 * T, T), T), :]

        return 0

    lax.fori_loop(0, slot_ref.shape[0], step, 0)


def rest(slots, got, base, tile_rows, tile_cols):
    size = T * tile_cols
    block = pl.BlockSpec((size, T), lambda a, s: (a, 0))
    return pl.pallas_call(
        functools.partial(rest_kernel, tile_cols, tile_rows * tile_cols),
        out_shape=jax.ShapeDtypeStruct(base.shape, F32),
        grid_spec=pltpu.PrefetchScalarGridSpec(
            num_scalar_prefetch=1,
            grid=(tile_rows,),
            in_specs=[pl.BlockSpec(got.shape, lambda a, s: (0, 0, 0)), block],
            out_specs=block,
        ),
        compiler_params=params(),
        cost_estimate=pl.CostEstimate(flops=10_000_000_000, bytes_accessed=26_000_000, transcendentals=0),
        name="rest",
    )(slots, got, base)


def load_rhs(order_ref, high_ref, low_ref, rhs_ref):
    for m in range(4):
        high, low = high_ref[order_ref[m]], low_ref[order_ref[m]]
        rhs_ref[m * T : (m + 1) * T, :] = high
        rhs_ref[(4 + m) * T : (5 + m) * T, :] = low
        rhs_ref[(8 + m) * T : (9 + m) * T, :] = high


def times_wt(parts, rhs_ref):
    pairs = [split(x) for x in parts]
    high, low = [p[0] for p in pairs], [p[1] for p in pairs]
    return lax.dot_general(
        jnp.concatenate(high + high + low, axis=1), rhs_ref[...], NN, preferred_element_type=F32
    )


def share_kernel(order_ref, x0, x1, x2, x3, high_ref, low_ref, out_ref, rhs_ref):
    load_rhs(order_ref, high_ref, low_ref, rhs_ref)
    out_ref[...] = times_wt([x[...] for x in (x0, x1, x2, x3)], rhs_ref)


def share_solve(order, parts, wt):
    return pl.pallas_call(
        share_kernel,
        out_shape=jax.ShapeDtypeStruct((parts[0].shape[0], 4 * T), F32),
        grid_spec=pltpu.PrefetchScalarGridSpec(
            num_scalar_prefetch=1,
            grid=(),
            in_specs=[VM()] * 6,
            out_specs=VM(),
            scratch_shapes=[pltpu.VMEM((12 * T, 4 * T), BF16)],
        ),
        compiler_params=params(),
        name="share_solve",
    )(order, *parts, *wt)


def rows_kernel(info_ref, x0, x1, x2, x3, high_ref, low_ref, lhs_ref, own_ref, rhs_ref):
    load_rhs(info_ref, high_ref, low_ref, rhs_ref)
    my_col, zero_first = info_ref[4], info_ref[5]
    chunk = 3 * T
    for c in range(x0.shape[0] // chunk):
        at = slice(c * chunk, (c + 1) * chunk)
        total = times_wt([x[at, :] for x in (x0, x1, x2, x3)], rhs_ref)
        for j in range(4):
            @pl.when(my_col == j)
            def _():
                own_ref[at, :] = total[:, j * T : (j + 1) * T]

        if c == 0:
            row = lax.broadcasted_iota(jnp.int32, total.shape, 0)
            total = jnp.where((row < T) & (zero_first == 1), 0.0, total)
        high, low = split(total)
        lhs_ref[at, 0:512] = high
        lhs_ref[at, 512:1024] = high
        lhs_ref[at, 1024:1536] = low


def rows_solve(info, parts, wt):
    rows = parts[0].shape[0]
    return pl.pallas_call(
        rows_kernel,
        out_shape=(jax.ShapeDtypeStruct((rows, 12 * T), BF16), jax.ShapeDtypeStruct((rows, T), F32)),
        grid_spec=pltpu.PrefetchScalarGridSpec(
            num_scalar_prefetch=1,
            grid=(),
            in_specs=[VM()] * 6,
            out_specs=(VM(), VM()),
            scratch_shapes=[pltpu.VMEM((12 * T, 4 * T), BF16)],
        ),
        compiler_params=params(),
        cost_estimate=pl.CostEstimate(flops=4_000_000_000, bytes_accessed=8_000_000, transcendentals=0),
        name="rows_solve",
    )(info, *parts, *wt)


def update_kernel(tile_cols, group, g_ref, lhs_ref, own_ref, base_ref, out_ref, rhs_ref):
    pairs = tile_cols // 2

    @pl.when(pl.program_id(0) == 0)
    def _():
        for q in range(pairs):
            x = g_ref[:, 32 * q : 32 * q + 32, :].reshape(2 * T, 4 * T)
            high, low = split(x)
            rhs_ref[q, :, 0:512] = high
            rhs_ref[q, :, 512:1024] = low
            rhs_ref[q, :, 1024:1536] = high

    for q in range(pairs):
        u = lax.dot_general(lhs_ref[...], rhs_ref[q], NT, preferred_element_type=F32)
        for a in range(group):
            for b in (2 * q, 2 * q + 1):
                at = pl.ds(a * T * tile_cols + b, T, stride=tile_cols)
                if b == 0:
                    out_ref[at, :] = own_ref[a * T : (a + 1) * T, :]
                else:
                    h = b - 2 * q
                    out_ref[at, :] = base_ref[at, :] - u[a * T : (a + 1) * T, h * T : (h + 1) * T]


def update(gathered, lhs, own, base, tile_rows, tile_cols):
    group = 3
    size = group * T * tile_cols
    return pl.pallas_call(
        functools.partial(update_kernel, tile_cols, group),
        out_shape=jax.ShapeDtypeStruct(base.shape, F32),
        grid=(tile_rows // group,),
        in_specs=[
            pl.BlockSpec(gathered.shape, lambda a: (0, 0, 0)),
            pl.BlockSpec((group * T, 12 * T), lambda a: (a, 0)),
            pl.BlockSpec((group * T, T), lambda a: (a, 0)),
            pl.BlockSpec((size, T), lambda a: (a, 0)),
        ],
        out_specs=pl.BlockSpec((size, T), lambda a: (a, 0)),
        scratch_shapes=[pltpu.VMEM((tile_cols // 2, 2 * T, 12 * T), BF16)],
        compiler_params=params(),
        name="update",
    )(gathered, lhs, own, base)


def local(front, child_updates, child_owner, child_rows, child_cols, child_slot):
    my_row = lax.axis_index("row")
    my_col = lax.axis_index("col")
    tile_rows, tile_cols = front.shape[1], front.shape[4]
    slot_total = tile_rows * tile_cols
    flat = front.reshape(tile_rows * T * tile_cols, T)
    base_panel = front[0, :, 0, :, 0, 0, :].reshape(tile_rows * T, T)

    send = route(child_owner[0, :, 0], child_slot[0], child_updates[0], child_rows[0], child_cols[0], 32, slot_total)
    got = lax.all_to_all(send, ("row", "col"), split_axis=0, concat_axis=0, tiled=True)

    lead = lax.all_gather(base_panel[:T], ("row", "col"), axis=0)
    lead = lead.reshape(8, 4, T, T)[:4]
    wt = leading_inverse(lead)

    slots = got[:, 2 * T : 2 * T + 2, 0].astype(jnp.int32).reshape(64)
    columns, *pieces = panel(slots, my_col.reshape(1), got, base_panel, tile_cols, slot_total)

    parts = []
    for m in range(4):
        moves = [
            ((4 * h + c) * 4 + j, (4 * h + (j + m) % 4) * 4 + c) for h in range(2) for c in range(4) for j in range(4)
        ]
        parts.append(lax.ppermute(pieces[m], ("row", "col"), moves))
    order = (my_row - jnp.arange(4, dtype=jnp.int32)) % 4
    share = share_solve(order, parts, wt)
    gathered = lax.all_gather(share, "row", axis=0)

    right = [(i, (i + 1) % 4) for i in range(4)]
    left = [(i, (i - 1) % 4) for i in range(4)]
    half = tile_rows * T // 2
    from_left = lax.ppermute(columns, "col", right)
    from_right = lax.ppermute(columns, "col", left)
    far_top = lax.ppermute(from_left[:half], "col", right)
    far_bottom = lax.ppermute(from_right[half:], "col", left)
    far = jnp.concatenate([far_top, far_bottom], axis=0)
    info = jnp.concatenate(
        [
            (my_col + jnp.array([0, -1, 1, 2], jnp.int32)) % 4,
            jnp.stack([my_col, (my_row < 4).astype(jnp.int32)]).astype(jnp.int32),
        ]
    )
    lhs, own = rows_solve(info, (columns, from_left, from_right, far), wt)
    base = rest(slots, got, flat, tile_rows, tile_cols)
    result = update(gathered, lhs, own, base, tile_rows, tile_cols)
    return result.reshape(front.shape)


def solution(mesh):
    in_specs = (
        P("front", None, "row", None, None, "col", None),
        P("front", ("row", "col"), None, None),
        P("front", ("row", "col"), None),
        P("front", ("row", "col"), None),
        P("front", ("row", "col"), None),
        P("front", ("row", "col")),
    )
    out_specs = P("front", None, "row", None, None, "col", None)
    return jax.shard_map(local, mesh=mesh, in_specs=in_specs, out_specs=out_specs, check_vma=False)
```

```python
import functools

import jax
import jax.numpy as jnp
from jax import lax
from jax.experimental import pallas as pl
from jax.experimental.pallas import tpu as pltpu
from jax.sharding import PartitionSpec as P

T = 128
F32 = jnp.float32
BF16 = jnp.bfloat16
HIGHEST = lax.Precision.HIGHEST
NT = (((1,), (1,)), ((), ()))
NN = (((1,), (0,)), ((), ()))
VM = functools.partial(pl.BlockSpec, memory_space=pltpu.VMEM)
ANY = functools.partial(pl.BlockSpec, memory_space=pl.ANY)
LIMIT = 60 * 1024 * 1024


def params():
    return pltpu.CompilerParams(vmem_limit_bytes=LIMIT)


def split(x):
    high = x.astype(BF16)
    low = (x - high.astype(F32)).astype(BF16)
    return high, low


def placed_block(block, rows, cols):
    inner = lax.broadcasted_iota(jnp.int32, (T, T), 0)
    row_hot = jnp.where(inner == rows, 1.0, 0.0).astype(BF16)
    col_hot = jnp.where(inner == cols, 1.0, 0.0).astype(BF16)
    high, low = split(block)
    x = lax.dot_general(
        jnp.concatenate([row_hot, row_hot], axis=1), jnp.concatenate([high, low], axis=0), NN, preferred_element_type=F32
    )
    high, low = split(x)
    return lax.dot_general(
        jnp.concatenate([high, low], axis=1), jnp.concatenate([col_hot, col_hot], axis=1), NT, preferred_element_type=F32
    )


def route_kernel(group, slot_total, owner_ref, slot_ref, blocks_ref, rows_ref, cols_ref, send_ref, meta, held, count, sem):
    owners = meta.shape[0]
    blocks = held.shape[0]
    step = pl.program_id(0)

    def at(g, o, k):
        return pltpu.make_async_copy(
            held.at[g], send_ref.at[o, pl.ds(pl.multiple_of(k * T, T), T), :], sem.at[g]
        )

    @pl.when(step == 0)
    def _():
        meta[...] = jnp.full(meta.shape, float(slot_total), F32)

        def clear(o, _):
            count[o] = 0
            return 0

        lax.fori_loop(0, owners, clear, 0)

    for q in range(group):
        g = step * group + q
        held[g] = placed_block(blocks_ref[q], rows_ref[pl.ds(g, 1), :], cols_ref[pl.ds(g, 1), :])
    for q in range(group):
        g = step * group + q
        o = owner_ref[g]
        k = jnp.minimum(count[o], 1)
        count[o] = k + 1
        meta[o, pl.ds(k, 1), :] = jnp.full((1, T), slot_ref[g], jnp.int32).astype(F32)
        at(g, o, k).start()

    @pl.when(step == pl.num_programs(0) - 1)
    def _():
        tail = pltpu.make_async_copy(meta, send_ref.at[:, pl.ds(2 * T, 8), :], sem.at[blocks])
        tail.start()

        def finish(g, _):
            at(g, 0, 0).wait()
            return 0

        lax.fori_loop(0, blocks, finish, 0)
        tail.wait()


def route(owner, slot, blocks, rows, cols, owners, slot_total):
    count = blocks.shape[0]
    group = 4
    whole = pl.BlockSpec((count, T), lambda i, *_: (0, 0))
    return pl.pallas_call(
        functools.partial(route_kernel, group, slot_total),
        out_shape=jax.ShapeDtypeStruct((owners, 2 * T + 8, T), F32),
        grid_spec=pltpu.PrefetchScalarGridSpec(
            num_scalar_prefetch=2,
            grid=(count // group,),
            in_specs=[pl.BlockSpec((group, T, T), lambda i, *_: (i, 0, 0)), whole, whole],
            out_specs=ANY(),
            scratch_shapes=[
                pltpu.VMEM((owners, 8, T), F32),
                pltpu.VMEM((count, T, T), F32),
                pltpu.SMEM((owners,), jnp.int32),
                pltpu.SemaphoreType.DMA((count + 1,)),
            ],
        ),
        compiler_params=params(),
        name="route",
    )(owner, slot, blocks, rows, cols)


def sub_row(x, k):
    return jnp.broadcast_to(x[k : k + 1, :], (8, T))


def lane_col(x, k):
    return jnp.broadcast_to(x[:, k : k + 1], (8, T))


def tree_sum(x):
    while len(x) > 1:
        x = [x[i] + x[i + 1] for i in range(0, len(x), 2)]
    return x[0]


def inverse_factor(s, out_ref):
    groups = T // 8
    lane = lax.broadcasted_iota(jnp.int32, (8, T), 1)
    sub = lax.broadcasted_iota(jnp.int32, (8, T), 0)
    m = [s[8 * g : 8 * g + 8, :] for g in range(groups)]
    e = [jnp.where(lane == sub + 8 * g, 1.0, 0.0).astype(F32) for g in range(groups)]
    for p in range(groups):
        v = [sub_row(m[p], k) for k in range(8)]
        x = [sub_row(e[p], k) for k in range(8)]
        column = [lane_col(m[p], 8 * p + c) for c in range(8)]
        d = [[sub_row(column[c], r) if c <= r else None for c in range(8)] for r in range(8)]
        below = {g: [lane_col(m[g], 8 * p + c) for c in range(8)] for g in range(p + 1, groups)}
        inv = [None] * 8
        low = [[None] * 8 for _ in range(8)]
        for k in range(8):
            inv[k] = 1.0 / d[k][k]
            for r in range(k + 1, 8):
                low[r][k] = d[r][k] * inv[k]
            for r in range(k + 1, 8):
                for c in range(k + 1, r + 1):
                    d[r][c] = d[r][c] - low[r][k] * d[c][k]
                v[r] = v[r] - low[r][k] * v[k]
                x[r] = x[r] - low[r][k] * x[k]
        for k in range(8):
            out_ref[8 * p + k : 8 * p + k + 1, :] = (x[k] * lax.sqrt(inv[k]))[0:1, :]
        if p == groups - 1:
            break
        v = [v[k] * inv[k] for k in range(8)]
        x = [x[k] * inv[k] for k in range(8)]
        for k in range(7, 0, -1):
            for j in range(k):
                v[j] = v[j] - low[k][j] * v[k]
                x[j] = x[j] - low[k][j] * x[k]
        for g in range(p + 1, groups):
            m[g] = m[g] - tree_sum([below[g][k] * v[k] for k in range(8)])
            e[g] = e[g] - tree_sum([below[g][k] * x[k] for k in range(8)])


def leading_kernel(lead_ref, high_ref, low_ref, s_ref, e_ref, w_ref):
    n = 4
    dot = functools.partial(lax.dot_general, precision=HIGHEST, preferred_element_type=F32)


    def tile(i, j):
        return jnp.concatenate([lead_ref[4 * i + j], lead_ref[4 * (i + 4) + j]], axis=0)

    for i in range(n):
        for j in range(i + 1):
            s_ref[i, j] = 0.5 * (tile(i, j) + tile(j, i).T)
    e_ref[...] = jnp.zeros_like(e_ref)

    def step(k, _):
        inverse_factor(s_ref[k, k], w_ref)
        wk = w_ref[...]
        own = dot(wk, e_ref[k], NN)
        column = lax.broadcasted_iota(jnp.int32, (T, n * T), 1)
        spread = jnp.concatenate([wk] * n, axis=1)
        own = jnp.where(column // T == k, spread, own)
        for j in range(n):
            at = pl.ds(pl.multiple_of(k * T, T), T)
            high, low = split(own[:, j * T : (j + 1) * T].T)
            high_ref[j, :, at] = high
            low_ref[j, :, at] = low

        for i in range(1, n):
            @pl.when(i > k)
            def _():
                lik = dot(s_ref[i, k], wk, NT)
                s_ref[i, k] = lik
                e_ref[i] = e_ref[i] - dot(lik, own, NN)
                for j in range(1, i + 1):
                    @pl.when(j > k)
                    def _():
                        s_ref[i, j] = s_ref[i, j] - dot(lik, s_ref[j, k], NT)
        return 0

    lax.fori_loop(0, n, step, 0)


def leading_inverse(lead):
    return pl.pallas_call(
        leading_kernel,
        out_shape=(jax.ShapeDtypeStruct((4, T, 4 * T), BF16),) * 2,
        in_specs=[VM()],
        out_specs=(VM(), VM()),
        scratch_shapes=[
            pltpu.VMEM((4, 4, T, T), F32),
            pltpu.VMEM((4, T, 4 * T), F32),
            pltpu.VMEM((T, T), F32),
        ],
        compiler_params=params(),
        cost_estimate=pl.CostEstimate(flops=60_000_000_000, bytes_accessed=2_000_000, transcendentals=0),
        name="leading_inverse",
    )(lead)


def panel_kernel(tile_cols, slot_total, slot_ref, col_ref, got_ref, base_ref, after_ref, out_ref, p0, p1, p2, p3, held, sem):
    total = slot_ref.shape[0]

    def wanted(n):
        slot = slot_ref[n]
        return (slot < slot_total) & (slot % tile_cols == 0)

    def copy(n):
        block = got_ref.at[n // 2, pl.ds(pl.multiple_of(n % 2 * T, T), T), :]
        return pltpu.make_async_copy(block, held.at[n], sem.at[n])

    def fetch(n, _):
        @pl.when(wanted(n))
        def _():
            copy(n).start()

        return 0

    lax.fori_loop(0, total, fetch, 0, unroll=8)
    out_ref[...] = base_ref[...]

    def add(n, _):
        @pl.when(wanted(n))
        def _():
            copy(n).wait()
            a = pl.ds(pl.multiple_of(slot_ref[n] // tile_cols * T, T), T)
            out_ref[a, :] = out_ref[a, :] + held[n]

        return 0

    lax.fori_loop(0, total, add, 0, unroll=8)
    quarter = T // 4
    for m, piece in enumerate((p0, p1, p2, p3)):
        first = lax.rem(col_ref[0] + m, 4) * quarter
        for a in range(out_ref.shape[0] // T):
            piece[a * quarter : (a + 1) * quarter, :] = out_ref[pl.ds(pl.multiple_of(a * T + first, quarter), quarter), :]


def panel(slots, col, got, base, after, tile_cols, slot_total):
    rows = base.shape[0]
    total = slots.shape[0]
    return pl.pallas_call(
        functools.partial(panel_kernel, tile_cols, slot_total),
        out_shape=(jax.ShapeDtypeStruct((rows, T), F32),) + (jax.ShapeDtypeStruct((rows // 4, T), F32),) * 4,
        grid_spec=pltpu.PrefetchScalarGridSpec(
            num_scalar_prefetch=2,
            grid=(),
            in_specs=[ANY(), VM(), ANY()],
            out_specs=(VM(),) * 5,
            scratch_shapes=[pltpu.VMEM((total, T, T), F32), pltpu.SemaphoreType.DMA((total,))],
        ),
        compiler_params=params(),
        name="panel",
    )(slots, col, got, base, after)


def load_rhs(order_ref, high_ref, low_ref, rhs_ref):
    for m in range(4):
        high, low = high_ref[order_ref[m]], low_ref[order_ref[m]]
        rhs_ref[m * T : (m + 1) * T, :] = high
        rhs_ref[(4 + m) * T : (5 + m) * T, :] = low
        rhs_ref[(8 + m) * T : (9 + m) * T, :] = high


def times_wt(parts, rhs_ref):
    pairs = [split(x) for x in parts]
    high, low = [p[0] for p in pairs], [p[1] for p in pairs]
    return lax.dot_general(
        jnp.concatenate(high + high + low, axis=1), rhs_ref[...], NN, preferred_element_type=F32
    )


def share_kernel(order_ref, x0, x1, x2, x3, high_ref, low_ref, out_ref, rhs_ref):
    load_rhs(order_ref, high_ref, low_ref, rhs_ref)
    out_ref[...] = times_wt([x[...] for x in (x0, x1, x2, x3)], rhs_ref)


def share_solve(order, parts, wt):
    return pl.pallas_call(
        share_kernel,
        out_shape=jax.ShapeDtypeStruct((parts[0].shape[0], 4 * T), F32),
        grid_spec=pltpu.PrefetchScalarGridSpec(
            num_scalar_prefetch=1,
            grid=(),
            in_specs=[VM()] * 6,
            out_specs=VM(),
            scratch_shapes=[pltpu.VMEM((12 * T, 4 * T), BF16)],
        ),
        compiler_params=params(),
        name="share_solve",
    )(order, *parts, *wt)


def rows_kernel(info_ref, x0, x1, x2, x3, high_ref, low_ref, lhs_ref, own_ref, rhs_ref):
    load_rhs(info_ref, high_ref, low_ref, rhs_ref)
    my_col, zero_first = info_ref[4], info_ref[5]
    chunk = 3 * T
    for c in range(x0.shape[0] // chunk):
        at = slice(c * chunk, (c + 1) * chunk)
        total = times_wt([x[at, :] for x in (x0, x1, x2, x3)], rhs_ref)
        for j in range(4):
            @pl.when(my_col == j)
            def _():
                own_ref[at, :] = total[:, j * T : (j + 1) * T]

        if c == 0:
            row = lax.broadcasted_iota(jnp.int32, total.shape, 0)
            total = jnp.where((row < T) & (zero_first == 1), 0.0, total)
        high, low = split(total)
        lhs_ref[at, 0:512] = high
        lhs_ref[at, 512:1024] = low


def rows_solve(info, parts, wt):
    rows = parts[0].shape[0]
    return pl.pallas_call(
        rows_kernel,
        out_shape=(jax.ShapeDtypeStruct((rows, 8 * T), BF16), jax.ShapeDtypeStruct((rows, T), F32)),
        grid_spec=pltpu.PrefetchScalarGridSpec(
            num_scalar_prefetch=1,
            grid=(),
            in_specs=[VM()] * 6,
            out_specs=(VM(), VM()),
            scratch_shapes=[pltpu.VMEM((12 * T, 4 * T), BF16)],
        ),
        compiler_params=params(),
        cost_estimate=pl.CostEstimate(flops=4_000_000_000, bytes_accessed=8_000_000, transcendentals=0),
        name="rows_solve",
    )(info, *parts, *wt)


def load_columns(k, pieces, rhs_ref):
    for d, arrays in enumerate(pieces):
        quarter = pl.multiple_of((k ^ d) * 32, 32)
        for first, ref in arrays:
            for q in range(ref.shape[0] // 32):
                high, low = split(ref[32 * q : 32 * q + 32, :])
                at = pl.ds((first + q) * T + quarter, 32)
                rhs_ref[at, 0:512] = high
                rhs_ref[at, 512:1024] = low


def subtract(h, tile_cols, lhs_ref, rhs_ref, from_ref, out_ref):
    tiles = tile_cols // 2
    both = lhs_ref[...]
    lhs = jnp.concatenate([both[:, 0:512], both], axis=1)
    for q in range(0, tiles, 2):
        width = min(2, tiles - q)
        rhs = rhs_ref[q * T : (q + width) * T, :]
        rhs = jnp.concatenate([rhs, rhs[:, 0:512]], axis=1)
        u = lax.dot_general(lhs, rhs, NT, preferred_element_type=F32)
        for a in range(lhs.shape[0] // T):
            for w in range(width):
                at = pl.ds(a * T * tile_cols + 2 * (q + w) + h, T, stride=tile_cols)
                out_ref[at, :] = from_ref[at, :] - u[a * T : (a + 1) * T, w * T : (w + 1) * T]


def first_kernel(tile_cols, group, slot_ref, row_ref, x0, x1, x2, x3, lhs_ref, got_ref, base_ref, out_ref, rhs_ref):
    i = pl.program_id(0)
    h, k = row_ref[0] // 4, row_ref[0] % 4

    @pl.when(i == 0)
    def _():
        load_columns(k, [[(0, x)] for x in (x0, x1, x2, x3)], rhs_ref)

    out_ref[...] = base_ref[...]
    low = i * group * tile_cols

    def step(n, _):
        slot = slot_ref[n] - low

        @pl.when((slot >= 0) & (slot < group * tile_cols))
        def _():
            at = pl.ds(slot // tile_cols * (T * tile_cols) + slot % tile_cols, T, stride=tile_cols)
            out_ref[at, :] = out_ref[at, :] + got_ref[n // 2, pl.ds(pl.multiple_of(n % 2 * T, T), T), :]

        return 0

    lax.fori_loop(0, slot_ref.shape[0], step, 0, unroll=4)
    subtract(h, tile_cols, lhs_ref, rhs_ref, out_ref, out_ref)


def first_half(slots, row, pieces, lhs, got, base, tile_rows, tile_cols):
    group = 3
    size = group * T * tile_cols
    block = pl.BlockSpec((size, T), lambda a, *_: (a, 0))
    piece = pl.BlockSpec(pieces[0].shape, lambda a, *_: (0, 0))
    return pl.pallas_call(
        functools.partial(first_kernel, tile_cols, group),
        out_shape=jax.ShapeDtypeStruct(base.shape, F32),
        grid_spec=pltpu.PrefetchScalarGridSpec(
            num_scalar_prefetch=2,
            grid=(tile_rows // group,),
            in_specs=[piece] * 4
            + [
                pl.BlockSpec((group * T, 8 * T), lambda a, *_: (a, 0)),
                pl.BlockSpec(got.shape, lambda a, *_: (0, 0, 0)),
                block,
            ],
            out_specs=block,
            scratch_shapes=[pltpu.VMEM((tile_cols // 2 * T, 8 * T), BF16)],
        ),
        compiler_params=params(),
        cost_estimate=pl.CostEstimate(flops=12_000_000_000, bytes_accessed=30_000_000, transcendentals=0),
        name="first_half",
    )(slots, row, *pieces, lhs, got, base)


def second_kernel(tile_cols, group, row_ref, f0, f1, g0, g1, x2, x3, lhs_ref, own_ref, base_ref, out_ref, rhs_ref):
    h, k = 1 - row_ref[0] // 4, row_ref[0] % 4
    top = f0.shape[0] // 32

    @pl.when(pl.program_id(0) == 0)
    def _():
        load_columns(k, [[(0, f0), (top, f1)], [(0, g0), (top, g1)], [(0, x2)], [(0, x3)]], rhs_ref)

    for a in range(group):
        for q in range(tile_cols // 2):
            at = pl.ds(a * T * tile_cols + 2 * q + 1 - h, T, stride=tile_cols)
            out_ref[at, :] = base_ref[at, :]
    subtract(h, tile_cols, lhs_ref, rhs_ref, base_ref, out_ref)
    for a in range(group):
        out_ref[pl.ds(a * T * tile_cols, T, stride=tile_cols), :] = own_ref[a * T : (a + 1) * T, :]


def second_half(row, pieces, lhs, own, base, tile_rows, tile_cols):
    group = 3
    size = group * T * tile_cols
    block = pl.BlockSpec((size, T), lambda a, *_: (a, 0))
    return pl.pallas_call(
        functools.partial(second_kernel, tile_cols, group),
        out_shape=jax.ShapeDtypeStruct(base.shape, F32),
        grid_spec=pltpu.PrefetchScalarGridSpec(
            num_scalar_prefetch=1,
            grid=(tile_rows // group,),
            in_specs=[pl.BlockSpec(x.shape, lambda a, *_: (0, 0)) for x in pieces]
            + [
                pl.BlockSpec((group * T, 8 * T), lambda a, *_: (a, 0)),
                pl.BlockSpec((group * T, T), lambda a, *_: (a, 0)),
                block,
            ],
            out_specs=block,
            scratch_shapes=[pltpu.VMEM((tile_cols // 2 * T, 8 * T), BF16)],
        ),
        compiler_params=params(),
        name="second_half",
    )(row, *pieces, lhs, own, base)


def local(front, child_updates, child_owner, child_rows, child_cols, child_slot):
    my_row = lax.axis_index("row")
    my_col = lax.axis_index("col")
    tile_rows, tile_cols = front.shape[1], front.shape[4]
    slot_total = tile_rows * tile_cols
    flat = front.reshape(tile_rows * T * tile_cols, T)
    base_panel = front[0, :, 0, :, 0, 0, :].reshape(tile_rows * T, T)

    send = route(child_owner[0, :, 0], child_slot[0], child_updates[0], child_rows[0], child_cols[0], 32, slot_total)
    got = lax.all_to_all(send, ("row", "col"), split_axis=0, concat_axis=0, tiled=True)

    tile = base_panel[:T]
    lower = lax.ppermute(tile[T // 2 :], "row", [(r, r + 4) for r in range(4)])
    half = jnp.where(my_row < 4, tile[: T // 2], lower)
    half = jnp.broadcast_to(half[None], (32, T // 2, T))
    lead = lax.all_to_all(half, ("row", "col"), split_axis=0, concat_axis=0, tiled=True)
    wt = leading_inverse(lead)

    slots = got[:, 2 * T : 2 * T + 2, 0].astype(jnp.int32).reshape(64)
    columns, *pieces = panel(slots, my_col.reshape(1), got, base_panel, wt[1], tile_cols, slot_total)

    parts = []
    for m in range(4):
        moves = [
            ((4 * h + c) * 4 + j, (4 * h + (j + m) % 4) * 4 + c) for h in range(2) for c in range(4) for j in range(4)
        ]
        parts.append(lax.ppermute(pieces[m], ("row", "col"), moves))
    order = (my_row - jnp.arange(4, dtype=jnp.int32)) % 4
    share = share_solve(order, parts, wt)

    def swap(x, bits):
        return lax.ppermute(x, "row", [(r, r ^ bits) for r in range(8)])

    cut = 5 * T // 4
    near, far_side = swap(share, 2), swap(share, 6)
    beside = swap(share, 1)
    near_beside = swap(near, 1)
    opposite = [swap(far_side[:cut], 2), swap(near[cut:], 6)]
    far_beside = swap(far_side, 1)
    opposite_beside = [swap(x, 1) for x in opposite]

    right = [(i, (i + 1) % 4) for i in range(4)]
    left = [(i, (i - 1) % 4) for i in range(4)]
    half = tile_rows * T // 2
    from_left = lax.ppermute(columns, "col", right)
    from_right = lax.ppermute(columns, "col", left)
    far_top = lax.ppermute(from_left[:half], "col", right)
    far_bottom = lax.ppermute(from_right[half:], "col", left)
    far = jnp.concatenate([far_top, far_bottom], axis=0)
    info = jnp.concatenate(
        [
            (my_col + jnp.array([0, -1, 1, 2], jnp.int32)) % 4,
            jnp.stack([my_col, (my_row < 4).astype(jnp.int32)]).astype(jnp.int32),
        ]
    )
    lhs, own = rows_solve(info, (columns, from_left, from_right, far), wt)
    row = my_row.reshape(1)
    base = first_half(slots, row, (share, beside, near, near_beside), lhs, got, flat, tile_rows, tile_cols)
    others = (*opposite, *opposite_beside, far_side, far_beside)
    result = second_half(row, others, lhs, own, base, tile_rows, tile_cols)
    return result.reshape(front.shape)


def solution(mesh):
    in_specs = (
        P("front", None, "row", None, None, "col", None),
        P("front", ("row", "col"), None, None),
        P("front", ("row", "col"), None),
        P("front", ("row", "col"), None),
        P("front", ("row", "col"), None),
        P("front", ("row", "col")),
    )
    out_specs = P("front", None, "row", None, None, "col", None)
    return jax.shard_map(local, mesh=mesh, in_specs=in_specs, out_specs=out_specs, check_vma=False)
```

```python
import functools

import jax
import jax.numpy as jnp
from jax import lax
from jax.experimental import pallas as pl
from jax.experimental.pallas import tpu as pltpu
from jax.sharding import PartitionSpec as P

T = 128
F32 = jnp.float32
BF16 = jnp.bfloat16
HIGHEST = lax.Precision.HIGHEST
NT = (((1,), (1,)), ((), ()))
NN = (((1,), (0,)), ((), ()))
VM = functools.partial(pl.BlockSpec, memory_space=pltpu.VMEM)
ANY = functools.partial(pl.BlockSpec, memory_space=pl.ANY)


def params(mebibytes=60):
    return pltpu.CompilerParams(vmem_limit_bytes=mebibytes * 1024 * 1024)


def split(x):
    high = x.astype(BF16)
    low = (x - high.astype(F32)).astype(BF16)
    return high, low


def placed_block(block, rows, cols):
    inner = lax.broadcasted_iota(jnp.int32, (T, T), 0)
    row_hot = jnp.where(inner == rows, 1.0, 0.0).astype(BF16)
    col_hot = jnp.where(inner == cols, 1.0, 0.0).astype(BF16)
    high, low = split(block)
    x = lax.dot_general(
        jnp.concatenate([row_hot, row_hot], axis=1), jnp.concatenate([high, low], axis=0), NN, preferred_element_type=F32
    )
    high, low = split(x)
    return lax.dot_general(
        jnp.concatenate([high, low], axis=1), jnp.concatenate([col_hot, col_hot], axis=1), NT, preferred_element_type=F32
    )


def route_kernel(group, slot_total, owner_ref, slot_ref, blocks_ref, rows_ref, cols_ref, send_ref, meta, held, count, sem):
    owners = meta.shape[0]
    blocks = held.shape[0]
    step = pl.program_id(0)

    def at(g, o, k):
        return pltpu.make_async_copy(
            held.at[g], send_ref.at[o, pl.ds(pl.multiple_of(k * T, T), T), :], sem.at[g]
        )

    @pl.when(step == 0)
    def _():
        meta[...] = jnp.full(meta.shape, float(slot_total), F32)

        def clear(o, _):
            count[o] = 0
            return 0

        lax.fori_loop(0, owners, clear, 0)

    for q in range(group):
        g = step * group + q
        held[g] = placed_block(blocks_ref[q], rows_ref[pl.ds(g, 1), :], cols_ref[pl.ds(g, 1), :])
    for q in range(group):
        g = step * group + q
        o = owner_ref[g]
        k = jnp.minimum(count[o], 1)
        count[o] = k + 1
        meta[o, pl.ds(k, 1), :] = jnp.full((1, T), slot_ref[g], jnp.int32).astype(F32)
        at(g, o, k).start()

    @pl.when(step == pl.num_programs(0) - 1)
    def _():
        tail = pltpu.make_async_copy(meta, send_ref.at[:, pl.ds(2 * T, 8), :], sem.at[blocks])
        tail.start()

        def finish(g, _):
            at(g, 0, 0).wait()
            return 0

        lax.fori_loop(0, blocks, finish, 0)
        tail.wait()


def route(owner, slot, blocks, rows, cols, owners, slot_total):
    count = blocks.shape[0]
    group = 4
    whole = pl.BlockSpec((count, T), lambda i, *_: (0, 0))
    return pl.pallas_call(
        functools.partial(route_kernel, group, slot_total),
        out_shape=jax.ShapeDtypeStruct((owners, 2 * T + 8, T), F32),
        grid_spec=pltpu.PrefetchScalarGridSpec(
            num_scalar_prefetch=2,
            grid=(count // group,),
            in_specs=[pl.BlockSpec((group, T, T), lambda i, *_: (i, 0, 0)), whole, whole],
            out_specs=ANY(),
            scratch_shapes=[
                pltpu.VMEM((owners, 8, T), F32),
                pltpu.VMEM((count, T, T), F32),
                pltpu.SMEM((owners,), jnp.int32),
                pltpu.SemaphoreType.DMA((count + 1,)),
            ],
        ),
        compiler_params=params(16),
        name="route",
    )(owner, slot, blocks, rows, cols)


def sub_row(x, k):
    return jnp.broadcast_to(x[k : k + 1, :], (8, T))


def lane_col(x, k):
    return jnp.broadcast_to(x[:, k : k + 1], (8, T))


def tree_sum(x):
    while len(x) > 1:
        x = [x[i] + x[i + 1] for i in range(0, len(x), 2)]
    return x[0]


def inverse_factor(s, out_ref):
    groups = T // 8
    lane = lax.broadcasted_iota(jnp.int32, (8, T), 1)
    sub = lax.broadcasted_iota(jnp.int32, (8, T), 0)
    m = [s[8 * g : 8 * g + 8, :] for g in range(groups)]
    e = [jnp.where(lane == sub + 8 * g, 1.0, 0.0).astype(F32) for g in range(groups)]
    for p in range(groups):
        v = [sub_row(m[p], k) for k in range(8)]
        x = [sub_row(e[p], k) for k in range(8)]
        column = [lane_col(m[p], 8 * p + c) for c in range(8)]
        d = [[sub_row(column[c], r) if c <= r else None for c in range(8)] for r in range(8)]
        below = {g: [lane_col(m[g], 8 * p + c) for c in range(8)] for g in range(p + 1, groups)}
        inv = [None] * 8
        low = [[None] * 8 for _ in range(8)]
        for k in range(8):
            inv[k] = 1.0 / d[k][k]
            for r in range(k + 1, 8):
                low[r][k] = d[r][k] * inv[k]
            for r in range(k + 1, 8):
                for c in range(k + 1, r + 1):
                    d[r][c] = d[r][c] - low[r][k] * d[c][k]
                v[r] = v[r] - low[r][k] * v[k]
                x[r] = x[r] - low[r][k] * x[k]
        for k in range(8):
            out_ref[8 * p + k : 8 * p + k + 1, :] = (x[k] * lax.sqrt(inv[k]))[0:1, :]
        if p == groups - 1:
            break
        v = [v[k] * inv[k] for k in range(8)]
        x = [x[k] * inv[k] for k in range(8)]
        for k in range(7, 0, -1):
            for j in range(k):
                v[j] = v[j] - low[k][j] * v[k]
                x[j] = x[j] - low[k][j] * x[k]
        for g in range(p + 1, groups):
            m[g] = m[g] - tree_sum([below[g][k] * v[k] for k in range(8)])
            e[g] = e[g] - tree_sum([below[g][k] * x[k] for k in range(8)])


def leading_kernel(core_ref, mine_ref, other_ref, high_ref, low_ref, s_ref, e_ref, w_ref):
    n = 4
    dot = functools.partial(lax.dot_general, precision=HIGHEST, preferred_element_type=F32)


    def tile(i, j):
        mine, other = mine_ref[4 * i + j], other_ref[4 * i + j]
        first = core_ref[0] == 0
        return jnp.concatenate([jnp.where(first, mine, other), jnp.where(first, other, mine)], axis=0)

    for i in range(n):
        for j in range(i + 1):
            s_ref[i, j] = 0.5 * (tile(i, j) + tile(j, i).T)
    e_ref[...] = jnp.zeros_like(e_ref)

    def step(k, _):
        inverse_factor(s_ref[k, k], w_ref)
        wk = w_ref[...]
        own = dot(wk, e_ref[k], NN)
        column = lax.broadcasted_iota(jnp.int32, (T, n * T), 1)
        spread = jnp.concatenate([wk] * n, axis=1)
        own = jnp.where(column // T == k, spread, own)
        for j in range(n):
            at = pl.ds(pl.multiple_of(k * T, T), T)
            high, low = split(own[:, j * T : (j + 1) * T].T)
            high_ref[j, :, at] = high
            low_ref[j, :, at] = low

        for i in range(1, n):
            @pl.when(i > k)
            def _():
                lik = dot(s_ref[i, k], wk, NT)
                s_ref[i, k] = lik
                e_ref[i] = e_ref[i] - dot(lik, own, NN)
                for j in range(1, i + 1):
                    @pl.when(j > k)
                    def _():
                        s_ref[i, j] = s_ref[i, j] - dot(lik, s_ref[j, k], NT)
        return 0

    lax.fori_loop(0, n, step, 0)


def leading_inverse(core, mine, other):
    return pl.pallas_call(
        leading_kernel,
        out_shape=(jax.ShapeDtypeStruct((4, T, 4 * T), BF16),) * 2,
        grid_spec=pltpu.PrefetchScalarGridSpec(
            num_scalar_prefetch=1,
            grid=(),
            in_specs=[VM(), VM()],
            out_specs=(VM(), VM()),
            scratch_shapes=[
                pltpu.VMEM((4, 4, T, T), F32),
                pltpu.VMEM((4, T, 4 * T), F32),
                pltpu.VMEM((T, T), F32),
            ],
        ),
        compiler_params=params(16),
        cost_estimate=pl.CostEstimate(flops=60_000_000_000, bytes_accessed=2_000_000, transcendentals=0),
        name="leading_inverse",
    )(core, mine, other)


def panel_kernel(tile_cols, slot_total, slot_ref, col_ref, got_ref, base_ref, after_ref, out_ref, p0, p1, p2, p3, held, sem):
    total = slot_ref.shape[0]

    def wanted(n):
        slot = slot_ref[n]
        return (slot < slot_total) & (slot % tile_cols == 0)

    def copy(n):
        block = got_ref.at[n // 2, pl.ds(pl.multiple_of(n % 2 * T, T), T), :]
        return pltpu.make_async_copy(block, held.at[n], sem.at[n])

    def fetch(n, _):
        @pl.when(wanted(n))
        def _():
            copy(n).start()

        return 0

    lax.fori_loop(0, total, fetch, 0, unroll=8)
    out_ref[...] = base_ref[...]

    def add(n, _):
        @pl.when(wanted(n))
        def _():
            copy(n).wait()
            a = pl.ds(pl.multiple_of(slot_ref[n] // tile_cols * T, T), T)
            out_ref[a, :] = out_ref[a, :] + held[n]

        return 0

    lax.fori_loop(0, total, add, 0, unroll=8)
    quarter = T // 4
    for m, piece in enumerate((p0, p1, p2, p3)):
        first = lax.rem(col_ref[0] + m, 4) * quarter
        for a in range(out_ref.shape[0] // T):
            piece[a * quarter : (a + 1) * quarter, :] = out_ref[pl.ds(pl.multiple_of(a * T + first, quarter), quarter), :]


def panel(slots, col, got, base, after, tile_cols, slot_total):
    rows = base.shape[0]
    total = slots.shape[0]
    return pl.pallas_call(
        functools.partial(panel_kernel, tile_cols, slot_total),
        out_shape=(jax.ShapeDtypeStruct((rows, T), F32),) + (jax.ShapeDtypeStruct((rows // 4, T), F32),) * 4,
        grid_spec=pltpu.PrefetchScalarGridSpec(
            num_scalar_prefetch=2,
            grid=(),
            in_specs=[ANY(), VM(), ANY()],
            out_specs=(VM(),) * 5,
            scratch_shapes=[pltpu.VMEM((total, T, T), F32), pltpu.SemaphoreType.DMA((total,))],
        ),
        compiler_params=params(16),
        name="panel",
    )(slots, col, got, base, after)


def load_rhs(order_ref, high_ref, low_ref, rhs_ref):
    for m in range(4):
        high, low = high_ref[order_ref[m]], low_ref[order_ref[m]]
        rhs_ref[m * T : (m + 1) * T, :] = high
        rhs_ref[(4 + m) * T : (5 + m) * T, :] = low
        rhs_ref[(8 + m) * T : (9 + m) * T, :] = high


def times_wt(parts, rhs_ref):
    pairs = [split(x) for x in parts]
    high, low = [p[0] for p in pairs], [p[1] for p in pairs]
    return lax.dot_general(
        jnp.concatenate(high + high + low, axis=1), rhs_ref[...], NN, preferred_element_type=F32
    )


def share_kernel(order_ref, x0, x1, x2, x3, high_ref, low_ref, after_ref, out_ref, rhs_ref):
    load_rhs(order_ref, high_ref, low_ref, rhs_ref)
    out_ref[...] = times_wt([x[...] for x in (x0, x1, x2, x3)], rhs_ref)


def share_solve(order, parts, wt, after):
    return pl.pallas_call(
        share_kernel,
        out_shape=jax.ShapeDtypeStruct((parts[0].shape[0], 4 * T), F32),
        grid_spec=pltpu.PrefetchScalarGridSpec(
            num_scalar_prefetch=1,
            grid=(),
            in_specs=[VM()] * 6 + [ANY()],
            out_specs=VM(),
            scratch_shapes=[pltpu.VMEM((12 * T, 4 * T), BF16)],
        ),
        compiler_params=params(16),
        name="share_solve",
    )(order, *parts, *wt, after)


def rows_kernel(info_ref, x0, x1, x2, x3, high_ref, low_ref, lhs_ref, own_ref, rhs_ref):
    load_rhs(info_ref, high_ref, low_ref, rhs_ref)
    my_col, zero_first = info_ref[4], info_ref[5]
    chunk = 3 * T
    for c in range(x0.shape[0] // chunk):
        at = slice(c * chunk, (c + 1) * chunk)
        total = times_wt([x[at, :] for x in (x0, x1, x2, x3)], rhs_ref)
        for j in range(4):
            @pl.when(my_col == j)
            def _():
                own_ref[at, :] = total[:, j * T : (j + 1) * T]

        if c == 0:
            row = lax.broadcasted_iota(jnp.int32, total.shape, 0)
            total = jnp.where((row < T) & (zero_first == 1), 0.0, total)
        high, low = split(total)
        lhs_ref[at, 0:512] = high
        lhs_ref[at, 512:1024] = low


def rows_solve(info, parts, wt):
    rows = parts[0].shape[0]
    return pl.pallas_call(
        rows_kernel,
        out_shape=(jax.ShapeDtypeStruct((rows, 8 * T), BF16), jax.ShapeDtypeStruct((rows, T), F32)),
        grid_spec=pltpu.PrefetchScalarGridSpec(
            num_scalar_prefetch=1,
            grid=(),
            in_specs=[VM()] * 6,
            out_specs=(VM(), VM()),
            scratch_shapes=[pltpu.VMEM((12 * T, 4 * T), BF16)],
        ),
        compiler_params=params(28),
        cost_estimate=pl.CostEstimate(flops=4_000_000_000, bytes_accessed=8_000_000, transcendentals=0),
        name="rows_solve",
    )(info, *parts, *wt)


def rest_kernel(tile_cols, group, slot_ref, got_ref, base_ref, out_ref):
    out_ref[...] = base_ref[...]
    first = pl.program_id(0) * group * tile_cols

    def step(n, _):
        slot = slot_ref[n] - first

        @pl.when((slot >= 0) & (slot < group * tile_cols))
        def _():
            at = pl.ds(slot // tile_cols * (T * tile_cols) + slot % tile_cols, T, stride=tile_cols)
            out_ref[at, :] = out_ref[at, :] + got_ref[n // 2, pl.ds(pl.multiple_of(n % 2 * T, T), T), :]

        return 0

    lax.fori_loop(0, slot_ref.shape[0], step, 0, unroll=4)


def rest(slots, got, base, tile_rows, tile_cols):
    group = 3
    size = group * T * tile_cols
    block = pl.BlockSpec((size, T), lambda a, s: (a, 0))
    return pl.pallas_call(
        functools.partial(rest_kernel, tile_cols, group),
        out_shape=jax.ShapeDtypeStruct(base.shape, F32),
        grid_spec=pltpu.PrefetchScalarGridSpec(
            num_scalar_prefetch=1,
            grid=(tile_rows // group,),
            in_specs=[pl.BlockSpec(got.shape, lambda a, s: (0, 0, 0)), block],
            out_specs=block,
        ),
        compiler_params=params(40),
        cost_estimate=pl.CostEstimate(flops=10_000_000_000, bytes_accessed=26_000_000, transcendentals=0),
        name="rest",
    )(slots, got, base)


def load_columns(h, k, pieces, rhs_ref):
    for d, arrays in enumerate(pieces):
        quarter = (k ^ d) * 32 + h * T
        for first, ref in arrays:
            for q in range(ref.shape[0] // 32):
                high, low = split(ref[32 * q : 32 * q + 32, :])
                at = pl.ds(pl.multiple_of((first + q) * 2 * T + quarter, 32), 32)
                rhs_ref[at, 0:512] = high
                rhs_ref[at, 512:1024] = low


def update_kernel(tile_cols, group, row_ref, s0, s1, s2, s3, f0, f1, g0, g1, t2, t3, lhs_ref, own_ref, base_ref, out_ref, rhs_ref):
    h, k = row_ref[0] // 4, row_ref[0] % 4
    top = f0.shape[0] // 32

    @pl.when(pl.program_id(0) == 0)
    def _():
        load_columns(h, k, [[(0, x)] for x in (s0, s1, s2, s3)], rhs_ref)
        load_columns(1 - h, k, [[(0, f0), (top, f1)], [(0, g0), (top, g1)], [(0, t2)], [(0, t3)]], rhs_ref)

    both = lhs_ref[...]
    lhs = jnp.concatenate([both[:, 0:512], both], axis=1)
    for q in range(0, tile_cols, 2):
        rhs = rhs_ref[q * T : (q + 2) * T, :]
        rhs = jnp.concatenate([rhs, rhs[:, 0:512]], axis=1)
        u = lax.dot_general(lhs, rhs, NT, preferred_element_type=F32)
        for a in range(group):
            for b in (q, q + 1):
                at = pl.ds(a * T * tile_cols + b, T, stride=tile_cols)
                if b == 0:
                    out_ref[at, :] = own_ref[a * T : (a + 1) * T, :]
                else:
                    out_ref[at, :] = base_ref[at, :] - u[a * T : (a + 1) * T, (b - q) * T : (b - q + 1) * T]


def update(row, pieces, lhs, own, base, tile_rows, tile_cols):
    group = 3
    size = group * T * tile_cols
    block = pl.BlockSpec((size, T), lambda a, *_: (a, 0))
    return pl.pallas_call(
        functools.partial(update_kernel, tile_cols, group),
        out_shape=jax.ShapeDtypeStruct(base.shape, F32),
        grid_spec=pltpu.PrefetchScalarGridSpec(
            num_scalar_prefetch=1,
            grid=(tile_rows // group,),
            in_specs=[pl.BlockSpec(x.shape, lambda a, *_: (0, 0)) for x in pieces]
            + [
                pl.BlockSpec((group * T, 8 * T), lambda a, *_: (a, 0)),
                pl.BlockSpec((group * T, T), lambda a, *_: (a, 0)),
                block,
            ],
            out_specs=block,
            scratch_shapes=[pltpu.VMEM((tile_cols * T, 8 * T), BF16)],
        ),
        compiler_params=params(44),
        name="update",
    )(row, *pieces, lhs, own, base)


def local(front, child_updates, child_owner, child_rows, child_cols, child_slot):
    my_row = lax.axis_index("row")
    my_col = lax.axis_index("col")
    tile_rows, tile_cols = front.shape[1], front.shape[4]
    slot_total = tile_rows * tile_cols
    flat = front.reshape(tile_rows * T * tile_cols, T)
    base_panel = front[0, :, 0, :, 0, 0, :].reshape(tile_rows * T, T)

    send = route(child_owner[0, :, 0], child_slot[0], child_updates[0], child_rows[0], child_cols[0], 32, slot_total)

    tile = base_panel[:T].reshape(1, 2, 1, T // 2, T)
    halves = jnp.broadcast_to(tile, (4, 2, 4, T // 2, T)).reshape(32, T // 2, T)
    mine = lax.all_to_all(halves, ("row", "col"), split_axis=0, concat_axis=0, tiled=True)[:16]
    mine, send = lax.optimization_barrier((mine, send))
    other = lax.ppermute(mine, "row", [(r, r ^ 1) for r in range(8)])
    got = lax.all_to_all(send, ("row", "col"), split_axis=0, concat_axis=0, tiled=True)
    wt = leading_inverse((my_row % 2).reshape(1), mine, other)

    slots = got[:, 2 * T : 2 * T + 2, 0].astype(jnp.int32).reshape(64)
    columns, *pieces = panel(slots, my_col.reshape(1), got, base_panel, wt[1], tile_cols, slot_total)

    parts = []
    for m in range(4):
        moves = [
            ((4 * h + c) * 4 + j, (4 * h + (j + m) % 4) * 4 + c) for h in range(2) for c in range(4) for j in range(4)
        ]
        parts.append(lax.ppermute(pieces[m], ("row", "col"), moves))
    order = (my_row - jnp.arange(4, dtype=jnp.int32)) % 4
    base = rest(slots, got, flat, tile_rows, tile_cols)
    share = share_solve(order, parts, wt, base)

    def swap(x, bits):
        return lax.ppermute(x, "row", [(r, r ^ bits) for r in range(8)])

    cut = 5 * T // 4
    near, far_side = swap(share, 2), swap(share, 6)
    beside = swap(share, 1)
    near_beside = swap(near, 1)
    opposite = [swap(far_side[:cut], 2), swap(near[cut:], 6)]
    far_beside = swap(far_side, 1)
    opposite_beside = [swap(x, 1) for x in opposite]

    columns, base, *_ = lax.optimization_barrier((columns, base, *parts))
    right = [(i, (i + 1) % 4) for i in range(4)]
    left = [(i, (i - 1) % 4) for i in range(4)]
    half = tile_rows * T // 2
    from_left = lax.ppermute(columns, "col", right)
    from_right = lax.ppermute(columns, "col", left)
    far_top = lax.ppermute(from_left[:half], "col", right)
    far_bottom = lax.ppermute(from_right[half:], "col", left)
    far = jnp.concatenate([far_top, far_bottom], axis=0)
    info = jnp.concatenate(
        [
            (my_col + jnp.array([0, -1, 1, 2], jnp.int32)) % 4,
            jnp.stack([my_col, (my_row < 4).astype(jnp.int32)]).astype(jnp.int32),
        ]
    )
    lhs, own = rows_solve(info, (columns, from_left, from_right, far), wt)
    row = my_row.reshape(1)
    pieces = (share, beside, near, near_beside, *opposite, *opposite_beside, far_side, far_beside)
    result = update(row, pieces, lhs, own, base, tile_rows, tile_cols)
    return result.reshape(front.shape)


def solution(mesh):
    in_specs = (
        P("front", None, "row", None, None, "col", None),
        P("front", ("row", "col"), None, None),
        P("front", ("row", "col"), None),
        P("front", ("row", "col"), None),
        P("front", ("row", "col"), None),
        P("front", ("row", "col")),
    )
    out_specs = P("front", None, "row", None, None, "col", None)
    return jax.shard_map(local, mesh=mesh, in_specs=in_specs, out_specs=out_specs, check_vma=False)
```

```python
import functools

import jax
import jax.numpy as jnp
from jax import lax
from jax.experimental import pallas as pl
from jax.experimental.pallas import tpu as pltpu
from jax.sharding import PartitionSpec as P

T = 128
F32 = jnp.float32
BF16 = jnp.bfloat16
HIGHEST = lax.Precision.HIGHEST
NT = (((1,), (1,)), ((), ()))
NN = (((1,), (0,)), ((), ()))
VM = functools.partial(pl.BlockSpec, memory_space=pltpu.VMEM)
ANY = functools.partial(pl.BlockSpec, memory_space=pl.ANY)


def params(mebibytes=60):
    return pltpu.CompilerParams(vmem_limit_bytes=mebibytes * 1024 * 1024)


def split(x):
    high = x.astype(BF16)
    low = (x - high.astype(F32)).astype(BF16)
    return high, low


def placed_block(block, rows, cols):
    inner = lax.broadcasted_iota(jnp.int32, (T, T), 0)
    row_hot = jnp.where(inner == rows, 1.0, 0.0).astype(BF16)
    col_hot = jnp.where(inner == cols, 1.0, 0.0).astype(BF16)
    high, low = split(block)
    x = lax.dot_general(
        jnp.concatenate([row_hot, row_hot], axis=1), jnp.concatenate([high, low], axis=0), NN, preferred_element_type=F32
    )
    high, low = split(x)
    return lax.dot_general(
        jnp.concatenate([high, low], axis=1), jnp.concatenate([col_hot, col_hot], axis=1), NT, preferred_element_type=F32
    )


def route_kernel(group, slot_total, tile_cols, owner_ref, slot_ref, blocks_ref, rows_ref, cols_ref, send_ref, meta, held, count, sem):
    owners = meta.shape[0]
    blocks = held.shape[0]
    step = pl.program_id(0)

    def at(g, o, k):
        return pltpu.make_async_copy(
            held.at[g], send_ref.at[o, pl.ds(pl.multiple_of(k * T, T), T), :], sem.at[g]
        )

    @pl.when(step == 0)
    def _():
        meta[...] = jnp.full(meta.shape, float(slot_total), F32)

        def clear(o, _):
            count[o] = 0
            return 0

        lax.fori_loop(0, owners, clear, 0)

    for q in range(group):
        g = step * group + q
        held[g] = placed_block(blocks_ref[q], rows_ref[pl.ds(g, 1), :], cols_ref[pl.ds(g, 1), :])
    for q in range(group):
        g = step * group + q
        o = owner_ref[g]
        k = jnp.minimum(count[o], 1)
        count[o] = k + 1
        slot = slot_ref[g]
        panel_row = jnp.where(lax.rem(slot, tile_cols) == 0, lax.div(slot, tile_cols), slot_total)
        lane = lax.broadcasted_iota(jnp.int32, (1, T), 1)
        marks = jnp.where(lane == k, slot, panel_row).astype(F32)
        meta[o, 0:1, :] = jnp.where((lane == k) | (lane == k + 2), marks, meta[o, 0:1, :])
        at(g, o, k).start()

    @pl.when(step == pl.num_programs(0) - 1)
    def _():
        tail = pltpu.make_async_copy(meta, send_ref.at[:, pl.ds(2 * T, 8), :], sem.at[blocks])
        tail.start()

        def finish(g, _):
            at(g, 0, 0).wait()
            return 0

        lax.fori_loop(0, blocks, finish, 0)
        tail.wait()


def route(owner, slot, blocks, rows, cols, owners, slot_total, tile_cols):
    count = blocks.shape[0]
    group = 4
    whole = pl.BlockSpec((count, T), lambda i, *_: (0, 0))
    return pl.pallas_call(
        functools.partial(route_kernel, group, slot_total, tile_cols),
        out_shape=jax.ShapeDtypeStruct((owners, 2 * T + 8, T), F32),
        grid_spec=pltpu.PrefetchScalarGridSpec(
            num_scalar_prefetch=2,
            grid=(count // group,),
            in_specs=[pl.BlockSpec((group, T, T), lambda i, *_: (i, 0, 0)), whole, whole],
            out_specs=ANY(),
            scratch_shapes=[
                pltpu.VMEM((owners, 8, T), F32),
                pltpu.VMEM((count, T, T), F32),
                pltpu.SMEM((owners,), jnp.int32),
                pltpu.SemaphoreType.DMA((count + 1,)),
            ],
        ),
        compiler_params=params(16),
        name="route",
    )(owner, slot, blocks, rows, cols)


def sub_row(x, k):
    return jnp.broadcast_to(x[k : k + 1, :], (8, T))


def lane_col(x, k):
    return jnp.broadcast_to(x[:, k : k + 1], (8, T))


def tree_sum(x):
    while len(x) > 1:
        x = [x[i] + x[i + 1] for i in range(0, len(x), 2)]
    return x[0]


def inverse_factor(s, out_ref):
    groups = T // 8
    lane = lax.broadcasted_iota(jnp.int32, (8, T), 1)
    sub = lax.broadcasted_iota(jnp.int32, (8, T), 0)
    m = [s[8 * g : 8 * g + 8, :] for g in range(groups)]
    e = [jnp.where(lane == sub + 8 * g, 1.0, 0.0).astype(F32) for g in range(groups)]
    for p in range(groups):
        v = [sub_row(m[p], k) for k in range(8)]
        x = [sub_row(e[p], k) for k in range(8)]
        column = [lane_col(m[p], 8 * p + c) for c in range(8)]
        d = [[sub_row(column[c], r) if c <= r else None for c in range(8)] for r in range(8)]
        below = {g: [lane_col(m[g], 8 * p + c) for c in range(8)] for g in range(p + 1, groups)}
        inv = [None] * 8
        low = [[None] * 8 for _ in range(8)]
        for k in range(8):
            inv[k] = 1.0 / d[k][k]
            for r in range(k + 1, 8):
                low[r][k] = d[r][k] * inv[k]
            for r in range(k + 1, 8):
                for c in range(k + 1, r + 1):
                    d[r][c] = d[r][c] - low[r][k] * d[c][k]
                v[r] = v[r] - low[r][k] * v[k]
                x[r] = x[r] - low[r][k] * x[k]
        for k in range(8):
            out_ref[8 * p + k : 8 * p + k + 1, :] = (x[k] * lax.sqrt(inv[k]))[0:1, :]
        if p == groups - 1:
            break
        v = [v[k] * inv[k] for k in range(8)]
        x = [x[k] * inv[k] for k in range(8)]
        for k in range(7, 0, -1):
            for j in range(k):
                v[j] = v[j] - low[k][j] * v[k]
                x[j] = x[j] - low[k][j] * x[k]
        for g in range(p + 1, groups):
            m[g] = m[g] - tree_sum([below[g][k] * v[k] for k in range(8)])
            e[g] = e[g] - tree_sum([below[g][k] * x[k] for k in range(8)])


def leading_kernel(core_ref, mine_ref, other_ref, high_ref, low_ref, s_ref, e_ref, w_ref):
    n = 4
    dot = functools.partial(lax.dot_general, precision=HIGHEST, preferred_element_type=F32)


    def tile(i, j):
        mine, other = mine_ref[4 * i + j], other_ref[4 * i + j]
        first = core_ref[0] == 0
        return jnp.concatenate([jnp.where(first, mine, other), jnp.where(first, other, mine)], axis=0)

    for i in range(n):
        for j in range(i + 1):
            s_ref[i, j] = 0.5 * (tile(i, j) + tile(j, i).T)
    e_ref[...] = jnp.zeros_like(e_ref)

    def step(k, _):
        inverse_factor(s_ref[k, k], w_ref)
        wk = w_ref[...]
        own = dot(wk, e_ref[k], NN)
        column = lax.broadcasted_iota(jnp.int32, (T, n * T), 1)
        spread = jnp.concatenate([wk] * n, axis=1)
        own = jnp.where(column // T == k, spread, own)
        for j in range(n):
            at = pl.ds(pl.multiple_of(k * T, T), T)
            high, low = split(own[:, j * T : (j + 1) * T].T)
            high_ref[j, :, at] = high
            low_ref[j, :, at] = low

        for i in range(1, n):
            @pl.when(i > k)
            def _():
                lik = dot(s_ref[i, k], wk, NT)
                s_ref[i, k] = lik
                e_ref[i] = e_ref[i] - dot(lik, own, NN)
                for j in range(1, i + 1):
                    @pl.when(j > k)
                    def _():
                        s_ref[i, j] = s_ref[i, j] - dot(lik, s_ref[j, k], NT)
        return 0

    lax.fori_loop(0, n, step, 0)


def leading_inverse(core, mine, other):
    return pl.pallas_call(
        leading_kernel,
        out_shape=(jax.ShapeDtypeStruct((4, T, 4 * T), BF16),) * 2,
        grid_spec=pltpu.PrefetchScalarGridSpec(
            num_scalar_prefetch=1,
            grid=(),
            in_specs=[VM(), VM()],
            out_specs=(VM(), VM()),
            scratch_shapes=[
                pltpu.VMEM((4, 4, T, T), F32),
                pltpu.VMEM((4, T, 4 * T), F32),
                pltpu.VMEM((T, T), F32),
            ],
        ),
        compiler_params=params(16),
        cost_estimate=pl.CostEstimate(flops=60_000_000_000, bytes_accessed=2_000_000, transcendentals=0),
        name="leading_inverse",
    )(core, mine, other)


def panel_kernel(col_ref, got_ref, base_ref, after_ref, out_ref, p0, p1, p2, p3, held, places, sem):
    total = held.shape[0]
    tile_rows = out_ref.shape[0] // T
    look = pltpu.make_async_copy(got_ref.at[:, 2 * T, :], places, sem.at[total])
    look.start()
    out_ref[...] = base_ref[...]
    look.wait()

    def tile_row(n):
        return places[n // 2, n % 2 + 2]

    def wanted(n):
        return tile_row(n) < tile_rows

    def copy(n):
        block = got_ref.at[n // 2, pl.ds(pl.multiple_of(n % 2 * T, T), T), :]
        return pltpu.make_async_copy(block, held.at[n], sem.at[n])

    def fetch(n, _):
        @pl.when(wanted(n))
        def _():
            copy(n).start()

        return 0

    lax.fori_loop(0, total, fetch, 0, unroll=8)

    def add(n, _):
        @pl.when(wanted(n))
        def _():
            copy(n).wait()
            a = pl.ds(pl.multiple_of(tile_row(n).astype(jnp.int32) * T, T), T)
            out_ref[a, :] = out_ref[a, :] + held[n]

        return 0

    lax.fori_loop(0, total, add, 0, unroll=8)
    quarter = T // 4
    for m, piece in enumerate((p0, p1, p2, p3)):
        first = lax.rem(col_ref[0] + m, 4) * quarter
        for a in range(out_ref.shape[0] // T):
            piece[a * quarter : (a + 1) * quarter, :] = out_ref[pl.ds(pl.multiple_of(a * T + first, quarter), quarter), :]


def panel(col, got, base, after):
    rows = base.shape[0]
    total = 2 * got.shape[0]
    return pl.pallas_call(
        panel_kernel,
        out_shape=(jax.ShapeDtypeStruct((rows, T), F32),) + (jax.ShapeDtypeStruct((rows // 4, T), F32),) * 4,
        grid_spec=pltpu.PrefetchScalarGridSpec(
            num_scalar_prefetch=1,
            grid=(),
            in_specs=[ANY(), VM(), ANY()],
            out_specs=(VM(),) * 5,
            scratch_shapes=[
                pltpu.VMEM((total, T, T), F32),
                pltpu.SMEM((total // 2, T), F32),
                pltpu.SemaphoreType.DMA((total + 1,)),
            ],
        ),
        compiler_params=params(16),
        name="panel",
    )(col, got, base, after)


def load_rhs(order_ref, high_ref, low_ref, rhs_ref):
    for m in range(4):
        high, low = high_ref[order_ref[m]], low_ref[order_ref[m]]
        rhs_ref[m * T : (m + 1) * T, :] = high
        rhs_ref[(4 + m) * T : (5 + m) * T, :] = low
        rhs_ref[(8 + m) * T : (9 + m) * T, :] = high


def times_wt(parts, rhs_ref):
    pairs = [split(x) for x in parts]
    high, low = [p[0] for p in pairs], [p[1] for p in pairs]
    return lax.dot_general(
        jnp.concatenate(high + high + low, axis=1), rhs_ref[...], NN, preferred_element_type=F32
    )


def share_kernel(order_ref, x0, x1, x2, x3, high_ref, low_ref, out_ref, rhs_ref):
    load_rhs(order_ref, high_ref, low_ref, rhs_ref)
    out_ref[...] = times_wt([x[...] for x in (x0, x1, x2, x3)], rhs_ref)


def share_solve(order, parts, wt):
    return pl.pallas_call(
        share_kernel,
        out_shape=jax.ShapeDtypeStruct((parts[0].shape[0], 4 * T), F32),
        grid_spec=pltpu.PrefetchScalarGridSpec(
            num_scalar_prefetch=1,
            grid=(),
            in_specs=[VM()] * 6,
            out_specs=VM(),
            scratch_shapes=[pltpu.VMEM((12 * T, 4 * T), BF16)],
        ),
        compiler_params=params(16),
        name="share_solve",
    )(order, *parts, *wt)


def rows_kernel(info_ref, x0, x1, x2, x3, high_ref, low_ref, lhs_ref, own_ref, rhs_ref):
    load_rhs(info_ref, high_ref, low_ref, rhs_ref)
    my_col, zero_first = info_ref[4], info_ref[5]
    chunk = 3 * T
    for c in range(x0.shape[0] // chunk):
        at = slice(c * chunk, (c + 1) * chunk)
        total = times_wt([x[at, :] for x in (x0, x1, x2, x3)], rhs_ref)
        for j in range(4):
            @pl.when(my_col == j)
            def _():
                own_ref[at, :] = total[:, j * T : (j + 1) * T]

        if c == 0:
            row = lax.broadcasted_iota(jnp.int32, total.shape, 0)
            total = jnp.where((row < T) & (zero_first == 1), 0.0, total)
        high, low = split(total)
        lhs_ref[at, 0:512] = high
        lhs_ref[at, 512:1024] = low


def rows_solve(info, parts, wt):
    rows = parts[0].shape[0]
    return pl.pallas_call(
        rows_kernel,
        out_shape=(jax.ShapeDtypeStruct((rows, 8 * T), BF16), jax.ShapeDtypeStruct((rows, T), F32)),
        grid_spec=pltpu.PrefetchScalarGridSpec(
            num_scalar_prefetch=1,
            grid=(),
            in_specs=[VM()] * 6,
            out_specs=(VM(), VM()),
            scratch_shapes=[pltpu.VMEM((12 * T, 4 * T), BF16)],
        ),
        compiler_params=params(28),
        cost_estimate=pl.CostEstimate(flops=4_000_000_000, bytes_accessed=8_000_000, transcendentals=0),
        name="rows_solve",
    )(info, *parts, *wt)


def rest_kernel(tile_cols, group, slot_ref, got_ref, base_ref, out_ref):
    out_ref[...] = base_ref[...]
    first = pl.program_id(0) * group * tile_cols

    def step(n, _):
        slot = slot_ref[n] - first

        @pl.when((slot >= 0) & (slot < group * tile_cols))
        def _():
            at = pl.ds(slot // tile_cols * (T * tile_cols) + slot % tile_cols, T, stride=tile_cols)
            out_ref[at, :] = out_ref[at, :] + got_ref[n // 2, pl.ds(pl.multiple_of(n % 2 * T, T), T), :]

        return 0

    lax.fori_loop(0, slot_ref.shape[0], step, 0, unroll=4)


def rest(slots, got, base, tile_rows, tile_cols):
    group = 3
    size = group * T * tile_cols
    block = pl.BlockSpec((size, T), lambda a, s: (a, 0))
    return pl.pallas_call(
        functools.partial(rest_kernel, tile_cols, group),
        out_shape=jax.ShapeDtypeStruct(base.shape, F32),
        grid_spec=pltpu.PrefetchScalarGridSpec(
            num_scalar_prefetch=1,
            grid=(tile_rows // group,),
            in_specs=[pl.BlockSpec(got.shape, lambda a, s: (0, 0, 0)), block],
            out_specs=block,
        ),
        compiler_params=params(28),
        cost_estimate=pl.CostEstimate(flops=10_000_000_000, bytes_accessed=26_000_000, transcendentals=0),
        name="rest",
    )(slots, got, base)


def load_columns(h, k, pieces, rhs_ref):
    for d, arrays in enumerate(pieces):
        quarter = (k ^ d) * 32 + h * T
        for first, ref in arrays:
            for q in range(ref.shape[0] // 32):
                high, low = split(ref[32 * q : 32 * q + 32, :])
                at = pl.ds(pl.multiple_of((first + q) * 2 * T + quarter, 32), 32)
                rhs_ref[at, 0:512] = high
                rhs_ref[at, 512:1024] = low


def update_kernel(tile_cols, group, row_ref, s0, s1, s2, s3, f0, f1, g0, g1, t2, t3, lhs_ref, own_ref, base_ref, out_ref, rhs_ref):
    h, k = row_ref[0] // 4, row_ref[0] % 4
    top = f0.shape[0] // 32

    @pl.when(pl.program_id(0) == 0)
    def _():
        load_columns(h, k, [[(0, x)] for x in (s0, s1, s2, s3)], rhs_ref)
        load_columns(1 - h, k, [[(0, f0), (top, f1)], [(0, g0), (top, g1)], [(0, t2)], [(0, t3)]], rhs_ref)

    both = lhs_ref[...]
    lhs = jnp.concatenate([both[:, 0:512], both], axis=1)
    for q in range(0, tile_cols, 2):
        rhs = rhs_ref[q * T : (q + 2) * T, :]
        rhs = jnp.concatenate([rhs, rhs[:, 0:512]], axis=1)
        u = lax.dot_general(lhs, rhs, NT, preferred_element_type=F32)
        for a in range(group):
            for b in (q, q + 1):
                at = pl.ds(a * T * tile_cols + b, T, stride=tile_cols)
                if b == 0:
                    out_ref[at, :] = own_ref[a * T : (a + 1) * T, :]
                else:
                    out_ref[at, :] = base_ref[at, :] - u[a * T : (a + 1) * T, (b - q) * T : (b - q + 1) * T]


def update(row, pieces, lhs, own, base, tile_rows, tile_cols):
    group = 3
    size = group * T * tile_cols
    block = pl.BlockSpec((size, T), lambda a, *_: (a, 0))
    return pl.pallas_call(
        functools.partial(update_kernel, tile_cols, group),
        out_shape=jax.ShapeDtypeStruct(base.shape, F32),
        grid_spec=pltpu.PrefetchScalarGridSpec(
            num_scalar_prefetch=1,
            grid=(tile_rows // group,),
            in_specs=[pl.BlockSpec(x.shape, lambda a, *_: (0, 0)) for x in pieces]
            + [
                pl.BlockSpec((group * T, 8 * T), lambda a, *_: (a, 0)),
                pl.BlockSpec((group * T, T), lambda a, *_: (a, 0)),
                block,
            ],
            out_specs=block,
            scratch_shapes=[pltpu.VMEM((tile_cols * T, 8 * T), BF16)],
        ),
        compiler_params=params(36),
        name="update",
    )(row, *pieces, lhs, own, base)


def local(front, child_updates, child_owner, child_rows, child_cols, child_slot):
    my_row = lax.axis_index("row")
    my_col = lax.axis_index("col")
    tile_rows, tile_cols = front.shape[1], front.shape[4]
    slot_total = tile_rows * tile_cols
    flat = front.reshape(tile_rows * T * tile_cols, T)
    base_panel = front[0, :, 0, :, 0, 0, :].reshape(tile_rows * T, T)

    send = route(child_owner[0, :, 0], child_slot[0], child_updates[0], child_rows[0], child_cols[0], 32, slot_total, tile_cols)

    tile = base_panel[:T].reshape(1, 2, 1, T // 2, T)
    halves = jnp.broadcast_to(tile, (4, 2, 4, T // 2, T)).reshape(32, T // 2, T)
    mine = lax.all_to_all(halves, ("row", "col"), split_axis=0, concat_axis=0, tiled=True)[:16]
    mine, send = lax.optimization_barrier((mine, send))
    other = lax.ppermute(mine, "row", [(r, r ^ 1) for r in range(8)])
    got = lax.all_to_all(send, ("row", "col"), split_axis=0, concat_axis=0, tiled=True)
    wt = leading_inverse((my_row % 2).reshape(1), mine, other)

    columns, *pieces = panel(my_col.reshape(1), got, base_panel, wt[1])

    parts = []
    for m in range(4):
        moves = [
            ((4 * h + c) * 4 + j, (4 * h + (j + m) % 4) * 4 + c) for h in range(2) for c in range(4) for j in range(4)
        ]
        parts.append(lax.ppermute(pieces[m], ("row", "col"), moves))
    order = (my_row - jnp.arange(4, dtype=jnp.int32)) % 4
    share = share_solve(order, parts, wt)
    got, share = lax.optimization_barrier((got, share))

    def swap(x, bits):
        return lax.ppermute(x, "row", [(r, r ^ bits) for r in range(8)])

    cut = 5 * T // 4
    near, far_side = swap(share, 2), swap(share, 6)
    beside = swap(share, 1)
    columns, beside = lax.optimization_barrier((columns, beside))
    near_beside = swap(near, 1)
    slots = got[:, 2 * T, 0:2].astype(jnp.int32).reshape(64)
    base = rest(slots, got, flat, tile_rows, tile_cols)
    near, far_side, base = lax.optimization_barrier((near, far_side, base))
    opposite = [swap(far_side[:cut], 2), swap(near[cut:], 6)]
    far_beside = swap(far_side, 1)
    opposite_beside = [swap(x, 1) for x in opposite]

    right = [(i, (i + 1) % 4) for i in range(4)]
    left = [(i, (i - 1) % 4) for i in range(4)]
    half = tile_rows * T // 2
    from_left = lax.ppermute(columns, "col", right)
    from_right = lax.ppermute(columns, "col", left)
    far_top = lax.ppermute(from_left[:half], "col", right)
    far_bottom = lax.ppermute(from_right[half:], "col", left)
    far = jnp.concatenate([far_top, far_bottom], axis=0)
    info = jnp.concatenate(
        [
            (my_col + jnp.array([0, -1, 1, 2], jnp.int32)) % 4,
            jnp.stack([my_col, (my_row < 4).astype(jnp.int32)]).astype(jnp.int32),
        ]
    )
    lhs, own = rows_solve(info, (columns, from_left, from_right, far), wt)
    row = my_row.reshape(1)
    pieces = (share, beside, near, near_beside, *opposite, *opposite_beside, far_side, far_beside)
    result = update(row, pieces, lhs, own, base, tile_rows, tile_cols)
    return result.reshape(front.shape)


def solution(mesh):
    in_specs = (
        P("front", None, "row", None, None, "col", None),
        P("front", ("row", "col"), None, None),
        P("front", ("row", "col"), None),
        P("front", ("row", "col"), None),
        P("front", ("row", "col"), None),
        P("front", ("row", "col")),
    )
    out_specs = P("front", None, "row", None, None, "col", None)
    return jax.shard_map(local, mesh=mesh, in_specs=in_specs, out_specs=out_specs, check_vma=False)
```

```python
import functools

import jax
import jax.numpy as jnp
from jax import lax
from jax.experimental import pallas as pl
from jax.experimental.pallas import tpu as pltpu
from jax.sharding import PartitionSpec as P

T = 128
F32 = jnp.float32
BF16 = jnp.bfloat16
HIGHEST = lax.Precision.HIGHEST
NT = (((1,), (1,)), ((), ()))
NN = (((1,), (0,)), ((), ()))
VM = functools.partial(pl.BlockSpec, memory_space=pltpu.VMEM)
ANY = functools.partial(pl.BlockSpec, memory_space=pl.ANY)


def params(mebibytes=60):
    return pltpu.CompilerParams(vmem_limit_bytes=mebibytes * 1024 * 1024)


def split(x):
    high = x.astype(BF16)
    low = (x - high.astype(F32)).astype(BF16)
    return high, low


def placed_block(block, rows, cols):
    inner = lax.broadcasted_iota(jnp.int32, (T, T), 0)
    row_hot = jnp.where(inner == rows, 1.0, 0.0).astype(BF16)
    col_hot = jnp.where(inner == cols, 1.0, 0.0).astype(BF16)
    high, low = split(block)
    x = lax.dot_general(
        jnp.concatenate([row_hot, row_hot], axis=1), jnp.concatenate([high, low], axis=0), NN, preferred_element_type=F32
    )
    high, low = split(x)
    return lax.dot_general(
        jnp.concatenate([high, low], axis=1), jnp.concatenate([col_hot, col_hot], axis=1), NT, preferred_element_type=F32
    )


def route_kernel(group, slot_total, tile_cols, owner_ref, slot_ref, blocks_ref, rows_ref, cols_ref, send_ref, meta, held, count, sem):
    owners = meta.shape[0]
    blocks = held.shape[0]
    step = pl.program_id(0)

    def at(g, o, k):
        return pltpu.make_async_copy(
            held.at[g], send_ref.at[o, pl.ds(pl.multiple_of(k * T, T), T), :], sem.at[g]
        )

    @pl.when(step == 0)
    def _():
        meta[...] = jnp.full(meta.shape, float(slot_total), F32)

        def clear(o, _):
            count[o] = 0
            return 0

        lax.fori_loop(0, owners, clear, 0)

    for q in range(group):
        g = step * group + q
        held[g] = placed_block(blocks_ref[q], rows_ref[pl.ds(g, 1), :], cols_ref[pl.ds(g, 1), :])
    for q in range(group):
        g = step * group + q
        o = owner_ref[g]
        k = jnp.minimum(count[o], 1)
        count[o] = k + 1
        slot = slot_ref[g]
        panel_row = jnp.where(lax.rem(slot, tile_cols) == 0, lax.div(slot, tile_cols), slot_total)
        lane = lax.broadcasted_iota(jnp.int32, (1, T), 1)
        marks = jnp.where(lane == k, slot, panel_row).astype(F32)
        meta[o, 0:1, :] = jnp.where((lane == k) | (lane == k + 2), marks, meta[o, 0:1, :])
        at(g, o, k).start()

    @pl.when(step == pl.num_programs(0) - 1)
    def _():
        tail = pltpu.make_async_copy(meta, send_ref.at[:, pl.ds(2 * T, 8), :], sem.at[blocks])
        tail.start()

        def finish(g, _):
            at(g, 0, 0).wait()
            return 0

        lax.fori_loop(0, blocks, finish, 0)
        tail.wait()


def route(owner, slot, blocks, rows, cols, owners, slot_total, tile_cols):
    count = blocks.shape[0]
    group = 4
    whole = pl.BlockSpec((count, T), lambda i, *_: (0, 0))
    return pl.pallas_call(
        functools.partial(route_kernel, group, slot_total, tile_cols),
        out_shape=jax.ShapeDtypeStruct((owners, 2 * T + 8, T), F32),
        grid_spec=pltpu.PrefetchScalarGridSpec(
            num_scalar_prefetch=2,
            grid=(count // group,),
            in_specs=[pl.BlockSpec((group, T, T), lambda i, *_: (i, 0, 0)), whole, whole],
            out_specs=ANY(),
            scratch_shapes=[
                pltpu.VMEM((owners, 8, T), F32),
                pltpu.VMEM((count, T, T), F32),
                pltpu.SMEM((owners,), jnp.int32),
                pltpu.SemaphoreType.DMA((count + 1,)),
            ],
        ),
        compiler_params=params(),
        name="route",
    )(owner, slot, blocks, rows, cols)


def sub_row(x, k):
    return jnp.broadcast_to(x[k : k + 1, :], (8, T))


def lane_col(x, k):
    return jnp.broadcast_to(x[:, k : k + 1], (8, T))


def tree_sum(x):
    while len(x) > 1:
        x = [x[i] + x[i + 1] for i in range(0, len(x), 2)]
    return x[0]


def inverse_factor(s, out_ref):
    groups = T // 8
    lane = lax.broadcasted_iota(jnp.int32, (8, T), 1)
    sub = lax.broadcasted_iota(jnp.int32, (8, T), 0)
    m = [s[8 * g : 8 * g + 8, :] for g in range(groups)]
    e = [jnp.where(lane == sub + 8 * g, 1.0, 0.0).astype(F32) for g in range(groups)]
    for p in range(groups):
        v = [sub_row(m[p], k) for k in range(8)]
        x = [sub_row(e[p], k) for k in range(8)]
        column = [lane_col(m[p], 8 * p + c) for c in range(8)]
        d = [[sub_row(column[c], r) if c <= r else None for c in range(8)] for r in range(8)]
        below = {g: [lane_col(m[g], 8 * p + c) for c in range(8)] for g in range(p + 1, groups)}
        inv = [None] * 8
        low = [[None] * 8 for _ in range(8)]
        for k in range(8):
            inv[k] = 1.0 / d[k][k]
            for r in range(k + 1, 8):
                low[r][k] = d[r][k] * inv[k]
            for r in range(k + 1, 8):
                for c in range(k + 1, r + 1):
                    d[r][c] = d[r][c] - low[r][k] * d[c][k]
                v[r] = v[r] - low[r][k] * v[k]
                x[r] = x[r] - low[r][k] * x[k]
        for k in range(8):
            out_ref[8 * p + k : 8 * p + k + 1, :] = (x[k] * lax.sqrt(inv[k]))[0:1, :]
        if p == groups - 1:
            break
        v = [v[k] * inv[k] for k in range(8)]
        x = [x[k] * inv[k] for k in range(8)]
        for k in range(7, 0, -1):
            for j in range(k):
                v[j] = v[j] - low[k][j] * v[k]
                x[j] = x[j] - low[k][j] * x[k]
        for g in range(p + 1, groups):
            m[g] = m[g] - tree_sum([below[g][k] * v[k] for k in range(8)])
            e[g] = e[g] - tree_sum([below[g][k] * x[k] for k in range(8)])


def leading_kernel(core_ref, mine_ref, other_ref, high_ref, low_ref, s_ref, e_ref, w_ref):
    n = 4
    dot = functools.partial(lax.dot_general, precision=HIGHEST, preferred_element_type=F32)


    def tile(i, j):
        mine, other = mine_ref[4 * i + j], other_ref[4 * i + j]
        first = core_ref[0] == 0
        return jnp.concatenate([jnp.where(first, mine, other), jnp.where(first, other, mine)], axis=0)

    for i in range(n):
        for j in range(i + 1):
            s_ref[i, j] = 0.5 * (tile(i, j) + tile(j, i).T)
    e_ref[...] = jnp.zeros_like(e_ref)

    def step(k, _):
        inverse_factor(s_ref[k, k], w_ref)
        wk = w_ref[...]
        own = dot(wk, e_ref[k], NN)
        column = lax.broadcasted_iota(jnp.int32, (T, n * T), 1)
        spread = jnp.concatenate([wk] * n, axis=1)
        own = jnp.where(column // T == k, spread, own)
        for j in range(n):
            at = pl.ds(pl.multiple_of(k * T, T), T)
            high, low = split(own[:, j * T : (j + 1) * T].T)
            high_ref[j, :, at] = high
            low_ref[j, :, at] = low

        for i in range(1, n):
            @pl.when(i > k)
            def _():
                lik = dot(s_ref[i, k], wk, NT)
                s_ref[i, k] = lik
                e_ref[i] = e_ref[i] - dot(lik, own, NN)
                for j in range(1, i + 1):
                    @pl.when(j > k)
                    def _():
                        s_ref[i, j] = s_ref[i, j] - dot(lik, s_ref[j, k], NT)
        return 0

    lax.fori_loop(0, n, step, 0)


def leading_inverse(core, mine, other):
    return pl.pallas_call(
        leading_kernel,
        out_shape=(jax.ShapeDtypeStruct((4, T, 4 * T), BF16),) * 2,
        grid_spec=pltpu.PrefetchScalarGridSpec(
            num_scalar_prefetch=1,
            grid=(),
            in_specs=[VM(), VM()],
            out_specs=(VM(), VM()),
            scratch_shapes=[
                pltpu.VMEM((4, 4, T, T), F32),
                pltpu.VMEM((4, T, 4 * T), F32),
                pltpu.VMEM((T, T), F32),
            ],
        ),
        compiler_params=params(16),
        cost_estimate=pl.CostEstimate(flops=60_000_000_000, bytes_accessed=2_000_000, transcendentals=0),
        name="leading_inverse",
    )(core, mine, other)


def panel_kernel(col_ref, got_ref, base_ref, after_ref, out_ref, p0, p1, p2, p3, held, places, sem):
    total = held.shape[0]
    tile_rows = out_ref.shape[0] // T
    look = pltpu.make_async_copy(got_ref.at[:, 2 * T, :], places, sem.at[total])
    look.start()
    out_ref[...] = base_ref[...]
    look.wait()

    def tile_row(n):
        return places[n // 2, n % 2 + 2]

    def wanted(n):
        return tile_row(n) < tile_rows

    def copy(n):
        block = got_ref.at[n // 2, pl.ds(pl.multiple_of(n % 2 * T, T), T), :]
        return pltpu.make_async_copy(block, held.at[n], sem.at[n])

    def fetch(n, _):
        @pl.when(wanted(n))
        def _():
            copy(n).start()

        return 0

    lax.fori_loop(0, total, fetch, 0, unroll=8)

    def add(n, _):
        @pl.when(wanted(n))
        def _():
            copy(n).wait()
            a = pl.ds(pl.multiple_of(tile_row(n).astype(jnp.int32) * T, T), T)
            out_ref[a, :] = out_ref[a, :] + held[n]

        return 0

    lax.fori_loop(0, total, add, 0, unroll=8)
    quarter = T // 4
    for m, piece in enumerate((p0, p1, p2, p3)):
        first = lax.rem(col_ref[0] + m, 4) * quarter
        for a in range(out_ref.shape[0] // T):
            piece[a * quarter : (a + 1) * quarter, :] = out_ref[pl.ds(pl.multiple_of(a * T + first, quarter), quarter), :]


def panel(col, got, base, after):
    rows = base.shape[0]
    total = 2 * got.shape[0]
    return pl.pallas_call(
        panel_kernel,
        out_shape=(jax.ShapeDtypeStruct((rows, T), F32),) + (jax.ShapeDtypeStruct((rows // 4, T), F32),) * 4,
        grid_spec=pltpu.PrefetchScalarGridSpec(
            num_scalar_prefetch=1,
            grid=(),
            in_specs=[ANY(), VM(), ANY()],
            out_specs=(VM(),) * 5,
            scratch_shapes=[
                pltpu.VMEM((total, T, T), F32),
                pltpu.SMEM((total // 2, T), F32),
                pltpu.SemaphoreType.DMA((total + 1,)),
            ],
        ),
        compiler_params=params(16),
        name="panel",
    )(col, got, base, after)


def load_rhs(order_ref, high_ref, low_ref, rhs_ref):
    for m in range(4):
        high, low = high_ref[order_ref[m]], low_ref[order_ref[m]]
        rhs_ref[m * T : (m + 1) * T, :] = high
        rhs_ref[(4 + m) * T : (5 + m) * T, :] = low
        rhs_ref[(8 + m) * T : (9 + m) * T, :] = high


def times_wt(parts, rhs_ref):
    pairs = [split(x) for x in parts]
    high, low = [p[0] for p in pairs], [p[1] for p in pairs]
    return lax.dot_general(
        jnp.concatenate(high + high + low, axis=1), rhs_ref[...], NN, preferred_element_type=F32
    )


def share_kernel(order_ref, x0, x1, x2, x3, high_ref, low_ref, out_ref, rhs_ref):
    load_rhs(order_ref, high_ref, low_ref, rhs_ref)
    out_ref[...] = times_wt([x[...] for x in (x0, x1, x2, x3)], rhs_ref)


def share_solve(order, parts, wt):
    return pl.pallas_call(
        share_kernel,
        out_shape=jax.ShapeDtypeStruct((parts[0].shape[0], 4 * T), F32),
        grid_spec=pltpu.PrefetchScalarGridSpec(
            num_scalar_prefetch=1,
            grid=(),
            in_specs=[VM()] * 6,
            out_specs=VM(),
            scratch_shapes=[pltpu.VMEM((12 * T, 4 * T), BF16)],
        ),
        compiler_params=params(16),
        name="share_solve",
    )(order, *parts, *wt)


def rows_kernel(info_ref, x0, x1, x2, x3, high_ref, low_ref, lhs_ref, own_ref, rhs_ref):
    load_rhs(info_ref, high_ref, low_ref, rhs_ref)
    my_col, zero_first = info_ref[4], info_ref[5]
    chunk = 3 * T
    for c in range(x0.shape[0] // chunk):
        at = slice(c * chunk, (c + 1) * chunk)
        total = times_wt([x[at, :] for x in (x0, x1, x2, x3)], rhs_ref)
        for j in range(4):
            @pl.when(my_col == j)
            def _():
                own_ref[at, :] = total[:, j * T : (j + 1) * T]

        if c == 0:
            row = lax.broadcasted_iota(jnp.int32, total.shape, 0)
            total = jnp.where((row < T) & (zero_first == 1), 0.0, total)
        high, low = split(total)
        lhs_ref[at, 0:512] = high
        lhs_ref[at, 512:1024] = low


def rows_solve(info, parts, wt):
    rows = parts[0].shape[0]
    return pl.pallas_call(
        rows_kernel,
        out_shape=(jax.ShapeDtypeStruct((rows, 8 * T), BF16), jax.ShapeDtypeStruct((rows, T), F32)),
        grid_spec=pltpu.PrefetchScalarGridSpec(
            num_scalar_prefetch=1,
            grid=(),
            in_specs=[VM()] * 6,
            out_specs=(VM(), VM()),
            scratch_shapes=[pltpu.VMEM((12 * T, 4 * T), BF16)],
        ),
        compiler_params=params(28),
        cost_estimate=pl.CostEstimate(flops=4_000_000_000, bytes_accessed=8_000_000, transcendentals=0),
        name="rows_solve",
    )(info, *parts, *wt)


def rest_kernel(tile_cols, group, slot_ref, got_ref, base_ref, out_ref):
    out_ref[...] = base_ref[...]
    first = pl.program_id(0) * group * tile_cols

    def step(n, _):
        slot = slot_ref[n] - first

        @pl.when((slot >= 0) & (slot < group * tile_cols))
        def _():
            at = pl.ds(slot // tile_cols * (T * tile_cols) + slot % tile_cols, T, stride=tile_cols)
            out_ref[at, :] = out_ref[at, :] + got_ref[n // 2, pl.ds(pl.multiple_of(n % 2 * T, T), T), :]

        return 0

    lax.fori_loop(0, slot_ref.shape[0], step, 0, unroll=4)


def rest(slots, got, base, tile_rows, tile_cols):
    group = 3
    size = group * T * tile_cols
    block = pl.BlockSpec((size, T), lambda a, s: (a, 0))
    return pl.pallas_call(
        functools.partial(rest_kernel, tile_cols, group),
        out_shape=jax.ShapeDtypeStruct(base.shape, F32),
        grid_spec=pltpu.PrefetchScalarGridSpec(
            num_scalar_prefetch=1,
            grid=(tile_rows // group,),
            in_specs=[pl.BlockSpec(got.shape, lambda a, s: (0, 0, 0)), block],
            out_specs=block,
        ),
        compiler_params=params(54),
        cost_estimate=pl.CostEstimate(flops=10_000_000_000, bytes_accessed=26_000_000, transcendentals=0),
        name="rest",
    )(slots, got, base)


def load_columns(h, k, pieces, rhs_ref):
    for d, ref in enumerate(pieces):
        quarter = (k ^ d) * 32 + h * T
        for q in range(ref.shape[0] // 32):
            high, low = split(ref[32 * q : 32 * q + 32, :])
            at = pl.ds(pl.multiple_of(q * 2 * T + quarter, 32), 32)
            rhs_ref[at, 0:512] = high
            rhs_ref[at, 512:1024] = low


def update_kernel(tile_cols, group, row_ref, s0, s1, s2, s3, t0, t1, t2, t3, lhs_ref, own_ref, base_ref, out_ref, rhs_ref):
    h, k = row_ref[0] // 4, row_ref[0] % 4

    @pl.when(pl.program_id(0) == 0)
    def _():
        load_columns(h, k, (s0, s1, s2, s3), rhs_ref)
        load_columns(1 - h, k, (t0, t1, t2, t3), rhs_ref)

    both = lhs_ref[...]
    lhs = jnp.concatenate([both[:, 0:512], both], axis=1)
    for q in range(0, tile_cols, 2):
        rhs = rhs_ref[q * T : (q + 2) * T, :]
        rhs = jnp.concatenate([rhs, rhs[:, 0:512]], axis=1)
        u = lax.dot_general(lhs, rhs, NT, preferred_element_type=F32)
        for a in range(group):
            for b in (q, q + 1):
                at = pl.ds(a * T * tile_cols + b, T, stride=tile_cols)
                if b == 0:
                    out_ref[at, :] = own_ref[a * T : (a + 1) * T, :]
                else:
                    out_ref[at, :] = base_ref[at, :] - u[a * T : (a + 1) * T, (b - q) * T : (b - q + 1) * T]


def update(row, pieces, lhs, own, base, tile_rows, tile_cols):
    group = 3
    size = group * T * tile_cols
    block = pl.BlockSpec((size, T), lambda a, *_: (a, 0))
    return pl.pallas_call(
        functools.partial(update_kernel, tile_cols, group),
        out_shape=jax.ShapeDtypeStruct(base.shape, F32),
        grid_spec=pltpu.PrefetchScalarGridSpec(
            num_scalar_prefetch=1,
            grid=(tile_rows // group,),
            in_specs=[pl.BlockSpec(x.shape, lambda a, *_: (0, 0)) for x in pieces]
            + [
                pl.BlockSpec((group * T, 8 * T), lambda a, *_: (a, 0)),
                pl.BlockSpec((group * T, T), lambda a, *_: (a, 0)),
                block,
            ],
            out_specs=block,
            scratch_shapes=[pltpu.VMEM((tile_cols * T, 8 * T), BF16)],
        ),
        compiler_params=params(36),
        name="update",
    )(row, *pieces, lhs, own, base)


def local(front, child_updates, child_owner, child_rows, child_cols, child_slot):
    my_row = lax.axis_index("row")
    my_col = lax.axis_index("col")
    tile_rows, tile_cols = front.shape[1], front.shape[4]
    slot_total = tile_rows * tile_cols
    flat = front.reshape(tile_rows * T * tile_cols, T)
    base_panel = front[0, :, 0, :, 0, 0, :].reshape(tile_rows * T, T)

    send = route(child_owner[0, :, 0], child_slot[0], child_updates[0], child_rows[0], child_cols[0], 32, slot_total, tile_cols)

    tile = base_panel[:T].reshape(1, 2, 1, T // 2, T)
    halves = jnp.broadcast_to(tile, (4, 2, 4, T // 2, T)).reshape(32, T // 2, T)
    mine = lax.all_to_all(halves, ("row", "col"), split_axis=0, concat_axis=0, tiled=True)[:16]
    mine, send = lax.optimization_barrier((mine, send))
    other = lax.ppermute(mine, "row", [(r, r ^ 1) for r in range(8)])
    got = lax.all_to_all(send, ("row", "col"), split_axis=0, concat_axis=0, tiled=True)
    wt = leading_inverse((my_row % 2).reshape(1), mine, other)

    columns, *pieces = panel(my_col.reshape(1), got, base_panel, wt[1])

    parts = []
    for m in range(4):
        moves = [
            ((4 * h + c) * 4 + j, (4 * h + (j + m) % 4) * 4 + c) for h in range(2) for c in range(4) for j in range(4)
        ]
        parts.append(lax.ppermute(pieces[m], ("row", "col"), moves))
    order = (my_row - jnp.arange(4, dtype=jnp.int32)) % 4
    first_core = my_row % 2 == 0
    columns, parts[0] = lax.optimization_barrier((columns, parts[0]))
    from_left = lax.ppermute(columns, "col", [(c, (c + 1) % 4) for c in range(4)])
    from_right = lax.ppermute(columns, "col", [(c, (c - 1) % 4) for c in range(4)])
    far = lax.ppermute(
        jnp.where(first_core, from_left, from_right),
        ("row", "col"),
        [(r * 4 + c, r * 4 + (c + 1 - 2 * (r % 2)) % 4) for r in range(8) for c in range(4)],
    )

    share = share_solve(order, parts, wt)
    got, share = lax.optimization_barrier((got, share))

    def swap(x, bits):
        return lax.ppermute(x, "row", [(r, r ^ bits) for r in range(8)])

    near, far_side = swap(share, 2), swap(share, 6)
    beside = swap(share, 1)
    slots = got[:, 2 * T, 0:2].astype(jnp.int32).reshape(64)
    base = rest(slots, got, flat, tile_rows, tile_cols)
    near, far_side, base = lax.optimization_barrier((near, far_side, base))
    opposite = lax.ppermute(
        jnp.where(first_core, far_side, near), "row", [(r, r ^ (2 if r % 2 == 0 else 6)) for r in range(8)]
    )
    near_beside, far_beside, opposite_beside = swap(near, 1), swap(far_side, 1), swap(opposite, 1)

    info = jnp.concatenate(
        [
            (my_col + jnp.array([0, -1, 1, 2], jnp.int32)) % 4,
            jnp.stack([my_col, (my_row < 4).astype(jnp.int32)]).astype(jnp.int32),
        ]
    )
    lhs, own = rows_solve(info, (columns, from_left, from_right, far), wt)
    row = my_row.reshape(1)
    pieces = (share, beside, near, near_beside, opposite, opposite_beside, far_side, far_beside)
    result = update(row, pieces, lhs, own, base, tile_rows, tile_cols)
    return result.reshape(front.shape)


def solution(mesh):
    in_specs = (
        P("front", None, "row", None, None, "col", None),
        P("front", ("row", "col"), None, None),
        P("front", ("row", "col"), None),
        P("front", ("row", "col"), None),
        P("front", ("row", "col"), None),
        P("front", ("row", "col")),
    )
    out_specs = P("front", None, "row", None, None, "col", None)
    return jax.shard_map(local, mesh=mesh, in_specs=in_specs, out_specs=out_specs, check_vma=False)
```

```python
import functools

import jax
import jax.numpy as jnp
from jax import lax
from jax.experimental import pallas as pl
from jax.experimental.pallas import tpu as pltpu
from jax.sharding import PartitionSpec as P

T = 128
F32 = jnp.float32
BF16 = jnp.bfloat16
HIGHEST = lax.Precision.HIGHEST
NT = (((1,), (1,)), ((), ()))
NN = (((1,), (0,)), ((), ()))
VM = functools.partial(pl.BlockSpec, memory_space=pltpu.VMEM)
ANY = functools.partial(pl.BlockSpec, memory_space=pl.ANY)


def params(mebibytes=60):
    return pltpu.CompilerParams(vmem_limit_bytes=mebibytes * 1024 * 1024)


def split(x):
    high = x.astype(BF16)
    low = (x - high.astype(F32)).astype(BF16)
    return high, low


def placed_block(block, rows, cols):
    inner = lax.broadcasted_iota(jnp.int32, (T, T), 0)
    row_hot = jnp.where(inner == rows, 1.0, 0.0).astype(BF16)
    col_hot = jnp.where(inner == cols, 1.0, 0.0).astype(BF16)
    high, low = split(block)
    x = lax.dot_general(
        jnp.concatenate([row_hot, row_hot], axis=1), jnp.concatenate([high, low], axis=0), NN, preferred_element_type=F32
    )
    high, low = split(x)
    return lax.dot_general(
        jnp.concatenate([high, low], axis=1), jnp.concatenate([col_hot, col_hot], axis=1), NT, preferred_element_type=F32
    )


def route_kernel(group, slot_total, tile_cols, owner_ref, slot_ref, blocks_ref, rows_ref, cols_ref, send_ref, meta, held, count, sem):
    owners = meta.shape[0]
    blocks = held.shape[0]
    step = pl.program_id(0)

    def at(g, o, k):
        return pltpu.make_async_copy(
            held.at[g], send_ref.at[o, pl.ds(pl.multiple_of(k * T, T), T), :], sem.at[g]
        )

    @pl.when(step == 0)
    def _():
        meta[...] = jnp.full(meta.shape, float(slot_total), F32)

        def clear(o, _):
            count[o] = 0
            return 0

        lax.fori_loop(0, owners, clear, 0)

    for q in range(group):
        g = step * group + q
        held[g] = placed_block(blocks_ref[q], rows_ref[pl.ds(g, 1), :], cols_ref[pl.ds(g, 1), :])
    for q in range(group):
        g = step * group + q
        o = owner_ref[g]
        k = jnp.minimum(count[o], 1)
        count[o] = k + 1
        slot = slot_ref[g]
        panel_row = jnp.where(lax.rem(slot, tile_cols) == 0, lax.div(slot, tile_cols), slot_total)
        lane = lax.broadcasted_iota(jnp.int32, (1, T), 1)
        marks = jnp.where(lane == k, slot, panel_row).astype(F32)
        meta[o, 0:1, :] = jnp.where((lane == k) | (lane == k + 2), marks, meta[o, 0:1, :])
        at(g, o, k).start()

    @pl.when(step == pl.num_programs(0) - 1)
    def _():
        tail = pltpu.make_async_copy(meta, send_ref.at[:, pl.ds(2 * T, 8), :], sem.at[blocks])
        tail.start()

        def finish(g, _):
            at(g, 0, 0).wait()
            return 0

        lax.fori_loop(0, blocks, finish, 0)
        tail.wait()


def route(owner, slot, blocks, rows, cols, owners, slot_total, tile_cols):
    count = blocks.shape[0]
    group = 4
    whole = pl.BlockSpec((count, T), lambda i, *_: (0, 0))
    return pl.pallas_call(
        functools.partial(route_kernel, group, slot_total, tile_cols),
        out_shape=jax.ShapeDtypeStruct((owners, 2 * T + 8, T), F32),
        grid_spec=pltpu.PrefetchScalarGridSpec(
            num_scalar_prefetch=2,
            grid=(count // group,),
            in_specs=[pl.BlockSpec((group, T, T), lambda i, *_: (i, 0, 0)), whole, whole],
            out_specs=ANY(),
            scratch_shapes=[
                pltpu.VMEM((owners, 8, T), F32),
                pltpu.VMEM((count, T, T), F32),
                pltpu.SMEM((owners,), jnp.int32),
                pltpu.SemaphoreType.DMA((count + 1,)),
            ],
        ),
        compiler_params=params(),
        name="route",
    )(owner, slot, blocks, rows, cols)


def sub_row(x, k):
    return jnp.broadcast_to(x[k : k + 1, :], (8, T))


def lane_col(x, k):
    return jnp.broadcast_to(x[:, k : k + 1], (8, T))


def tree_sum(x):
    while len(x) > 1:
        x = [x[i] + x[i + 1] for i in range(0, len(x), 2)]
    return x[0]


def inverse_factor(s, out_ref):
    groups = T // 8
    lane = lax.broadcasted_iota(jnp.int32, (8, T), 1)
    sub = lax.broadcasted_iota(jnp.int32, (8, T), 0)
    m = [s[8 * g : 8 * g + 8, :] for g in range(groups)]
    e = [jnp.where(lane == sub + 8 * g, 1.0, 0.0).astype(F32) for g in range(groups)]
    for p in range(groups):
        v = [sub_row(m[p], k) for k in range(8)]
        x = [sub_row(e[p], k) for k in range(8)]
        column = [lane_col(m[p], 8 * p + c) for c in range(8)]
        d = [[sub_row(column[c], r) if c <= r else None for c in range(8)] for r in range(8)]
        below = {g: [lane_col(m[g], 8 * p + c) for c in range(8)] for g in range(p + 1, groups)}
        inv = [None] * 8
        low = [[None] * 8 for _ in range(8)]
        for k in range(8):
            inv[k] = 1.0 / d[k][k]
            for r in range(k + 1, 8):
                low[r][k] = d[r][k] * inv[k]
            for r in range(k + 1, 8):
                for c in range(k + 1, r + 1):
                    d[r][c] = d[r][c] - low[r][k] * d[c][k]
                v[r] = v[r] - low[r][k] * v[k]
                x[r] = x[r] - low[r][k] * x[k]
        for k in range(8):
            out_ref[8 * p + k : 8 * p + k + 1, :] = (x[k] * lax.sqrt(inv[k]))[0:1, :]
        if p == groups - 1:
            break
        v = [v[k] * inv[k] for k in range(8)]
        x = [x[k] * inv[k] for k in range(8)]
        for k in range(7, 0, -1):
            for j in range(k):
                v[j] = v[j] - low[k][j] * v[k]
                x[j] = x[j] - low[k][j] * x[k]
        for g in range(p + 1, groups):
            m[g] = m[g] - tree_sum([below[g][k] * v[k] for k in range(8)])
            e[g] = e[g] - tree_sum([below[g][k] * x[k] for k in range(8)])


def leading_kernel(quarter_ref, x0, x1, x2, x3, high_ref, low_ref, lead_ref, s_ref, e_ref, w_ref):
    n = 4
    dot = functools.partial(lax.dot_general, precision=HIGHEST, preferred_element_type=F32)


    for d, x in enumerate((x0, x1, x2, x3)):
        lead_ref[:, pl.ds(pl.multiple_of((quarter_ref[0] ^ d) * 32, 32), 32), :] = x[...]

    def tile(i, j):
        return lead_ref[4 * i + j]

    for i in range(n):
        for j in range(i + 1):
            s_ref[i, j] = 0.5 * (tile(i, j) + tile(j, i).T)
    e_ref[...] = jnp.zeros_like(e_ref)

    def step(k, _):
        inverse_factor(s_ref[k, k], w_ref)
        wk = w_ref[...]
        own = dot(wk, e_ref[k], NN)
        column = lax.broadcasted_iota(jnp.int32, (T, n * T), 1)
        spread = jnp.concatenate([wk] * n, axis=1)
        own = jnp.where(column // T == k, spread, own)
        for j in range(n):
            at = pl.ds(pl.multiple_of(k * T, T), T)
            high, low = split(own[:, j * T : (j + 1) * T].T)
            high_ref[j, :, at] = high
            low_ref[j, :, at] = low

        for i in range(1, n):
            @pl.when(i > k)
            def _():
                lik = dot(s_ref[i, k], wk, NT)
                s_ref[i, k] = lik
                e_ref[i] = e_ref[i] - dot(lik, own, NN)
                for j in range(1, i + 1):
                    @pl.when(j > k)
                    def _():
                        s_ref[i, j] = s_ref[i, j] - dot(lik, s_ref[j, k], NT)
        return 0

    lax.fori_loop(0, n, step, 0)


def leading_inverse(quarter, parts):
    return pl.pallas_call(
        leading_kernel,
        out_shape=(jax.ShapeDtypeStruct((4, T, 4 * T), BF16),) * 2,
        grid_spec=pltpu.PrefetchScalarGridSpec(
            num_scalar_prefetch=1,
            grid=(),
            in_specs=[VM()] * 4,
            out_specs=(VM(), VM()),
            scratch_shapes=[
                pltpu.VMEM((16, T, T), F32),
                pltpu.VMEM((4, 4, T, T), F32),
                pltpu.VMEM((4, T, 4 * T), F32),
                pltpu.VMEM((T, T), F32),
            ],
        ),
        compiler_params=params(16),
        cost_estimate=pl.CostEstimate(flops=60_000_000_000, bytes_accessed=2_000_000, transcendentals=0),
        name="leading_inverse",
    )(quarter, *parts)


def panel_kernel(col_ref, got_ref, base_ref, after_ref, out_ref, p0, p1, p2, p3, held, places, sem):
    total = held.shape[0]
    tile_rows = out_ref.shape[0] // T
    look = pltpu.make_async_copy(got_ref.at[:, 2 * T, :], places, sem.at[total])
    look.start()
    out_ref[...] = base_ref[...]
    look.wait()

    def tile_row(n):
        return places[n // 2, n % 2 + 2]

    def wanted(n):
        return tile_row(n) < tile_rows

    def copy(n):
        block = got_ref.at[n // 2, pl.ds(pl.multiple_of(n % 2 * T, T), T), :]
        return pltpu.make_async_copy(block, held.at[n], sem.at[n])

    def fetch(n, _):
        @pl.when(wanted(n))
        def _():
            copy(n).start()

        return 0

    lax.fori_loop(0, total, fetch, 0, unroll=8)

    def add(n, _):
        @pl.when(wanted(n))
        def _():
            copy(n).wait()
            a = pl.ds(pl.multiple_of(tile_row(n).astype(jnp.int32) * T, T), T)
            out_ref[a, :] = out_ref[a, :] + held[n]

        return 0

    lax.fori_loop(0, total, add, 0, unroll=8)
    quarter = T // 4
    for m, piece in enumerate((p0, p1, p2, p3)):
        first = lax.rem(col_ref[0] + m, 4) * quarter
        for a in range(out_ref.shape[0] // T):
            piece[a * quarter : (a + 1) * quarter, :] = out_ref[pl.ds(pl.multiple_of(a * T + first, quarter), quarter), :]


def panel(col, got, base, after):
    rows = base.shape[0]
    total = 2 * got.shape[0]
    return pl.pallas_call(
        panel_kernel,
        out_shape=(jax.ShapeDtypeStruct((rows, T), F32),) + (jax.ShapeDtypeStruct((rows // 4, T), F32),) * 4,
        grid_spec=pltpu.PrefetchScalarGridSpec(
            num_scalar_prefetch=1,
            grid=(),
            in_specs=[ANY(), VM(), ANY()],
            out_specs=(VM(),) * 5,
            scratch_shapes=[
                pltpu.VMEM((total, T, T), F32),
                pltpu.SMEM((total // 2, T), F32),
                pltpu.SemaphoreType.DMA((total + 1,)),
            ],
        ),
        compiler_params=params(16),
        name="panel",
    )(col, got, base, after)


def load_rhs(order_ref, high_ref, low_ref, rhs_ref):
    for m in range(4):
        high, low = high_ref[order_ref[m]], low_ref[order_ref[m]]
        rhs_ref[m * T : (m + 1) * T, :] = high
        rhs_ref[(4 + m) * T : (5 + m) * T, :] = low
        rhs_ref[(8 + m) * T : (9 + m) * T, :] = high


def times_wt(parts, rhs_ref):
    pairs = [split(x) for x in parts]
    high, low = [p[0] for p in pairs], [p[1] for p in pairs]
    return lax.dot_general(
        jnp.concatenate(high + high + low, axis=1), rhs_ref[...], NN, preferred_element_type=F32
    )


def share_kernel(order_ref, x0, x1, x2, x3, high_ref, low_ref, out_ref, rhs_ref):
    load_rhs(order_ref, high_ref, low_ref, rhs_ref)
    out_ref[...] = times_wt([x[...] for x in (x0, x1, x2, x3)], rhs_ref)


def share_solve(order, parts, wt):
    return pl.pallas_call(
        share_kernel,
        out_shape=jax.ShapeDtypeStruct((parts[0].shape[0], 4 * T), F32),
        grid_spec=pltpu.PrefetchScalarGridSpec(
            num_scalar_prefetch=1,
            grid=(),
            in_specs=[VM()] * 6,
            out_specs=VM(),
            scratch_shapes=[pltpu.VMEM((12 * T, 4 * T), BF16)],
        ),
        compiler_params=params(16),
        name="share_solve",
    )(order, *parts, *wt)


def rest_kernel(tile_cols, group, marks_ref, got_ref, base_ref, out_ref, slots, sem):
    @pl.when(pl.program_id(0) == 0)
    def _():
        look = pltpu.make_async_copy(marks_ref.at[:, 2 * T, :], slots, sem)
        look.start()
        look.wait()

    out_ref[...] = base_ref[...]
    first = pl.program_id(0) * group * tile_cols

    def step(n, _):
        slot = slots[n // 2, n % 2].astype(jnp.int32) - first

        @pl.when((slot >= 0) & (slot < group * tile_cols))
        def _():
            at = pl.ds(slot // tile_cols * (T * tile_cols) + slot % tile_cols, T, stride=tile_cols)
            out_ref[at, :] = out_ref[at, :] + got_ref[n // 2, pl.ds(pl.multiple_of(n % 2 * T, T), T), :]

        return 0

    lax.fori_loop(0, 2 * slots.shape[0], step, 0, unroll=4)


def rest(got, base, tile_rows, tile_cols):
    group = 3
    size = group * T * tile_cols
    block = pl.BlockSpec((size, T), lambda a: (a, 0))
    return pl.pallas_call(
        functools.partial(rest_kernel, tile_cols, group),
        out_shape=jax.ShapeDtypeStruct(base.shape, F32),
        grid=(tile_rows // group,),
        in_specs=[ANY(), pl.BlockSpec(got.shape, lambda a: (0, 0, 0)), block],
        out_specs=block,
        scratch_shapes=[pltpu.SMEM((got.shape[0], T), F32), pltpu.SemaphoreType.DMA],
        compiler_params=params(54),
        cost_estimate=pl.CostEstimate(flops=10_000_000_000, bytes_accessed=26_000_000, transcendentals=0),
        name="rest",
    )(got, got, base)


def load_columns(h, k, pieces, rhs_ref):
    for d, ref in enumerate(pieces):
        quarter = (k ^ d) * 32 + h * T
        for q in range(ref.shape[0] // 32):
            high, low = split(ref[32 * q : 32 * q + 32, :])
            at = pl.ds(pl.multiple_of(q * 2 * T + quarter, 32), 32)
            rhs_ref[at, 0:512] = high
            rhs_ref[at, 512:1024] = low


def update_kernel(
    tile_cols, group, info_ref, s0, s1, s2, s3, t0, t1, t2, t3, x0, x1, x2, x3, high_ref, low_ref, base_ref, out_ref, wt_ref, rhs_ref
):
    my_col, my_row = info_ref[4], info_ref[5]
    h, k = my_row // 4, my_row % 4

    @pl.when(pl.program_id(0) == 0)
    def _():
        load_rhs(info_ref, high_ref, low_ref, wt_ref)
        load_columns(h, k, (s0, s1, s2, s3), rhs_ref)
        load_columns(1 - h, k, (t0, t1, t2, t3), rhs_ref)

    panel_rows = times_wt([x[...] for x in (x0, x1, x2, x3)], wt_ref)
    own = panel_rows[:, 0:T]
    for j in range(1, 4):
        own = jnp.where(my_col == j, panel_rows[:, j * T : (j + 1) * T], own)
    row = lax.broadcasted_iota(jnp.int32, panel_rows.shape, 0)
    leading = (pl.program_id(0) == 0) & (my_row < 4)
    high, low = split(jnp.where((row < T) & leading, 0.0, panel_rows))
    lhs = jnp.concatenate([high, high, low], axis=1)
    for q in range(0, tile_cols, 2):
        rhs = rhs_ref[q * T : (q + 2) * T, :]
        rhs = jnp.concatenate([rhs, rhs[:, 0:512]], axis=1)
        u = lax.dot_general(lhs, rhs, NT, preferred_element_type=F32)
        for a in range(group):
            for b in (q, q + 1):
                at = pl.ds(a * T * tile_cols + b, T, stride=tile_cols)
                if b == 0:
                    out_ref[at, :] = own[a * T : (a + 1) * T, :]
                else:
                    out_ref[at, :] = base_ref[at, :] - u[a * T : (a + 1) * T, (b - q) * T : (b - q + 1) * T]


def update(info, pieces, parts, wt, base, tile_rows, tile_cols):
    group = 3
    size = group * T * tile_cols
    block = pl.BlockSpec((size, T), lambda a, *_: (a, 0))
    return pl.pallas_call(
        functools.partial(update_kernel, tile_cols, group),
        out_shape=jax.ShapeDtypeStruct(base.shape, F32),
        grid_spec=pltpu.PrefetchScalarGridSpec(
            num_scalar_prefetch=1,
            grid=(tile_rows // group,),
            in_specs=[pl.BlockSpec(x.shape, lambda a, *_: (0, 0)) for x in pieces]
            + [pl.BlockSpec((group * T, T), lambda a, *_: (a, 0))] * 4
            + [pl.BlockSpec(x.shape, lambda a, *_: (0, 0, 0)) for x in wt]
            + [block],
            out_specs=block,
            scratch_shapes=[pltpu.VMEM((12 * T, 4 * T), BF16), pltpu.VMEM((tile_cols * T, 8 * T), BF16)],
        ),
        compiler_params=params(42),
        name="update",
    )(info, *pieces, *parts, *wt, base)


def local(front, child_updates, child_owner, child_rows, child_cols, child_slot):
    my_row = lax.axis_index("row")
    my_col = lax.axis_index("col")
    tile_rows, tile_cols = front.shape[1], front.shape[4]
    slot_total = tile_rows * tile_cols
    flat = front.reshape(tile_rows * T * tile_cols, T)

    send = route(child_owner[0, :, 0], child_slot[0], child_updates[0], child_rows[0], child_cols[0], 32, slot_total, tile_cols)

    tile = front[0, 0, 0, :, 0, 0, :].reshape(1, 4, 1, T // 4, T)
    quarters = jnp.broadcast_to(tile, (2, 4, 4, T // 4, T)).reshape(32, T // 4, T)
    mine = lax.all_to_all(quarters, ("row", "col"), split_axis=0, concat_axis=0, tiled=True)[:16]
    mine, send = lax.optimization_barrier((mine, send))
    lead = [mine] + [lax.ppermute(mine, "row", [(r, r ^ d) for r in range(8)]) for d in (1, 2, 3)]
    got = lax.all_to_all(send, ("row", "col"), split_axis=0, concat_axis=0, tiled=True)
    wt = leading_inverse((my_row % 4).reshape(1), lead)
    base_panel = lax.optimization_barrier((front, lead[1]))[0][0, :, 0, :, 0, 0, :].reshape(tile_rows * T, T)

    columns, *pieces = panel(my_col.reshape(1), got, base_panel, wt[1])

    parts = []
    for m in range(4):
        moves = [
            ((4 * h + c) * 4 + j, (4 * h + (j + m) % 4) * 4 + c) for h in range(2) for c in range(4) for j in range(4)
        ]
        parts.append(lax.ppermute(pieces[m], ("row", "col"), moves))
    order = (my_row - jnp.arange(4, dtype=jnp.int32)) % 4
    first_core = my_row % 2 == 0
    columns, parts[0] = lax.optimization_barrier((columns, parts[0]))
    from_left = lax.ppermute(columns, "col", [(c, (c + 1) % 4) for c in range(4)])
    from_right = lax.ppermute(columns, "col", [(c, (c - 1) % 4) for c in range(4)])
    far = lax.ppermute(
        jnp.where(first_core, from_left, from_right),
        ("row", "col"),
        [(r * 4 + c, r * 4 + (c + 1 - 2 * (r % 2)) % 4) for r in range(8) for c in range(4)],
    )

    share = share_solve(order, parts, wt)
    got, share = lax.optimization_barrier((got, share))

    def swap(x, bits):
        return lax.ppermute(x, "row", [(r, r ^ bits) for r in range(8)])

    near, far_side = swap(share, 2), swap(share, 6)
    beside = swap(share, 1)
    base = rest(got, flat, tile_rows, tile_cols)
    near, far_side, base = lax.optimization_barrier((near, far_side, base))
    opposite = lax.ppermute(
        jnp.where(first_core, far_side, near), "row", [(r, r ^ (2 if r % 2 == 0 else 6)) for r in range(8)]
    )
    near_beside, far_beside, opposite_beside = swap(near, 1), swap(far_side, 1), swap(opposite, 1)

    info = jnp.concatenate([(my_col + jnp.array([0, -1, 1, 2], jnp.int32)) % 4, jnp.stack([my_col, my_row])])
    shares = (share, beside, near, near_beside, opposite, opposite_beside, far_side, far_beside)
    result = update(info, shares, (columns, from_left, from_right, far), wt, base, tile_rows, tile_cols)
    return result.reshape(front.shape)


def solution(mesh):
    in_specs = (
        P("front", None, "row", None, None, "col", None),
        P("front", ("row", "col"), None, None),
        P("front", ("row", "col"), None),
        P("front", ("row", "col"), None),
        P("front", ("row", "col"), None),
        P("front", ("row", "col")),
    )
    out_specs = P("front", None, "row", None, None, "col", None)
    return jax.shard_map(local, mesh=mesh, in_specs=in_specs, out_specs=out_specs, check_vma=False)
```

```python
import functools

import jax
import jax.numpy as jnp
from jax import lax
from jax.experimental import pallas as pl
from jax.experimental.pallas import tpu as pltpu
from jax.sharding import PartitionSpec as P

T = 128
F32 = jnp.float32
BF16 = jnp.bfloat16
HIGHEST = lax.Precision.HIGHEST
NT = (((1,), (1,)), ((), ()))
NN = (((1,), (0,)), ((), ()))
VM = functools.partial(pl.BlockSpec, memory_space=pltpu.VMEM)
ANY = functools.partial(pl.BlockSpec, memory_space=pl.ANY)


def params(mebibytes=60):
    return pltpu.CompilerParams(vmem_limit_bytes=mebibytes * 1024 * 1024)


def split(x):
    high = x.astype(BF16)
    low = (x - high.astype(F32)).astype(BF16)
    return high, low


def placed_block(block, rows, cols):
    inner = lax.broadcasted_iota(jnp.int32, (T, T), 0)
    row_hot = jnp.where(inner == rows, 1.0, 0.0).astype(BF16)
    col_hot = jnp.where(inner == cols, 1.0, 0.0).astype(BF16)
    high, low = split(block)
    x = lax.dot_general(
        jnp.concatenate([row_hot, row_hot], axis=1), jnp.concatenate([high, low], axis=0), NN, preferred_element_type=F32
    )
    high, low = split(x)
    return lax.dot_general(
        jnp.concatenate([high, low], axis=1), jnp.concatenate([col_hot, col_hot], axis=1), NT, preferred_element_type=F32
    )


def route_kernel(group, slot_total, tile_cols, owner_ref, slot_ref, blocks_ref, rows_ref, cols_ref, send_ref, meta, held, count, sem):
    owners = meta.shape[0]
    blocks = held.shape[0]
    step = pl.program_id(0)

    def at(g, o, k):
        return pltpu.make_async_copy(
            held.at[g], send_ref.at[o, pl.ds(pl.multiple_of(k * T, T), T), :], sem.at[g]
        )

    @pl.when(step == 0)
    def _():
        meta[...] = jnp.full(meta.shape, float(slot_total), F32)

        def clear(o, _):
            count[o] = 0
            return 0

        lax.fori_loop(0, owners, clear, 0)

    for q in range(group):
        g = step * group + q
        held[g] = placed_block(blocks_ref[q], rows_ref[pl.ds(g, 1), :], cols_ref[pl.ds(g, 1), :])
    for q in range(group):
        g = step * group + q
        o = owner_ref[g]
        k = jnp.minimum(count[o], 1)
        count[o] = k + 1
        slot = slot_ref[g]
        panel_row = jnp.where(lax.rem(slot, tile_cols) == 0, lax.div(slot, tile_cols), slot_total)
        lane = lax.broadcasted_iota(jnp.int32, (1, T), 1)
        marks = jnp.where(lane == k, slot, panel_row).astype(F32)
        meta[o, 0:1, :] = jnp.where((lane == k) | (lane == k + 2), marks, meta[o, 0:1, :])
        at(g, o, k).start()

    @pl.when(step == pl.num_programs(0) - 1)
    def _():
        tail = pltpu.make_async_copy(meta, send_ref.at[:, pl.ds(2 * T, 8), :], sem.at[blocks])
        tail.start()

        def finish(g, _):
            at(g, 0, 0).wait()
            return 0

        lax.fori_loop(0, blocks, finish, 0)
        tail.wait()


def route(owner, slot, blocks, rows, cols, owners, slot_total, tile_cols):
    count = blocks.shape[0]
    group = 4
    whole = pl.BlockSpec((count, T), lambda i, *_: (0, 0))
    return pl.pallas_call(
        functools.partial(route_kernel, group, slot_total, tile_cols),
        out_shape=jax.ShapeDtypeStruct((owners, 2 * T + 8, T), F32),
        grid_spec=pltpu.PrefetchScalarGridSpec(
            num_scalar_prefetch=2,
            grid=(count // group,),
            in_specs=[pl.BlockSpec((group, T, T), lambda i, *_: (i, 0, 0)), whole, whole],
            out_specs=ANY(),
            scratch_shapes=[
                pltpu.VMEM((owners, 8, T), F32),
                pltpu.VMEM((count, T, T), F32),
                pltpu.SMEM((owners,), jnp.int32),
                pltpu.SemaphoreType.DMA((count + 1,)),
            ],
        ),
        compiler_params=params(),
        name="route",
    )(owner, slot, blocks, rows, cols)


def sub_row(x, k):
    return jnp.broadcast_to(x[k : k + 1, :], (8, T))


def lane_col(x, k):
    return jnp.broadcast_to(x[:, k : k + 1], (8, T))


def tree_sum(x):
    while len(x) > 1:
        x = [x[i] + x[i + 1] for i in range(0, len(x), 2)]
    return x[0]


def inverse_factor(s, out_ref):
    groups = T // 8
    lane = lax.broadcasted_iota(jnp.int32, (8, T), 1)
    sub = lax.broadcasted_iota(jnp.int32, (8, T), 0)
    m = [s[8 * g : 8 * g + 8, :] for g in range(groups)]
    e = [jnp.where(lane == sub + 8 * g, 1.0, 0.0).astype(F32) for g in range(groups)]
    for p in range(groups):
        v = [sub_row(m[p], k) for k in range(8)]
        x = [sub_row(e[p], k) for k in range(8)]
        column = [lane_col(m[p], 8 * p + c) for c in range(8)]
        d = [[sub_row(column[c], r) if c <= r else None for c in range(8)] for r in range(8)]
        below = {g: [lane_col(m[g], 8 * p + c) for c in range(8)] for g in range(p + 1, groups)}
        inv = [None] * 8
        low = [[None] * 8 for _ in range(8)]
        for k in range(8):
            inv[k] = 1.0 / d[k][k]
            for r in range(k + 1, 8):
                low[r][k] = d[r][k] * inv[k]
            for r in range(k + 1, 8):
                for c in range(k + 1, r + 1):
                    d[r][c] = d[r][c] - low[r][k] * d[c][k]
                v[r] = v[r] - low[r][k] * v[k]
                x[r] = x[r] - low[r][k] * x[k]
        for k in range(8):
            out_ref[8 * p + k : 8 * p + k + 1, :] = (x[k] * lax.sqrt(inv[k]))[0:1, :]
        if p == groups - 1:
            break
        v = [v[k] * inv[k] for k in range(8)]
        x = [x[k] * inv[k] for k in range(8)]
        for k in range(7, 0, -1):
            for j in range(k):
                v[j] = v[j] - low[k][j] * v[k]
                x[j] = x[j] - low[k][j] * x[k]
        for g in range(p + 1, groups):
            m[g] = m[g] - tree_sum([below[g][k] * v[k] for k in range(8)])
            e[g] = e[g] - tree_sum([below[g][k] * x[k] for k in range(8)])


def leading_kernel(quarter_ref, x0, x1, x2, x3, high_ref, low_ref, lead_ref, s_ref, e_ref, w_ref):
    n = 4
    dot = functools.partial(lax.dot_general, precision=HIGHEST, preferred_element_type=F32)


    for d, x in enumerate((x0, x1, x2, x3)):
        lead_ref[:, pl.ds(pl.multiple_of((quarter_ref[0] ^ d) * 32, 32), 32), :] = x[...]

    def tile(i, j):
        return lead_ref[4 * i + j]

    for i in range(n):
        for j in range(i + 1):
            s_ref[i, j] = 0.5 * (tile(i, j) + tile(j, i).T)
    e_ref[...] = jnp.zeros_like(e_ref)

    def step(k, _):
        inverse_factor(s_ref[k, k], w_ref)
        wk = w_ref[...]
        own = dot(wk, e_ref[k], NN)
        column = lax.broadcasted_iota(jnp.int32, (T, n * T), 1)
        spread = jnp.concatenate([wk] * n, axis=1)
        own = jnp.where(column // T == k, spread, own)
        for j in range(n):
            at = pl.ds(pl.multiple_of(k * T, T), T)
            high, low = split(own[:, j * T : (j + 1) * T].T)
            high_ref[j, :, at] = high
            low_ref[j, :, at] = low

        for i in range(1, n):
            @pl.when(i > k)
            def _():
                lik = dot(s_ref[i, k], wk, NT)
                s_ref[i, k] = lik
                e_ref[i] = e_ref[i] - dot(lik, own, NN)
                for j in range(1, i + 1):
                    @pl.when(j > k)
                    def _():
                        s_ref[i, j] = s_ref[i, j] - dot(lik, s_ref[j, k], NT)
        return 0

    lax.fori_loop(0, n, step, 0)


def leading_inverse(quarter, parts):
    return pl.pallas_call(
        leading_kernel,
        out_shape=(jax.ShapeDtypeStruct((4, T, 4 * T), BF16),) * 2,
        grid_spec=pltpu.PrefetchScalarGridSpec(
            num_scalar_prefetch=1,
            grid=(),
            in_specs=[VM()] * 4,
            out_specs=(VM(), VM()),
            scratch_shapes=[
                pltpu.VMEM((16, T, T), F32),
                pltpu.VMEM((4, 4, T, T), F32),
                pltpu.VMEM((4, T, 4 * T), F32),
                pltpu.VMEM((T, T), F32),
            ],
        ),
        compiler_params=params(16),
        cost_estimate=pl.CostEstimate(flops=60_000_000_000, bytes_accessed=2_000_000, transcendentals=0),
        name="leading_inverse",
    )(quarter, *parts)


def panel_kernel(col_ref, got_ref, base_ref, after_ref, out_ref, p0, p1, p2, p3, held, places, sem):
    total = held.shape[0]
    tile_rows = out_ref.shape[0] // T
    look = pltpu.make_async_copy(got_ref.at[:, 2 * T, :], places, sem.at[total])
    look.start()
    out_ref[...] = base_ref[...]
    look.wait()

    def tile_row(n):
        return places[n // 2, n % 2 + 2]

    def wanted(n):
        return tile_row(n) < tile_rows

    def copy(n):
        block = got_ref.at[n // 2, pl.ds(pl.multiple_of(n % 2 * T, T), T), :]
        return pltpu.make_async_copy(block, held.at[n], sem.at[n])

    def fetch(n, _):
        @pl.when(wanted(n))
        def _():
            copy(n).start()

        return 0

    lax.fori_loop(0, total, fetch, 0, unroll=8)

    def add(n, _):
        @pl.when(wanted(n))
        def _():
            copy(n).wait()
            a = pl.ds(pl.multiple_of(tile_row(n).astype(jnp.int32) * T, T), T)
            out_ref[a, :] = out_ref[a, :] + held[n]

        return 0

    lax.fori_loop(0, total, add, 0, unroll=8)
    quarter = T // 4
    for m, piece in enumerate((p0, p1, p2, p3)):
        first = lax.rem(col_ref[0] + m, 4) * quarter
        for a in range(out_ref.shape[0] // T):
            piece[a * quarter : (a + 1) * quarter, :] = out_ref[pl.ds(pl.multiple_of(a * T + first, quarter), quarter), :]


def panel(col, got, base, after):
    rows = base.shape[0]
    total = 2 * got.shape[0]
    return pl.pallas_call(
        panel_kernel,
        out_shape=(jax.ShapeDtypeStruct((rows, T), F32),) + (jax.ShapeDtypeStruct((rows // 4, T), F32),) * 4,
        grid_spec=pltpu.PrefetchScalarGridSpec(
            num_scalar_prefetch=1,
            grid=(),
            in_specs=[ANY(), VM(), ANY()],
            out_specs=(VM(),) * 5,
            scratch_shapes=[
                pltpu.VMEM((total, T, T), F32),
                pltpu.SMEM((total // 2, T), F32),
                pltpu.SemaphoreType.DMA((total + 1,)),
            ],
        ),
        compiler_params=params(16),
        name="panel",
    )(col, got, base, after)


def load_rhs(order_ref, high_ref, low_ref, rhs_ref):
    for m in range(4):
        high, low = high_ref[order_ref[m]], low_ref[order_ref[m]]
        rhs_ref[m * T : (m + 1) * T, :] = high
        rhs_ref[(4 + m) * T : (5 + m) * T, :] = low
        rhs_ref[(8 + m) * T : (9 + m) * T, :] = high


def times_wt(parts, rhs_ref):
    pairs = [split(x) for x in parts]
    high, low = [p[0] for p in pairs], [p[1] for p in pairs]
    return lax.dot_general(
        jnp.concatenate(high + high + low, axis=1), rhs_ref[...], NN, preferred_element_type=F32
    )


def share_kernel(order_ref, x0, x1, x2, x3, high_ref, low_ref, out_ref, rhs_ref):
    load_rhs(order_ref, high_ref, low_ref, rhs_ref)
    out_ref[...] = times_wt([x[...] for x in (x0, x1, x2, x3)], rhs_ref)


def share_solve(order, parts, wt):
    return pl.pallas_call(
        share_kernel,
        out_shape=jax.ShapeDtypeStruct((parts[0].shape[0], 4 * T), F32),
        grid_spec=pltpu.PrefetchScalarGridSpec(
            num_scalar_prefetch=1,
            grid=(),
            in_specs=[VM()] * 6,
            out_specs=VM(),
            scratch_shapes=[pltpu.VMEM((12 * T, 4 * T), BF16)],
        ),
        compiler_params=params(16),
        name="share_solve",
    )(order, *parts, *wt)


def rest_kernel(tile_cols, group, marks_ref, got_ref, base_ref, out_ref, marks, slots, sem):
    @pl.when(pl.program_id(0) == 0)
    def _():
        look = pltpu.make_async_copy(marks_ref.at[:, 2 * T, :], marks, sem)
        look.start()
        look.wait()

        def convert(n, _):
            slots[n] = marks[n // 2, n % 2].astype(jnp.int32)
            return 0

        lax.fori_loop(0, slots.shape[0], convert, 0, unroll=8)

    out_ref[...] = base_ref[...]
    first = pl.program_id(0) * group * tile_cols

    def step(n, _):
        slot = slots[n] - first

        @pl.when((slot >= 0) & (slot < group * tile_cols))
        def _():
            at = pl.ds(slot // tile_cols * (T * tile_cols) + slot % tile_cols, T, stride=tile_cols)
            out_ref[at, :] = out_ref[at, :] + got_ref[n // 2, pl.ds(pl.multiple_of(n % 2 * T, T), T), :]

        return 0

    lax.fori_loop(0, slots.shape[0], step, 0, unroll=4)


def rest(got, base, tile_rows, tile_cols):
    group = 3
    size = group * T * tile_cols
    block = pl.BlockSpec((size, T), lambda a: (a, 0))
    return pl.pallas_call(
        functools.partial(rest_kernel, tile_cols, group),
        out_shape=jax.ShapeDtypeStruct(base.shape, F32),
        grid=(tile_rows // group,),
        in_specs=[ANY(), pl.BlockSpec(got.shape, lambda a: (0, 0, 0), pipeline_mode=pl.Buffered(1)), block],
        out_specs=block,
        scratch_shapes=[
            pltpu.SMEM((got.shape[0], T), F32),
            pltpu.SMEM((2 * got.shape[0],), jnp.int32),
            pltpu.SemaphoreType.DMA,
        ],
        compiler_params=params(32),
        cost_estimate=pl.CostEstimate(flops=10_000_000_000, bytes_accessed=26_000_000, transcendentals=0),
        name="rest",
    )(got, got, base)


def load_columns(h, k, pieces, rhs_ref):
    for d, ref in enumerate(pieces):
        quarter = (k ^ d) * 32 + h * T
        for q in range(ref.shape[0] // 32):
            high, low = split(ref[32 * q : 32 * q + 32, :])
            at = pl.ds(pl.multiple_of(q * 2 * T + quarter, 32), 32)
            rhs_ref[at, 0:512] = high
            rhs_ref[at, 512:1024] = low


def update_kernel(
    tile_cols, group, info_ref, s0, s1, s2, s3, t0, t1, t2, t3, x0, x1, x2, x3, high_ref, low_ref, base_ref, out_ref, wt_ref, rhs_ref
):
    my_col, my_row = info_ref[4], info_ref[5]
    h, k = my_row // 4, my_row % 4

    @pl.when(pl.program_id(0) == 0)
    def _():
        load_rhs(info_ref, high_ref, low_ref, wt_ref)
        load_columns(h, k, (s0, s1, s2, s3), rhs_ref)
        load_columns(1 - h, k, (t0, t1, t2, t3), rhs_ref)

    panel_rows = times_wt([x[...] for x in (x0, x1, x2, x3)], wt_ref)
    own = panel_rows[:, 0:T]
    for j in range(1, 4):
        own = jnp.where(my_col == j, panel_rows[:, j * T : (j + 1) * T], own)
    row = lax.broadcasted_iota(jnp.int32, panel_rows.shape, 0)
    leading = (pl.program_id(0) == 0) & (my_row < 4)
    high, low = split(jnp.where((row < T) & leading, 0.0, panel_rows))
    lhs = jnp.concatenate([high, high, low], axis=1)
    for q in range(0, tile_cols, 2):
        rhs = rhs_ref[q * T : (q + 2) * T, :]
        rhs = jnp.concatenate([rhs, rhs[:, 0:512]], axis=1)
        u = lax.dot_general(lhs, rhs, NT, preferred_element_type=F32)
        for a in range(group):
            for b in (q, q + 1):
                at = pl.ds(a * T * tile_cols + b, T, stride=tile_cols)
                if b == 0:
                    out_ref[at, :] = own[a * T : (a + 1) * T, :]
                else:
                    out_ref[at, :] = base_ref[at, :] - u[a * T : (a + 1) * T, (b - q) * T : (b - q + 1) * T]


def update(info, pieces, parts, wt, base, tile_rows, tile_cols):
    group = 3
    size = group * T * tile_cols
    block = pl.BlockSpec((size, T), lambda a, *_: (a, 0))
    return pl.pallas_call(
        functools.partial(update_kernel, tile_cols, group),
        out_shape=jax.ShapeDtypeStruct(base.shape, F32),
        grid_spec=pltpu.PrefetchScalarGridSpec(
            num_scalar_prefetch=1,
            grid=(tile_rows // group,),
            in_specs=[pl.BlockSpec(x.shape, lambda a, *_: (0, 0), pipeline_mode=pl.Buffered(1)) for x in pieces]
            + [pl.BlockSpec((group * T, T), lambda a, *_: (a, 0))] * 4
            + [pl.BlockSpec(x.shape, lambda a, *_: (0, 0, 0), pipeline_mode=pl.Buffered(1)) for x in wt]
            + [block],
            out_specs=block,
            scratch_shapes=[pltpu.VMEM((12 * T, 4 * T), BF16), pltpu.VMEM((tile_cols * T, 8 * T), BF16)],
        ),
        compiler_params=params(30),
        name="update",
    )(info, *pieces, *parts, *wt, base)


def local(front, child_updates, child_owner, child_rows, child_cols, child_slot):
    my_row = lax.axis_index("row")
    my_col = lax.axis_index("col")
    tile_rows, tile_cols = front.shape[1], front.shape[4]
    slot_total = tile_rows * tile_cols
    flat = front.reshape(tile_rows * T * tile_cols, T)

    send = route(child_owner[0, :, 0], child_slot[0], child_updates[0], child_rows[0], child_cols[0], 32, slot_total, tile_cols)

    tile = front[0, 0, 0, :, 0, 0, :].reshape(1, 4, 1, T // 4, T)
    quarters = jnp.broadcast_to(tile, (2, 4, 4, T // 4, T)).reshape(32, T // 4, T)
    mine = lax.all_to_all(quarters, ("row", "col"), split_axis=0, concat_axis=0, tiled=True)[:16]
    mine, send = lax.optimization_barrier((mine, send))
    lead = [mine] + [lax.ppermute(mine, "row", [(r, r ^ d) for r in range(8)]) for d in (1, 2, 3)]
    got = lax.all_to_all(send, ("row", "col"), split_axis=0, concat_axis=0, tiled=True)
    wt = leading_inverse((my_row % 4).reshape(1), lead)
    base_panel = lax.optimization_barrier((front, lead[1]))[0][0, :, 0, :, 0, 0, :].reshape(tile_rows * T, T)

    columns, *pieces = panel(my_col.reshape(1), got, base_panel, wt[1])

    parts = []
    for m in range(4):
        moves = [
            ((4 * h + c) * 4 + j, (4 * h + (j + m) % 4) * 4 + c) for h in range(2) for c in range(4) for j in range(4)
        ]
        parts.append(lax.ppermute(pieces[m], ("row", "col"), moves))
    order = (my_row - jnp.arange(4, dtype=jnp.int32)) % 4
    first_core = my_row % 2 == 0
    columns, parts[0] = lax.optimization_barrier((columns, parts[0]))
    from_left = lax.ppermute(columns, "col", [(c, (c + 1) % 4) for c in range(4)])
    from_right = lax.ppermute(columns, "col", [(c, (c - 1) % 4) for c in range(4)])
    far = lax.ppermute(
        jnp.where(first_core, from_left, from_right),
        ("row", "col"),
        [(r * 4 + c, r * 4 + (c + 1 - 2 * (r % 2)) % 4) for r in range(8) for c in range(4)],
    )

    share = share_solve(order, parts, wt)
    got, share = lax.optimization_barrier((got, share))

    def swap(x, bits):
        return lax.ppermute(x, "row", [(r, r ^ bits) for r in range(8)])

    near, far_side = swap(share, 2), swap(share, 6)
    beside = swap(share, 1)
    base = rest(got, flat, tile_rows, tile_cols)
    near, far_side, base = lax.optimization_barrier((near, far_side, base))
    opposite = lax.ppermute(
        jnp.where(first_core, far_side, near), "row", [(r, r ^ (2 if r % 2 == 0 else 6)) for r in range(8)]
    )
    near_beside, far_beside, opposite_beside = swap(near, 1), swap(far_side, 1), swap(opposite, 1)

    info = jnp.concatenate([(my_col + jnp.array([0, -1, 1, 2], jnp.int32)) % 4, jnp.stack([my_col, my_row])])
    shares = (share, beside, near, near_beside, opposite, opposite_beside, far_side, far_beside)
    result = update(info, shares, (columns, from_left, from_right, far), wt, base, tile_rows, tile_cols)
    return result.reshape(front.shape)


def solution(mesh):
    in_specs = (
        P("front", None, "row", None, None, "col", None),
        P("front", ("row", "col"), None, None),
        P("front", ("row", "col"), None),
        P("front", ("row", "col"), None),
        P("front", ("row", "col"), None),
        P("front", ("row", "col")),
    )
    out_specs = P("front", None, "row", None, None, "col", None)
    return jax.shard_map(local, mesh=mesh, in_specs=in_specs, out_specs=out_specs, check_vma=False)
```

```python
import functools

import jax
import jax.numpy as jnp
from jax import lax
from jax.experimental import pallas as pl
from jax.experimental.pallas import tpu as pltpu
from jax.sharding import PartitionSpec as P

T = 128
F32 = jnp.float32
BF16 = jnp.bfloat16
HIGHEST = lax.Precision.HIGHEST
NT = (((1,), (1,)), ((), ()))
NN = (((1,), (0,)), ((), ()))
VM = functools.partial(pl.BlockSpec, memory_space=pltpu.VMEM)
ANY = functools.partial(pl.BlockSpec, memory_space=pl.ANY)


def params(mebibytes=60):
    return pltpu.CompilerParams(vmem_limit_bytes=mebibytes * 1024 * 1024)


def split(x):
    high = x.astype(BF16)
    low = (x - high.astype(F32)).astype(BF16)
    return high, low


def placed_block(block, rows, cols):
    inner = lax.broadcasted_iota(jnp.int32, (T, T), 0)
    row_hot = jnp.where(inner == rows, 1.0, 0.0).astype(BF16)
    col_hot = jnp.where(inner == cols, 1.0, 0.0).astype(BF16)
    high, low = split(block)
    x = lax.dot_general(
        jnp.concatenate([row_hot, row_hot], axis=1), jnp.concatenate([high, low], axis=0), NN, preferred_element_type=F32
    )
    high, low = split(x)
    return lax.dot_general(
        jnp.concatenate([high, low], axis=1), jnp.concatenate([col_hot, col_hot], axis=1), NT, preferred_element_type=F32
    )


def route_kernel(group, slot_total, tile_cols, owner_ref, slot_ref, blocks_ref, rows_ref, cols_ref, send_ref, meta, held, count, sem):
    owners = meta.shape[0]
    blocks = held.shape[0]
    step = pl.program_id(0)

    def at(g, o, k):
        return pltpu.make_async_copy(
            held.at[g], send_ref.at[o, pl.ds(pl.multiple_of(k * T, T), T), :], sem.at[g]
        )

    @pl.when(step == 0)
    def _():
        meta[...] = jnp.full(meta.shape, float(slot_total), F32)

        def clear(o, _):
            count[o] = 0
            return 0

        lax.fori_loop(0, owners, clear, 0)

    for q in range(group):
        g = step * group + q
        held[g] = placed_block(blocks_ref[q], rows_ref[pl.ds(g, 1), :], cols_ref[pl.ds(g, 1), :])
    for q in range(group):
        g = step * group + q
        o = owner_ref[g]
        k = jnp.minimum(count[o], 1)
        count[o] = k + 1
        slot = slot_ref[g]
        panel_row = jnp.where(lax.rem(slot, tile_cols) == 0, lax.div(slot, tile_cols), slot_total)
        lane = lax.broadcasted_iota(jnp.int32, (1, T), 1)
        marks = jnp.where(lane == k, slot, panel_row).astype(F32)
        meta[o, 0:1, :] = jnp.where((lane == k) | (lane == k + 2), marks, meta[o, 0:1, :])
        at(g, o, k).start()

    @pl.when(step == pl.num_programs(0) - 1)
    def _():
        tail = pltpu.make_async_copy(meta, send_ref.at[:, pl.ds(2 * T, 8), :], sem.at[blocks])
        tail.start()

        def finish(g, _):
            at(g, 0, 0).wait()
            return 0

        lax.fori_loop(0, blocks, finish, 0)
        tail.wait()


def route(owner, slot, blocks, rows, cols, owners, slot_total, tile_cols):
    count = blocks.shape[0]
    group = 4
    whole = pl.BlockSpec((count, T), lambda i, *_: (0, 0))
    return pl.pallas_call(
        functools.partial(route_kernel, group, slot_total, tile_cols),
        out_shape=jax.ShapeDtypeStruct((owners, 2 * T + 8, T), F32),
        grid_spec=pltpu.PrefetchScalarGridSpec(
            num_scalar_prefetch=2,
            grid=(count // group,),
            in_specs=[pl.BlockSpec((group, T, T), lambda i, *_: (i, 0, 0)), whole, whole],
            out_specs=ANY(),
            scratch_shapes=[
                pltpu.VMEM((owners, 8, T), F32),
                pltpu.VMEM((count, T, T), F32),
                pltpu.SMEM((owners,), jnp.int32),
                pltpu.SemaphoreType.DMA((count + 1,)),
            ],
        ),
        compiler_params=params(),
        name="route",
    )(owner, slot, blocks, rows, cols)


def sub_row(x, k):
    return jnp.broadcast_to(x[k : k + 1, :], (8, T))


def lane_col(x, k):
    return jnp.broadcast_to(x[:, k : k + 1], (8, T))


def tree_sum(x):
    while len(x) > 1:
        x = [x[i] + x[i + 1] for i in range(0, len(x), 2)]
    return x[0]


def inverse_factor(s, out_ref):
    groups = T // 8
    lane = lax.broadcasted_iota(jnp.int32, (8, T), 1)
    sub = lax.broadcasted_iota(jnp.int32, (8, T), 0)
    m = [s[8 * g : 8 * g + 8, :] for g in range(groups)]
    e = [jnp.where(lane == sub + 8 * g, 1.0, 0.0).astype(F32) for g in range(groups)]
    for p in range(groups):
        v = [sub_row(m[p], k) for k in range(8)]
        x = [sub_row(e[p], k) for k in range(8)]
        column = [lane_col(m[p], 8 * p + c) for c in range(8)]
        d = [[sub_row(column[c], r) if c <= r else None for c in range(8)] for r in range(8)]
        below = {g: [lane_col(m[g], 8 * p + c) for c in range(8)] for g in range(p + 1, groups)}
        inv = [None] * 8
        low = [[None] * 8 for _ in range(8)]
        for k in range(8):
            inv[k] = 1.0 / d[k][k]
            for r in range(k + 1, 8):
                low[r][k] = d[r][k] * inv[k]
            for r in range(k + 1, 8):
                for c in range(k + 1, r + 1):
                    d[r][c] = d[r][c] - low[r][k] * d[c][k]
                v[r] = v[r] - low[r][k] * v[k]
                x[r] = x[r] - low[r][k] * x[k]
        for k in range(8):
            out_ref[8 * p + k : 8 * p + k + 1, :] = (x[k] * lax.sqrt(inv[k]))[0:1, :]
        if p == groups - 1:
            break
        v = [v[k] * inv[k] for k in range(8)]
        x = [x[k] * inv[k] for k in range(8)]
        for k in range(7, 0, -1):
            for j in range(k):
                v[j] = v[j] - low[k][j] * v[k]
                x[j] = x[j] - low[k][j] * x[k]
        for g in range(p + 1, groups):
            m[g] = m[g] - tree_sum([below[g][k] * v[k] for k in range(8)])
            e[g] = e[g] - tree_sum([below[g][k] * x[k] for k in range(8)])


def leading_kernel(offsets, me_ref, halves_ref, high_ref, low_ref, lead_ref, s_ref, e_ref, w_ref):
    n = 4
    dot = functools.partial(lax.dot_general, precision=HIGHEST, preferred_element_type=F32)


    for i, offset in enumerate(offsets):
        source = me_ref[0] ^ offset
        at = pl.ds(pl.multiple_of(source // 16 * (T // 2), T // 2), T // 2)
        lead_ref[source % 16, at, :] = halves_ref[i]

    def tile(i, j):
        return lead_ref[4 * i + j]

    for i in range(n):
        for j in range(i + 1):
            s_ref[i, j] = 0.5 * (tile(i, j) + tile(j, i).T)
    e_ref[...] = jnp.zeros_like(e_ref)

    def step(k, _):
        inverse_factor(s_ref[k, k], w_ref)
        wk = w_ref[...]
        own = dot(wk, e_ref[k], NN)
        column = lax.broadcasted_iota(jnp.int32, (T, n * T), 1)
        spread = jnp.concatenate([wk] * n, axis=1)
        own = jnp.where(column // T == k, spread, own)
        for j in range(n):
            at = pl.ds(pl.multiple_of(k * T, T), T)
            high, low = split(own[:, j * T : (j + 1) * T].T)
            high_ref[j, :, at] = high
            low_ref[j, :, at] = low

        for i in range(1, n):
            @pl.when(i > k)
            def _():
                lik = dot(s_ref[i, k], wk, NT)
                s_ref[i, k] = lik
                e_ref[i] = e_ref[i] - dot(lik, own, NN)
                for j in range(1, i + 1):
                    @pl.when(j > k)
                    def _():
                        s_ref[i, j] = s_ref[i, j] - dot(lik, s_ref[j, k], NT)
        return 0

    lax.fori_loop(0, n, step, 0)


def leading_inverse(me, halves, offsets):
    return pl.pallas_call(
        functools.partial(leading_kernel, offsets),
        out_shape=(jax.ShapeDtypeStruct((4, T, 4 * T), BF16),) * 2,
        grid_spec=pltpu.PrefetchScalarGridSpec(
            num_scalar_prefetch=1,
            grid=(),
            in_specs=[VM()],
            out_specs=(VM(), VM()),
            scratch_shapes=[
                pltpu.VMEM((16, T, T), F32),
                pltpu.VMEM((4, 4, T, T), F32),
                pltpu.VMEM((4, T, 4 * T), F32),
                pltpu.VMEM((T, T), F32),
            ],
        ),
        compiler_params=params(16),
        cost_estimate=pl.CostEstimate(flops=1_000_000, bytes_accessed=2_000_000, transcendentals=0),
        name="leading_inverse",
    )(me, halves)


def panel_kernel(col_ref, got_ref, base_ref, after_ref, out_ref, p0, p1, p2, p3, held, places, sem):
    total = held.shape[0]
    tile_rows = out_ref.shape[0] // T
    look = pltpu.make_async_copy(got_ref.at[:, 2 * T, :], places, sem.at[total])
    look.start()
    out_ref[...] = base_ref[...]
    look.wait()

    def tile_row(n):
        return places[n // 2, n % 2 + 2]

    def wanted(n):
        return tile_row(n) < tile_rows

    def copy(n):
        block = got_ref.at[n // 2, pl.ds(pl.multiple_of(n % 2 * T, T), T), :]
        return pltpu.make_async_copy(block, held.at[n], sem.at[n])

    def fetch(n, _):
        @pl.when(wanted(n))
        def _():
            copy(n).start()

        return 0

    lax.fori_loop(0, total, fetch, 0, unroll=8)

    def add(n, _):
        @pl.when(wanted(n))
        def _():
            copy(n).wait()
            a = pl.ds(pl.multiple_of(tile_row(n).astype(jnp.int32) * T, T), T)
            out_ref[a, :] = out_ref[a, :] + held[n]

        return 0

    lax.fori_loop(0, total, add, 0, unroll=8)
    quarter = T // 4
    for m, piece in enumerate((p0, p1, p2, p3)):
        first = lax.rem(col_ref[0] + m, 4) * quarter
        for a in range(out_ref.shape[0] // T):
            piece[a * quarter : (a + 1) * quarter, :] = out_ref[pl.ds(pl.multiple_of(a * T + first, quarter), quarter), :]


def panel(col, got, base, after):
    rows = base.shape[0]
    total = 2 * got.shape[0]
    return pl.pallas_call(
        panel_kernel,
        out_shape=(jax.ShapeDtypeStruct((rows, T), F32),) + (jax.ShapeDtypeStruct((rows // 4, T), F32),) * 4,
        grid_spec=pltpu.PrefetchScalarGridSpec(
            num_scalar_prefetch=1,
            grid=(),
            in_specs=[ANY(), VM(), ANY()],
            out_specs=(VM(),) * 5,
            scratch_shapes=[
                pltpu.VMEM((total, T, T), F32),
                pltpu.SMEM((total // 2, T), F32),
                pltpu.SemaphoreType.DMA((total + 1,)),
            ],
        ),
        compiler_params=params(16),
        name="panel",
    )(col, got, base, after)


def load_rhs(order_ref, high_ref, low_ref, rhs_ref):
    for m in range(4):
        high, low = high_ref[order_ref[m]], low_ref[order_ref[m]]
        rhs_ref[m * T : (m + 1) * T, :] = high
        rhs_ref[(4 + m) * T : (5 + m) * T, :] = low
        rhs_ref[(8 + m) * T : (9 + m) * T, :] = high


def times_wt(parts, rhs_ref):
    pairs = [split(x) for x in parts]
    high, low = [p[0] for p in pairs], [p[1] for p in pairs]
    return lax.dot_general(
        jnp.concatenate(high + high + low, axis=1), rhs_ref[...], NN, preferred_element_type=F32
    )


def share_kernel(order_ref, x0, x1, x2, x3, high_ref, low_ref, out_ref, rhs_ref):
    load_rhs(order_ref, high_ref, low_ref, rhs_ref)
    out_ref[...] = times_wt([x[...] for x in (x0, x1, x2, x3)], rhs_ref)


def share_solve(order, parts, wt):
    return pl.pallas_call(
        share_kernel,
        out_shape=jax.ShapeDtypeStruct((parts[0].shape[0], 4 * T), F32),
        grid_spec=pltpu.PrefetchScalarGridSpec(
            num_scalar_prefetch=1,
            grid=(),
            in_specs=[VM()] * 6,
            out_specs=VM(),
            scratch_shapes=[pltpu.VMEM((12 * T, 4 * T), BF16)],
        ),
        compiler_params=params(16),
        name="share_solve",
    )(order, *parts, *wt)


def rest_kernel(tile_cols, group, marks_ref, got_ref, base_ref, out_ref, marks, slots, sem):
    @pl.when(pl.program_id(0) == 0)
    def _():
        look = pltpu.make_async_copy(marks_ref.at[:, 2 * T, :], marks, sem)
        look.start()
        look.wait()

        def convert(n, _):
            slots[n] = marks[n // 2, n % 2].astype(jnp.int32)
            return 0

        lax.fori_loop(0, slots.shape[0], convert, 0, unroll=8)

    out_ref[...] = base_ref[...]
    first = pl.program_id(0) * group * tile_cols

    def step(n, _):
        slot = slots[n] - first

        @pl.when((slot >= 0) & (slot < group * tile_cols))
        def _():
            at = pl.ds(slot // tile_cols * (T * tile_cols) + slot % tile_cols, T, stride=tile_cols)
            out_ref[at, :] = out_ref[at, :] + got_ref[n // 2, pl.ds(pl.multiple_of(n % 2 * T, T), T), :]

        return 0

    lax.fori_loop(0, slots.shape[0], step, 0, unroll=4)


def rest(got, base, tile_rows, tile_cols):
    group = 3
    size = group * T * tile_cols
    block = pl.BlockSpec((size, T), lambda a: (a, 0))
    return pl.pallas_call(
        functools.partial(rest_kernel, tile_cols, group),
        out_shape=jax.ShapeDtypeStruct(base.shape, F32),
        grid=(tile_rows // group,),
        in_specs=[ANY(), pl.BlockSpec(got.shape, lambda a: (0, 0, 0), pipeline_mode=pl.Buffered(1)), block],
        out_specs=block,
        scratch_shapes=[
            pltpu.SMEM((got.shape[0], T), F32),
            pltpu.SMEM((2 * got.shape[0],), jnp.int32),
            pltpu.SemaphoreType.DMA,
        ],
        compiler_params=params(32),
        cost_estimate=pl.CostEstimate(flops=10_000_000_000, bytes_accessed=26_000_000, transcendentals=0),
        name="rest",
    )(got, got, base)


def load_columns(h, k, pieces, rhs_ref):
    for d, ref in enumerate(pieces):
        quarter = (k ^ d) * 32 + h * T
        for q in range(ref.shape[0] // 32):
            high, low = split(ref[32 * q : 32 * q + 32, :])
            at = pl.ds(pl.multiple_of(q * 2 * T + quarter, 32), 32)
            rhs_ref[at, 0:512] = high
            rhs_ref[at, 512:1024] = low


def update_kernel(
    tile_cols, group, info_ref, s0, s1, s2, s3, t0, t1, t2, t3, x0, x1, x2, x3, high_ref, low_ref, base_ref, out_ref, wt_ref, rhs_ref
):
    my_col, my_row = info_ref[4], info_ref[5]
    h, k = my_row // 4, my_row % 4

    @pl.when(pl.program_id(0) == 0)
    def _():
        load_rhs(info_ref, high_ref, low_ref, wt_ref)
        load_columns(h, k, (s0, s1, s2, s3), rhs_ref)
        load_columns(1 - h, k, (t0, t1, t2, t3), rhs_ref)

    panel_rows = times_wt([x[...] for x in (x0, x1, x2, x3)], wt_ref)
    own = panel_rows[:, 0:T]
    for j in range(1, 4):
        own = jnp.where(my_col == j, panel_rows[:, j * T : (j + 1) * T], own)
    row = lax.broadcasted_iota(jnp.int32, panel_rows.shape, 0)
    leading = (pl.program_id(0) == 0) & (my_row < 4)
    high, low = split(jnp.where((row < T) & leading, 0.0, panel_rows))
    lhs = jnp.concatenate([high, high, low], axis=1)
    for q in range(0, tile_cols, 2):
        rhs = rhs_ref[q * T : (q + 2) * T, :]
        rhs = jnp.concatenate([rhs, rhs[:, 0:512]], axis=1)
        u = lax.dot_general(lhs, rhs, NT, preferred_element_type=F32)
        for a in range(group):
            for b in (q, q + 1):
                at = pl.ds(a * T * tile_cols + b, T, stride=tile_cols)
                if b == 0:
                    out_ref[at, :] = own[a * T : (a + 1) * T, :]
                else:
                    out_ref[at, :] = base_ref[at, :] - u[a * T : (a + 1) * T, (b - q) * T : (b - q + 1) * T]


def update(info, pieces, parts, wt, base, tile_rows, tile_cols):
    group = 3
    size = group * T * tile_cols
    block = pl.BlockSpec((size, T), lambda a, *_: (a, 0))
    return pl.pallas_call(
        functools.partial(update_kernel, tile_cols, group),
        out_shape=jax.ShapeDtypeStruct(base.shape, F32),
        grid_spec=pltpu.PrefetchScalarGridSpec(
            num_scalar_prefetch=1,
            grid=(tile_rows // group,),
            in_specs=[pl.BlockSpec(x.shape, lambda a, *_: (0, 0), pipeline_mode=pl.Buffered(1)) for x in pieces]
            + [pl.BlockSpec((group * T, T), lambda a, *_: (a, 0))] * 4
            + [pl.BlockSpec(x.shape, lambda a, *_: (0, 0, 0), pipeline_mode=pl.Buffered(1)) for x in wt]
            + [block],
            out_specs=block,
            scratch_shapes=[pltpu.VMEM((12 * T, 4 * T), BF16), pltpu.VMEM((tile_cols * T, 8 * T), BF16)],
        ),
        compiler_params=params(30),
        name="update",
    )(info, *pieces, *parts, *wt, base)


def local(front, child_updates, child_owner, child_rows, child_cols, child_slot):
    my_row = lax.axis_index("row")
    my_col = lax.axis_index("col")
    tile_rows, tile_cols = front.shape[1], front.shape[4]
    slot_total = tile_rows * tile_cols
    flat = front.reshape(tile_rows * T * tile_cols, T)

    send = route(child_owner[0, :, 0], child_slot[0], child_updates[0], child_rows[0], child_cols[0], 32, slot_total, tile_cols)

    tile = front[0, 0, 0, :, 0, 0, :]
    lower = lax.ppermute(tile[T // 2 :], "row", [(r, r + 4) for r in range(4)])
    lead = jnp.where(my_row < 4, tile[: T // 2], lower)[None]
    offsets = [0]
    for axis, size, bit, offset in (("row", 8, 4, 16), ("col", 4, 2, 2), ("col", 4, 1, 1), ("row", 8, 2, 8), ("row", 8, 1, 4)):
        lead = jnp.concatenate([lead, lax.ppermute(lead, axis, [(i, i ^ bit) for i in range(size)])], axis=0)
        offsets = offsets + [o ^ offset for o in offsets]
        if offset == 16:
            lead, send = lax.optimization_barrier((lead, send))
    got = lax.all_to_all(send, ("row", "col"), split_axis=0, concat_axis=0, tiled=True)
    wt = leading_inverse((my_row * 4 + my_col).reshape(1), lead, offsets)
    base_panel = lax.optimization_barrier((front, lead))[0][0, :, 0, :, 0, 0, :].reshape(tile_rows * T, T)

    columns, *pieces = panel(my_col.reshape(1), got, base_panel, wt[1])

    parts = []
    for m in range(4):
        moves = [
            ((4 * h + c) * 4 + j, (4 * h + (j + m) % 4) * 4 + c) for h in range(2) for c in range(4) for j in range(4)
        ]
        parts.append(lax.ppermute(pieces[m], ("row", "col"), moves))
    order = (my_row - jnp.arange(4, dtype=jnp.int32)) % 4
    first_core = my_row % 2 == 0
    columns, parts[0] = lax.optimization_barrier((columns, parts[0]))
    from_left = lax.ppermute(columns, "col", [(c, (c + 1) % 4) for c in range(4)])
    from_right = lax.ppermute(columns, "col", [(c, (c - 1) % 4) for c in range(4)])
    far = lax.ppermute(
        jnp.where(first_core, from_left, from_right),
        ("row", "col"),
        [(r * 4 + c, r * 4 + (c + 1 - 2 * (r % 2)) % 4) for r in range(8) for c in range(4)],
    )

    share = share_solve(order, parts, wt)
    got, share = lax.optimization_barrier((got, share))

    def swap(x, bits):
        return lax.ppermute(x, "row", [(r, r ^ bits) for r in range(8)])

    near, far_side = swap(share, 2), swap(share, 6)
    beside = swap(share, 1)
    base = rest(got, flat, tile_rows, tile_cols)
    near, far_side, base = lax.optimization_barrier((near, far_side, base))
    opposite = lax.ppermute(
        jnp.where(first_core, far_side, near), "row", [(r, r ^ (2 if r % 2 == 0 else 6)) for r in range(8)]
    )
    near_beside, far_beside, opposite_beside = swap(near, 1), swap(far_side, 1), swap(opposite, 1)

    info = jnp.concatenate([(my_col + jnp.array([0, -1, 1, 2], jnp.int32)) % 4, jnp.stack([my_col, my_row])])
    shares = (share, beside, near, near_beside, opposite, opposite_beside, far_side, far_beside)
    result = update(info, shares, (columns, from_left, from_right, far), wt, base, tile_rows, tile_cols)
    return result.reshape(front.shape)


def solution(mesh):
    in_specs = (
        P("front", None, "row", None, None, "col", None),
        P("front", ("row", "col"), None, None),
        P("front", ("row", "col"), None),
        P("front", ("row", "col"), None),
        P("front", ("row", "col"), None),
        P("front", ("row", "col")),
    )
    out_specs = P("front", None, "row", None, None, "col", None)
    return jax.shard_map(local, mesh=mesh, in_specs=in_specs, out_specs=out_specs, check_vma=False)
```

```python
import functools

import jax
import jax.numpy as jnp
from jax import lax
from jax.experimental import pallas as pl
from jax.experimental.pallas import tpu as pltpu
from jax.sharding import PartitionSpec as P

T = 128
F32 = jnp.float32
BF16 = jnp.bfloat16
HIGHEST = lax.Precision.HIGHEST
NT = (((1,), (1,)), ((), ()))
NN = (((1,), (0,)), ((), ()))
VM = functools.partial(pl.BlockSpec, memory_space=pltpu.VMEM)
ANY = functools.partial(pl.BlockSpec, memory_space=pl.ANY)


def params(mebibytes=60):
    return pltpu.CompilerParams(vmem_limit_bytes=mebibytes * 1024 * 1024)


def split(x):
    high = x.astype(BF16)
    low = (x - high.astype(F32)).astype(BF16)
    return high, low


def placed_block(block, rows, cols):
    inner = lax.broadcasted_iota(jnp.int32, (T, T), 0)
    row_hot = jnp.where(inner == rows, 1.0, 0.0).astype(BF16)
    col_hot = jnp.where(inner == cols, 1.0, 0.0).astype(BF16)
    high, low = split(block)
    x = lax.dot_general(
        jnp.concatenate([row_hot, row_hot], axis=1), jnp.concatenate([high, low], axis=0), NN, preferred_element_type=F32
    )
    high, low = split(x)
    return lax.dot_general(
        jnp.concatenate([high, low], axis=1), jnp.concatenate([col_hot, col_hot], axis=1), NT, preferred_element_type=F32
    )


def route_kernel(group, slot_total, tile_cols, owner_ref, slot_ref, blocks_ref, rows_ref, cols_ref, send_ref, meta, held, count, sem):
    owners = meta.shape[0]
    blocks = held.shape[0]
    step = pl.program_id(0)

    def at(g, o, k):
        return pltpu.make_async_copy(
            held.at[g], send_ref.at[o, pl.ds(pl.multiple_of(k * T, T), T), :], sem.at[g]
        )

    @pl.when(step == 0)
    def _():
        meta[...] = jnp.full(meta.shape, float(slot_total), F32)

        def clear(o, _):
            count[o] = 0
            return 0

        lax.fori_loop(0, owners, clear, 0)

    for q in range(group):
        g = step * group + q
        held[g] = placed_block(blocks_ref[q], rows_ref[pl.ds(g, 1), :], cols_ref[pl.ds(g, 1), :])
    for q in range(group):
        g = step * group + q
        o = owner_ref[g]
        k = jnp.minimum(count[o], 1)
        count[o] = k + 1
        slot = slot_ref[g]
        panel_row = jnp.where(lax.rem(slot, tile_cols) == 0, lax.div(slot, tile_cols), slot_total)
        lane = lax.broadcasted_iota(jnp.int32, (1, T), 1)
        marks = jnp.where(lane == k, slot, panel_row).astype(F32)
        meta[o, 0:1, :] = jnp.where((lane == k) | (lane == k + 2), marks, meta[o, 0:1, :])
        at(g, o, k).start()

    @pl.when(step == pl.num_programs(0) - 1)
    def _():
        tail = pltpu.make_async_copy(meta, send_ref.at[:, pl.ds(2 * T, 8), :], sem.at[blocks])
        tail.start()

        def finish(g, _):
            at(g, 0, 0).wait()
            return 0

        lax.fori_loop(0, blocks, finish, 0)
        tail.wait()


def route(owner, slot, blocks, rows, cols, owners, slot_total, tile_cols):
    count = blocks.shape[0]
    group = 4
    whole = pl.BlockSpec((count, T), lambda i, *_: (0, 0))
    return pl.pallas_call(
        functools.partial(route_kernel, group, slot_total, tile_cols),
        out_shape=jax.ShapeDtypeStruct((owners, 2 * T + 8, T), F32),
        grid_spec=pltpu.PrefetchScalarGridSpec(
            num_scalar_prefetch=2,
            grid=(count // group,),
            in_specs=[pl.BlockSpec((group, T, T), lambda i, *_: (i, 0, 0)), whole, whole],
            out_specs=ANY(),
            scratch_shapes=[
                pltpu.VMEM((owners, 8, T), F32),
                pltpu.VMEM((count, T, T), F32),
                pltpu.SMEM((owners,), jnp.int32),
                pltpu.SemaphoreType.DMA((count + 1,)),
            ],
        ),
        compiler_params=params(),
        name="route",
    )(owner, slot, blocks, rows, cols)


def sub_row(x, k):
    return jnp.broadcast_to(x[k : k + 1, :], (8, T))


def lane_col(x, k):
    return jnp.broadcast_to(x[:, k : k + 1], (8, T))


def tree_sum(x):
    while len(x) > 1:
        x = [x[i] + x[i + 1] for i in range(0, len(x), 2)]
    return x[0]


def inverse_factor(s, out_ref):
    groups = T // 8
    lane = lax.broadcasted_iota(jnp.int32, (8, T), 1)
    sub = lax.broadcasted_iota(jnp.int32, (8, T), 0)
    m = [s[8 * g : 8 * g + 8, :] for g in range(groups)]
    e = [jnp.where(lane == sub + 8 * g, 1.0, 0.0).astype(F32) for g in range(groups)]
    for p in range(groups):
        v = [sub_row(m[p], k) for k in range(8)]
        x = [sub_row(e[p], k) for k in range(8)]
        column = [lane_col(m[p], 8 * p + c) for c in range(8)]
        d = [[sub_row(column[c], r) if c <= r else None for c in range(8)] for r in range(8)]
        below = {g: [lane_col(m[g], 8 * p + c) for c in range(8)] for g in range(p + 1, groups)}
        inv = [None] * 8
        low = [[None] * 8 for _ in range(8)]
        for k in range(8):
            inv[k] = 1.0 / d[k][k]
            for r in range(k + 1, 8):
                low[r][k] = d[r][k] * inv[k]
            for r in range(k + 1, 8):
                for c in range(k + 1, r + 1):
                    d[r][c] = d[r][c] - low[r][k] * d[c][k]
                v[r] = v[r] - low[r][k] * v[k]
                x[r] = x[r] - low[r][k] * x[k]
        for k in range(8):
            out_ref[8 * p + k : 8 * p + k + 1, :] = (x[k] * lax.sqrt(inv[k]))[0:1, :]
        if p == groups - 1:
            break
        v = [v[k] * inv[k] for k in range(8)]
        x = [x[k] * inv[k] for k in range(8)]
        for k in range(7, 0, -1):
            for j in range(k):
                v[j] = v[j] - low[k][j] * v[k]
                x[j] = x[j] - low[k][j] * x[k]
        for g in range(p + 1, groups):
            m[g] = m[g] - tree_sum([below[g][k] * v[k] for k in range(8)])
            e[g] = e[g] - tree_sum([below[g][k] * x[k] for k in range(8)])


def leading_kernel(core_ref, x0, x1, high_ref, low_ref, lead_ref, s_ref, e_ref, w_ref):
    n = 4
    dot = functools.partial(lax.dot_general, precision=HIGHEST, preferred_element_type=F32)


    for d, x in enumerate((x0, x1)):
        lead_ref[:, pl.ds(pl.multiple_of((core_ref[0] ^ d) * 64, 64), 64), :] = x[...]

    def tile(i, j):
        return lead_ref[4 * i + j]

    for i in range(n):
        for j in range(i + 1):
            s_ref[i, j] = 0.5 * (tile(i, j) + tile(j, i).T)
    e_ref[...] = jnp.zeros_like(e_ref)

    def step(k, _):
        inverse_factor(s_ref[k, k], w_ref)
        wk = w_ref[...]
        own = dot(wk, e_ref[k], NN)
        column = lax.broadcasted_iota(jnp.int32, (T, n * T), 1)
        spread = jnp.concatenate([wk] * n, axis=1)
        own = jnp.where(column // T == k, spread, own)
        for j in range(n):
            at = pl.ds(pl.multiple_of(k * T, T), T)
            high, low = split(own[:, j * T : (j + 1) * T].T)
            high_ref[j, :, at] = high
            low_ref[j, :, at] = low

        for i in range(1, n):
            @pl.when(i > k)
            def _():
                lik = dot(s_ref[i, k], wk, NT)
                s_ref[i, k] = lik
                e_ref[i] = e_ref[i] - dot(lik, own, NN)
                for j in range(1, i + 1):
                    @pl.when(j > k)
                    def _():
                        s_ref[i, j] = s_ref[i, j] - dot(lik, s_ref[j, k], NT)
        return 0

    lax.fori_loop(0, n, step, 0)


def leading_inverse(core, parts):
    return pl.pallas_call(
        leading_kernel,
        out_shape=(jax.ShapeDtypeStruct((4, T, 4 * T), BF16),) * 2,
        grid_spec=pltpu.PrefetchScalarGridSpec(
            num_scalar_prefetch=1,
            grid=(),
            in_specs=[VM()] * 2,
            out_specs=(VM(), VM()),
            scratch_shapes=[
                pltpu.VMEM((16, T, T), F32),
                pltpu.VMEM((4, 4, T, T), F32),
                pltpu.VMEM((4, T, 4 * T), F32),
                pltpu.VMEM((T, T), F32),
            ],
        ),
        compiler_params=params(16),
        cost_estimate=pl.CostEstimate(flops=60_000_000_000, bytes_accessed=2_000_000, transcendentals=0),
        name="leading_inverse",
    )(core, *parts)


def panel_kernel(col_ref, got_ref, base_ref, after_ref, out_ref, p0, p1, p2, p3, held, places, sem):
    total = held.shape[0]
    tile_rows = out_ref.shape[0] // T
    look = pltpu.make_async_copy(got_ref.at[:, 2 * T, :], places, sem.at[total])
    look.start()
    out_ref[...] = base_ref[...]
    look.wait()

    def tile_row(n):
        return places[n // 2, n % 2 + 2]

    def wanted(n):
        return tile_row(n) < tile_rows

    def copy(n):
        block = got_ref.at[n // 2, pl.ds(pl.multiple_of(n % 2 * T, T), T), :]
        return pltpu.make_async_copy(block, held.at[n], sem.at[n])

    def fetch(n, _):
        @pl.when(wanted(n))
        def _():
            copy(n).start()

        return 0

    lax.fori_loop(0, total, fetch, 0, unroll=8)

    def add(n, _):
        @pl.when(wanted(n))
        def _():
            copy(n).wait()
            a = pl.ds(pl.multiple_of(tile_row(n).astype(jnp.int32) * T, T), T)
            out_ref[a, :] = out_ref[a, :] + held[n]

        return 0

    lax.fori_loop(0, total, add, 0, unroll=8)
    quarter = T // 4
    for m, piece in enumerate((p0, p1, p2, p3)):
        first = lax.rem(col_ref[0] + m, 4) * quarter
        for a in range(out_ref.shape[0] // T):
            piece[a * quarter : (a + 1) * quarter, :] = out_ref[pl.ds(pl.multiple_of(a * T + first, quarter), quarter), :]


def panel(col, got, base, after):
    rows = base.shape[0]
    total = 2 * got.shape[0]
    return pl.pallas_call(
        panel_kernel,
        out_shape=(jax.ShapeDtypeStruct((rows, T), F32),) + (jax.ShapeDtypeStruct((rows // 4, T), F32),) * 4,
        grid_spec=pltpu.PrefetchScalarGridSpec(
            num_scalar_prefetch=1,
            grid=(),
            in_specs=[ANY(), VM(), ANY()],
            out_specs=(VM(),) * 5,
            scratch_shapes=[
                pltpu.VMEM((total, T, T), F32),
                pltpu.SMEM((total // 2, T), F32),
                pltpu.SemaphoreType.DMA((total + 1,)),
            ],
        ),
        compiler_params=params(16),
        name="panel",
    )(col, got, base, after)


def load_rhs(order_ref, high_ref, low_ref, rhs_ref):
    for m in range(4):
        high, low = high_ref[order_ref[m]], low_ref[order_ref[m]]
        rhs_ref[m * T : (m + 1) * T, :] = high
        rhs_ref[(4 + m) * T : (5 + m) * T, :] = low
        rhs_ref[(8 + m) * T : (9 + m) * T, :] = high


def times_wt(parts, rhs_ref):
    pairs = [split(x) for x in parts]
    high, low = [p[0] for p in pairs], [p[1] for p in pairs]
    return lax.dot_general(
        jnp.concatenate(high + high + low, axis=1), rhs_ref[...], NN, preferred_element_type=F32
    )


def share_kernel(order_ref, x0, x1, x2, x3, high_ref, low_ref, out_ref, rhs_ref):
    load_rhs(order_ref, high_ref, low_ref, rhs_ref)
    out_ref[...] = times_wt([x[...] for x in (x0, x1, x2, x3)], rhs_ref)


def share_solve(order, parts, wt):
    return pl.pallas_call(
        share_kernel,
        out_shape=jax.ShapeDtypeStruct((parts[0].shape[0], 4 * T), F32),
        grid_spec=pltpu.PrefetchScalarGridSpec(
            num_scalar_prefetch=1,
            grid=(),
            in_specs=[VM()] * 6,
            out_specs=VM(),
            scratch_shapes=[pltpu.VMEM((12 * T, 4 * T), BF16)],
        ),
        compiler_params=params(16),
        name="share_solve",
    )(order, *parts, *wt)


def rest_kernel(tile_cols, group, marks_ref, got_ref, base_ref, out_ref, marks, slots, sem):
    @pl.when(pl.program_id(0) == 0)
    def _():
        look = pltpu.make_async_copy(marks_ref.at[:, 2 * T, :], marks, sem)
        look.start()
        look.wait()

        def convert(n, _):
            slots[n] = marks[n // 2, n % 2].astype(jnp.int32)
            return 0

        lax.fori_loop(0, slots.shape[0], convert, 0, unroll=8)

    out_ref[...] = base_ref[...]
    first = pl.program_id(0) * group * tile_cols

    def step(n, _):
        slot = slots[n] - first

        @pl.when((slot >= 0) & (slot < group * tile_cols))
        def _():
            at = pl.ds(slot // tile_cols * (T * tile_cols) + slot % tile_cols, T, stride=tile_cols)
            out_ref[at, :] = out_ref[at, :] + got_ref[n // 2, pl.ds(pl.multiple_of(n % 2 * T, T), T), :]

        return 0

    lax.fori_loop(0, slots.shape[0], step, 0, unroll=4)


def rest(got, base, tile_rows, tile_cols):
    group = 3
    size = group * T * tile_cols
    block = pl.BlockSpec((size, T), lambda a: (a, 0))
    return pl.pallas_call(
        functools.partial(rest_kernel, tile_cols, group),
        out_shape=jax.ShapeDtypeStruct(base.shape, F32),
        grid=(tile_rows // group,),
        in_specs=[ANY(), pl.BlockSpec(got.shape, lambda a: (0, 0, 0), pipeline_mode=pl.Buffered(1)), block],
        out_specs=block,
        scratch_shapes=[
            pltpu.SMEM((got.shape[0], T), F32),
            pltpu.SMEM((2 * got.shape[0],), jnp.int32),
            pltpu.SemaphoreType.DMA,
        ],
        compiler_params=params(32),
        cost_estimate=pl.CostEstimate(flops=10_000_000_000, bytes_accessed=26_000_000, transcendentals=0),
        name="rest",
    )(got, got, base)


def load_columns(h, k, pieces, rhs_ref):
    for d, ref in enumerate(pieces):
        quarter = (k ^ d) * 32 + h * T
        for q in range(ref.shape[0] // 32):
            high, low = split(ref[32 * q : 32 * q + 32, :])
            at = pl.ds(pl.multiple_of(q * 2 * T + quarter, 32), 32)
            rhs_ref[at, 0:512] = high
            rhs_ref[at, 512:1024] = low


def update_kernel(
    tile_cols, group, info_ref, s0, s1, s2, s3, t0, t1, t2, t3, x0, x1, x2, x3, high_ref, low_ref, base_ref, out_ref, wt_ref, rhs_ref
):
    my_col, my_row = info_ref[4], info_ref[5]
    h, k = my_row // 4, my_row % 4

    @pl.when(pl.program_id(0) == 0)
    def _():
        load_rhs(info_ref, high_ref, low_ref, wt_ref)
        load_columns(h, k, (s0, s1, s2, s3), rhs_ref)
        load_columns(1 - h, k, (t0, t1, t2, t3), rhs_ref)

    panel_rows = times_wt([x[...] for x in (x0, x1, x2, x3)], wt_ref)
    own = panel_rows[:, 0:T]
    for j in range(1, 4):
        own = jnp.where(my_col == j, panel_rows[:, j * T : (j + 1) * T], own)
    row = lax.broadcasted_iota(jnp.int32, panel_rows.shape, 0)
    leading = (pl.program_id(0) == 0) & (my_row < 4)
    high, low = split(jnp.where((row < T) & leading, 0.0, panel_rows))
    lhs = jnp.concatenate([high, high, low], axis=1)
    for q in range(0, tile_cols, 2):
        rhs = rhs_ref[q * T : (q + 2) * T, :]
        rhs = jnp.concatenate([rhs, rhs[:, 0:512]], axis=1)
        u = lax.dot_general(lhs, rhs, NT, preferred_element_type=F32)
        for a in range(group):
            for b in (q, q + 1):
                at = pl.ds(a * T * tile_cols + b, T, stride=tile_cols)
                if b == 0:
                    out_ref[at, :] = own[a * T : (a + 1) * T, :]
                else:
                    out_ref[at, :] = base_ref[at, :] - u[a * T : (a + 1) * T, (b - q) * T : (b - q + 1) * T]


def update(info, pieces, parts, wt, base, tile_rows, tile_cols):
    group = 3
    size = group * T * tile_cols
    block = pl.BlockSpec((size, T), lambda a, *_: (a, 0))
    return pl.pallas_call(
        functools.partial(update_kernel, tile_cols, group),
        out_shape=jax.ShapeDtypeStruct(base.shape, F32),
        grid_spec=pltpu.PrefetchScalarGridSpec(
            num_scalar_prefetch=1,
            grid=(tile_rows // group,),
            in_specs=[pl.BlockSpec(x.shape, lambda a, *_: (0, 0), pipeline_mode=pl.Buffered(1)) for x in pieces]
            + [pl.BlockSpec((group * T, T), lambda a, *_: (a, 0))] * 4
            + [pl.BlockSpec(x.shape, lambda a, *_: (0, 0, 0), pipeline_mode=pl.Buffered(1)) for x in wt]
            + [block],
            out_specs=block,
            scratch_shapes=[pltpu.VMEM((12 * T, 4 * T), BF16), pltpu.VMEM((tile_cols * T, 8 * T), BF16)],
        ),
        compiler_params=params(30),
        name="update",
    )(info, *pieces, *parts, *wt, base)


def local(front, child_updates, child_owner, child_rows, child_cols, child_slot):
    my_row = lax.axis_index("row")
    my_col = lax.axis_index("col")
    tile_rows, tile_cols = front.shape[1], front.shape[4]
    slot_total = tile_rows * tile_cols
    flat = front.reshape(tile_rows * T * tile_cols, T)

    send = route(child_owner[0, :, 0], child_slot[0], child_updates[0], child_rows[0], child_cols[0], 32, slot_total, tile_cols)

    tile = front[0, 0, 0, :, 0, 0, :].reshape(1, 2, 1, T // 2, T)
    halves = jnp.broadcast_to(tile, (4, 2, 4, T // 2, T)).reshape(32, T // 2, T)
    mine = lax.all_to_all(halves, ("row", "col"), split_axis=0, concat_axis=0, tiled=True)[:16]
    mine, send = lax.optimization_barrier((mine, send))
    lead = [mine] + [lax.ppermute(mine, "row", [(r, r ^ d) for r in range(8)]) for d in (1,)]
    got = lax.all_to_all(send, ("row", "col"), split_axis=0, concat_axis=0, tiled=True)
    wt = leading_inverse((my_row % 2).reshape(1), lead)
    base_panel = lax.optimization_barrier((front, lead[1]))[0][0, :, 0, :, 0, 0, :].reshape(tile_rows * T, T)

    columns, *pieces = panel(my_col.reshape(1), got, base_panel, wt[1])

    parts = []
    for m in range(4):
        moves = [
            ((4 * h + c) * 4 + j, (4 * h + (j + m) % 4) * 4 + c) for h in range(2) for c in range(4) for j in range(4)
        ]
        parts.append(lax.ppermute(pieces[m], ("row", "col"), moves))
    order = (my_row - jnp.arange(4, dtype=jnp.int32)) % 4
    first_core = my_row % 2 == 0
    columns, parts[0] = lax.optimization_barrier((columns, parts[0]))
    from_left = lax.ppermute(columns, "col", [(c, (c + 1) % 4) for c in range(4)])
    from_right = lax.ppermute(columns, "col", [(c, (c - 1) % 4) for c in range(4)])
    far = lax.ppermute(
        jnp.where(first_core, from_left, from_right),
        ("row", "col"),
        [(r * 4 + c, r * 4 + (c + 1 - 2 * (r % 2)) % 4) for r in range(8) for c in range(4)],
    )

    share = share_solve(order, parts, wt)
    got, share = lax.optimization_barrier((got, share))

    def swap(x, bits):
        return lax.ppermute(x, "row", [(r, r ^ bits) for r in range(8)])

    near, far_side = swap(share, 2), swap(share, 6)
    beside = swap(share, 1)
    base = rest(got, flat, tile_rows, tile_cols)
    near, far_side, base = lax.optimization_barrier((near, far_side, base))
    opposite = lax.ppermute(
        jnp.where(first_core, far_side, near), "row", [(r, r ^ (2 if r % 2 == 0 else 6)) for r in range(8)]
    )
    near_beside, far_beside, opposite_beside = swap(near, 1), swap(far_side, 1), swap(opposite, 1)

    info = jnp.concatenate([(my_col + jnp.array([0, -1, 1, 2], jnp.int32)) % 4, jnp.stack([my_col, my_row])])
    shares = (share, beside, near, near_beside, opposite, opposite_beside, far_side, far_beside)
    result = update(info, shares, (columns, from_left, from_right, far), wt, base, tile_rows, tile_cols)
    return result.reshape(front.shape)


def solution(mesh):
    in_specs = (
        P("front", None, "row", None, None, "col", None),
        P("front", ("row", "col"), None, None),
        P("front", ("row", "col"), None),
        P("front", ("row", "col"), None),
        P("front", ("row", "col"), None),
        P("front", ("row", "col")),
    )
    out_specs = P("front", None, "row", None, None, "col", None)
    return jax.shard_map(local, mesh=mesh, in_specs=in_specs, out_specs=out_specs, check_vma=False)
```
